32 devices in a mesh: blk: 8 (over z, x), uly: 4 (over y, core).
Axes of the slice: x: 2, y: 2, z: 4, core: 2. Of those that a mesh axis runs over, the one named last changes fastest.
Arguments:
- tokens: bfloat16 [768, 2560], P(('blk', 'uly')), may hold values from -6 to 6
- in_bits: int32 [768, 2560], P(('blk', 'uly')), may hold values from 0 to 1
- qkv_weights: bfloat16 [2, 3, 2560, 2560], P(None, None, 'blk', 'uly'), may hold values from -0.125 to 0.125
- qkv_bits: int32 [768, 3, 2560], P('blk', None, 'uly'), may hold values from 0 to 1
- gain_query: float32 [2560], P('uly'), may hold values from 0.7 to 1.8
- gain_key: float32 [2560], P('uly'), may hold values from 0.7 to 1.8
- out_weights: bfloat16 [2, 2560, 2560], P(None, 'uly', 'blk'), may hold values from -0.5 to 0.5
- mix_bits: int32 [768, 2560], P('blk', 'uly'), may hold values from 0 to 1
- out_bits: int32 [768, 2560], P('blk'), may hold values from 0 to 1
Outputs:
- layer_output: bfloat16 [768, 2560], P(('blk', 'uly'))
The draws below stay inside these ranges and needn't reach their ends.
Inputs may be any that keep to these rules, and one draw needn't show every extreme that they name: `in_bits`: a bit of 1 stands for the sign +1, a bit of 0 for -1. `qkv_bits`: a bit of 1 stands for the sign +1, a bit of 0 for -1. `mix_bits`: a bit of 1 stands for the sign +1, a bit of 0 for -1. `out_bits`: a bit of 1 stands for the sign +1, a bit of 0 for -1.
All inputs are finite; a program needn't handle non-finite values.
Results may differ from the reference program's by a relative error of at most 0.018.
Values may be sent and summed in bfloat16 or wider, within the bound.
No kernel may reach another device: no remote copies, remote signals or barrier semaphores. Data moves between devices by JAX's collectives and lax.ppermute only.
A program may use at most 128 MiB of HBM per device.

```python
import math
import jax
import jax.numpy as jnp
from jax import lax

D = 2560
HEADS = 20
HEAD = 128
TOKENS = 768


def touch_ends(drawn, rng, smallest, top_value):
    longest = drawn.shape.index(max(drawn.shape))
    spots = []
    for shift in (0, 1):
        where = [jax.random.randint(jax.random.fold_in(rng, axis), (), 0, length) for axis, length in enumerate(drawn.shape)]
        where[longest] = (where[longest] + shift) % drawn.shape[longest]
        spots.append(tuple(where))
    return drawn.at[spots[0]].set(smallest).at[spots[1]].set(top_value)


def block_levels(own_key, extent, shards, smallest, largest):
    gain, own = 1.0, jax.random.fold_in(own_key, 6)
    for position, blocks in shards:
        heights = jnp.exp(jax.random.uniform(jax.random.fold_in(own, position), (blocks,), jnp.float32, smallest / len(shards), largest / len(shards)))
        gain = gain * jnp.repeat(heights, extent[position] // blocks).reshape([-1 if axis == position else 1 for axis in range(len(extent))])
    return gain


def normal_values(key, extent, deviation, most, pieces=(), held_as=jnp.bfloat16):
    level = block_levels(key, extent, pieces, -0.22, 0.18) if pieces else 1.0
    values = jax.random.normal(key, extent, jnp.float32) * deviation * level
    return jnp.minimum(jnp.maximum(values, -most), most).astype(held_as)


def setup_inputs(seed: int = 0) -> dict:
    keys = jax.random.split(jax.random.key(seed), 10)
    return {
        "tokens": normal_values(keys[0], (TOKENS, D), 1.0, 6.0, ((0, 32),)),
        "in_bits": touch_ends(jax.random.randint(keys[1], (TOKENS, D), 0, 2), jax.random.fold_in(keys[1], 1), 0, 1).astype(jnp.int32),
        "qkv_weights": normal_values(keys[2], (2, 3, D, HEADS * HEAD), D ** -0.5, 0.125, ((2, 8), (3, 4))),
        "qkv_bits": touch_ends(jax.random.randint(keys[3], (TOKENS, 3, HEADS * HEAD), 0, 2), jax.random.fold_in(keys[3], 1), 0, 1).astype(jnp.int32),
        "gain_query": jnp.clip(jnp.exp(math.log(1.8) - 0.9444616 * jax.random.uniform(keys[4], (HEADS * HEAD,), jnp.float32) ** block_levels(keys[4], (HEADS * HEAD,), ((0, 4),), -0.2, 0.2)), 0.7, 1.8),
        "gain_key": jnp.clip(jnp.exp(math.log(1.8) - 0.9444616 * jax.random.uniform(keys[5], (HEADS * HEAD,), jnp.float32) ** block_levels(keys[5], (HEADS * HEAD,), ((0, 4),), -0.2, 0.2)), 0.7, 1.8),
        "out_weights": normal_values(keys[6], (2, HEADS * HEAD, D), (HEADS * HEAD // 16) ** -0.5, 0.5, ((1, 4), (2, 8))),
        "mix_bits": touch_ends(jax.random.randint(keys[7], (TOKENS, HEADS * HEAD), 0, 2), jax.random.fold_in(keys[7], 1), 0, 1).astype(jnp.int32),
        "out_bits": touch_ends(jax.random.randint(keys[8], (TOKENS, D), 0, 2), jax.random.fold_in(keys[8], 1), 0, 1).astype(jnp.int32),
    }


epsilon = 1e-06

def signed(bit_values):
    return (2 * bit_values - 1).astype(jnp.float32)

def normalize(values, gain_vector):
    row_count = values.shape[0]
    by_head = values.astype(jnp.float32).reshape(row_count, -1, HEAD)
    inverse_rms = lax.rsqrt(lax.optimization_barrier(jnp.mean(by_head * by_head, axis=-1, keepdims=True)) + epsilon)
    return (by_head * inverse_rms * gain_vector.reshape(-1, HEAD)).astype(jnp.bfloat16)

def reference(tokens, in_bits, qkv_weights, qkv_bits, gain_query, gain_key, out_weights, mix_bits, out_bits):
    flipped = (tokens.astype(jnp.float32) * signed(in_bits)).astype(jnp.bfloat16)
    qkv_signs = signed(qkv_bits)
    projections = []
    for qkv_slot in range(3):
        mean_part = jnp.dot(tokens, qkv_weights[0, qkv_slot], preferred_element_type=jnp.float32)
        delta_part = jnp.dot(flipped, qkv_weights[1, qkv_slot], preferred_element_type=jnp.float32)
        projections.append((mean_part + qkv_signs[:, qkv_slot] * delta_part).astype(jnp.bfloat16))
    queries = normalize(projections[0], gain_query)
    keys_normed = normalize(projections[1], gain_key)
    values_all = projections[2].reshape(projections[2].shape[0], -1, HEAD)
    score_scale = 1.0 / math.sqrt(HEAD)

    def one_head(operands):
        query_head, key_head, value_head = operands
        scores = jnp.dot(query_head, key_head.T, preferred_element_type=jnp.float32) * score_scale
        weights = jnp.exp(scores).astype(jnp.bfloat16)
        totals = lax.optimization_barrier(jnp.sum(weights.astype(jnp.float32), axis=1))
        return (jnp.dot(weights, value_head, preferred_element_type=jnp.float32) / totals[:, None]).astype(jnp.bfloat16)
    heads_out = lax.map(one_head, (jnp.transpose(queries, (1, 0, 2)), jnp.transpose(keys_normed, (1, 0, 2)), jnp.transpose(values_all, (1, 0, 2))))
    attended = jnp.transpose(heads_out, (1, 0, 2)).reshape(tokens.shape[0], -1)
    attended_flipped = (attended.astype(jnp.float32) * signed(mix_bits)).astype(jnp.bfloat16)
    mean_out = jnp.dot(attended, out_weights[0], preferred_element_type=jnp.float32)
    delta_out = jnp.dot(attended_flipped, out_weights[1], preferred_element_type=jnp.float32)
    return (mean_out + signed(out_bits) * delta_out).astype(jnp.bfloat16)
```

```python
import math

import jax
import jax.numpy as jnp
from jax import lax
from jax.sharding import PartitionSpec as P

HEAD = 128


epsilon = 1e-06


def signed(bit_values):
    return (2 * bit_values - 1).astype(jnp.float32)


def normalize(values, gain_vector):
    row_count = values.shape[0]
    by_head = values.astype(jnp.float32).reshape(row_count, -1, HEAD)
    inverse_rms = lax.rsqrt(jnp.mean(by_head * by_head, axis=-1, keepdims=True) + epsilon)
    return (by_head * inverse_rms * gain_vector.reshape(-1, HEAD)).astype(jnp.bfloat16)


def gather_plan(
    tokens, in_bits, qkv_weights, qkv_bits, gain_query, gain_key, out_weights, mix_bits, out_bits
):
    flipped = (tokens.astype(jnp.float32) * signed(in_bits)).astype(jnp.bfloat16)
    group_rows = lax.all_gather(jnp.stack([tokens, flipped]), "uly", axis=1, tiled=True)
    row_total = group_rows.shape[1]
    projections = jnp.einsum(
        "mrd,mkdc->rmkc",
        group_rows,
        lax.all_gather(qkv_weights, "blk", axis=2, tiled=True),
        preferred_element_type=jnp.float32,
    )
    projected = (projections[:, 0] + signed(qkv_bits) * projections[:, 1]).astype(jnp.bfloat16)
    queries = normalize(projected[:, 0], gain_query)
    head_count = queries.shape[1]
    keys_normed = normalize(projected[:, 1], gain_key).reshape(row_total, -1)
    values_block = projected[:, 2]
    score_scale = 1.0 / math.sqrt(HEAD)

    def attend(running, shard_piece):
        numerator, denominator = running
        key_rows = shard_piece[0].reshape(shard_piece[0].shape[0], head_count, HEAD)
        value_rows = shard_piece[1].reshape(shard_piece[1].shape[0], head_count, HEAD)
        scores = (
            jnp.einsum("rhd,nhd->hrn", queries, key_rows, preferred_element_type=jnp.float32)
            * score_scale
        )
        weights = jnp.exp(scores).astype(jnp.bfloat16)
        numerator = numerator + jnp.einsum(
            "hrn,nhd->rhd", weights, value_rows, preferred_element_type=jnp.float32
        )
        denominator = denominator + jnp.sum(weights.astype(jnp.float32), axis=2).T
        return (numerator, denominator)

    start_state = (
        jnp.zeros((row_total, head_count, HEAD), jnp.float32),
        jnp.zeros((row_total, head_count), jnp.float32),
    )
    all_keys, all_values = (
        lax.all_gather(keys_normed, "blk", axis=0, tiled=True),
        lax.all_gather(values_block, "blk", axis=0, tiled=True),
    )
    group_count = lax.axis_size("blk")
    per_block = 1
    while per_block * row_total < 512 and group_count % (per_block * 2) == 0:
        per_block = per_block * 2
    block_rows = per_block * row_total
    block_count = group_count // per_block
    key_blocks = all_keys.reshape(block_count, block_rows, all_keys.shape[1])
    value_blocks = all_values.reshape(block_count, block_rows, all_values.shape[1])

    def scan_step(running, block_pair):
        return (attend(running, block_pair), None)

    (numerator, denominator), unused = lax.scan(scan_step, start_state, (key_blocks, value_blocks))
    attended = (numerator / denominator[:, :, None]).astype(jnp.bfloat16).reshape(row_total, -1)
    attended_flipped = (attended.astype(jnp.float32) * signed(mix_bits)).astype(jnp.bfloat16)
    attended_pair = jnp.stack([attended, attended_flipped])
    out_signs = signed(out_bits)
    partial_out = jnp.einsum(
        "mrc,mcn->rmn",
        attended_pair,
        lax.all_gather(out_weights, "blk", axis=2, tiled=True),
        preferred_element_type=jnp.float32,
    )
    summed = lax.psum_scatter(
        partial_out.astype(jnp.bfloat16), "uly", scatter_dimension=0, tiled=True
    ).astype(jnp.float32)
    own_rows = summed.shape[0]
    own_signs = lax.dynamic_slice_in_dim(out_signs, lax.axis_index("uly") * own_rows, own_rows, 0)
    result_rows = summed[:, 0] + own_signs * summed[:, 1]
    return result_rows.astype(jnp.bfloat16)


def dot32(a, b):
    return lax.dot_general(
        a, b, (((1,), (0,)), ((), ())), preferred_element_type=jnp.float32
    )


def dot32_t(a, b):
    return lax.dot_general(
        a, b, (((1,), (1,)), ((), ())), preferred_element_type=jnp.float32
    )


def norm_rows(values, gain_row):
    wide = values.astype(jnp.float32)
    inverse_rms = lax.rsqrt(jnp.mean(wide * wide, axis=-1, keepdims=True) + epsilon)
    return (wide * inverse_rms * gain_row).astype(jnp.bfloat16)


def attend(queries, keys, values):
    scores = dot32_t(queries, keys) * (1.0 / math.sqrt(HEAD))
    weights = jnp.exp(scores).astype(jnp.bfloat16)
    totals = jnp.sum(weights.astype(jnp.float32), axis=1, keepdims=True)
    return (dot32(weights, values) / totals).astype(jnp.bfloat16)


def stationary_plan(
    tokens, in_bits, qkv_weights, qkv_bits, gain_query, gain_key, out_weights, mix_bits, out_bits
):
    groups = lax.axis_size("blk")
    team = lax.axis_size("uly")
    depth = groups // 2
    z = lax.axis_index("blk") // 2
    x = lax.axis_index("blk") % 2
    u = lax.axis_index("uly")
    own_rows, width = tokens.shape
    slab = qkv_weights.shape[2]
    columns = qkv_weights.shape[3]
    group_rows = own_rows * team
    heads = columns // HEAD
    half_rows = depth * group_rows

    def swap_x(value):
        return lax.ppermute(value, "blk", [(i, i ^ 1) for i in range(groups)])

    def swap_z(value, step):
        return lax.ppermute(value, "blk", [(i, i ^ (2 * step)) for i in range(groups)])

    def swap_u(value, bit):
        return lax.ppermute(value, "uly", [(i, i ^ bit) for i in range(team)])

    bf = jnp.bfloat16
    steps = range(depth)

    flipped = (tokens.astype(jnp.float32) * signed(in_bits)).astype(bf)
    pair = jnp.stack([tokens, flipped])

    def feature_block(target):
        first = lax.dynamic_slice_in_dim(pair, (2 * target + x) * slab, slab, 2)
        second = lax.dynamic_slice_in_dim(pair, (2 * target + 1 - x) * slab, slab, 2)
        return jnp.concatenate([first, second], axis=2)

    pieces = [feature_block(z)] + [swap_z(feature_block(z ^ k), k) for k in steps if k]
    held = jnp.stack(pieces, axis=1)
    held = lax.all_gather(held, "uly", axis=2, tiled=False)
    rows = held.reshape(2, half_rows, 2 * slab)

    signs_own = jnp.transpose(2 * qkv_bits - 1, (1, 0, 2)).astype(bf)
    signs = {}
    partner = {}
    for part in (2, 1, 0):
        signs[part] = jnp.concatenate(
            [signs_own[part]] + [swap_z(signs_own[part], k) for k in steps if k], axis=0
        )
        partner[part] = swap_x(qkv_weights[:, part])

    out_t = jnp.transpose(out_weights, (0, 2, 1))
    out_partner = swap_x(out_t)
    mix_own = (2 * mix_bits - 1).astype(bf)
    mix_all = [mix_own] + [swap_z(mix_own, k) for k in steps if k]

    whole_heads = heads // depth
    rest = heads - whole_heads * depth
    assert whole_heads == 1 and rest == 1

    def head_of(value, index):
        return lax.dynamic_slice_in_dim(value, index * HEAD, HEAD, 1)

    def project(part):
        total = [
            dot32(rows[m, :, :slab], qkv_weights[m, part])
            + dot32(rows[m, :, slab:], partner[part][m])
            for m in (0, 1)
        ]
        partial = (total[0] + signs[part].astype(jnp.float32) * total[1]).astype(bf)
        shared = partial[:, depth * HEAD :]
        got_main, got_rest = [], []
        for k in steps:
            block = jnp.concatenate(
                [
                    head_of(partial, z ^ k),
                    shared[k * group_rows : (k + 1) * group_rows],
                ],
                axis=0,
            )
            if k:
                block = swap_z(block, k)
            main = block[:half_rows].reshape(depth, group_rows, HEAD)
            got_main.append(jnp.stack([main[j ^ k] for j in steps]))
            got_rest.append(block[half_rows:])
        main = sum(g.astype(jnp.float32) for g in got_main).reshape(half_rows, HEAD)
        other = sum(g.astype(jnp.float32) for g in got_rest)
        return main.astype(bf), other.astype(bf)

    gain_q = gain_query.reshape(heads, HEAD)
    gain_k = gain_key.reshape(heads, HEAD)

    def gains(table):
        return lax.dynamic_slice_in_dim(table, z, 1, 0), table[depth : depth + 1]

    def spread(main, other):
        both = jnp.concatenate([main, swap_x(main)], axis=0)
        line = jnp.concatenate([other] + [swap_z(other, k) for k in steps if k], axis=0)
        return both, jnp.concatenate([line, swap_x(line)], axis=0)

    value_main, value_rest = spread(*project(2))
    key_main, key_rest = project(1)
    gain_main, gain_rest = gains(gain_k)
    key_main, key_rest = spread(norm_rows(key_main, gain_main), norm_rows(key_rest, gain_rest))
    query_main, query_rest = project(0)
    gain_main, gain_rest = gains(gain_q)
    query_main, query_rest = norm_rows(query_main, gain_main), norm_rows(query_rest, gain_rest)

    done_main = attend(query_main, key_main, value_main)
    done_rest = attend(query_rest, key_rest, value_rest)
    done = jnp.concatenate([done_main, done_rest], axis=0)

    by_head, last_head = [], []
    for k in steps:
        block = swap_z(done, k) if k else done
        main = block[:half_rows].reshape(depth, group_rows, HEAD)
        by_head.append(jnp.concatenate([main[j ^ k] for j in steps], axis=0))
        last_head.append(block[half_rows:])
    attended = jnp.concatenate(by_head + [jnp.concatenate(last_head, axis=0)], axis=1)

    def relative(value, axis):
        parts = [
            lax.dynamic_slice_in_dim(value, (z ^ k) * HEAD, HEAD, axis) for k in steps
        ] + [lax.slice_in_dim(value, depth * HEAD, heads * HEAD, axis=axis)]
        return jnp.concatenate(parts, axis=axis)

    mix = relative(jnp.concatenate(mix_all, axis=0), 1)
    attended_flipped = attended * mix
    first = jnp.where(x == 0, out_t, out_partner)
    second = jnp.where(x == 0, out_partner, out_t)
    out_full = relative(jnp.concatenate([first, second], axis=1), 2)
    partial = jnp.stack(
        [dot32_t(attended, out_full[0]), dot32_t(attended_flipped, out_full[1])]
    ).astype(bf)
    partial = partial.reshape(2, depth, 2, 2, own_rows, 2 * slab)
    core = u % 2
    y = u // 2
    keep = lax.dynamic_index_in_dim(partial, core, 3, keepdims=False)
    send = lax.dynamic_index_in_dim(partial, 1 - core, 3, keepdims=False)
    summed = keep.astype(jnp.float32) + swap_u(send, 1).astype(jnp.float32)
    keep = lax.dynamic_index_in_dim(summed, y, 2, keepdims=False)
    send = lax.dynamic_index_in_dim(summed, 1 - y, 2, keepdims=False).astype(bf)
    summed = (keep + swap_u(send, 2).astype(jnp.float32)).astype(bf)
    final = [summed[:, 0]] + [swap_z(summed[:, k], k) for k in steps if k]
    placed = jnp.zeros((2, own_rows, depth, 2 * slab), bf)
    for k in steps:
        placed = lax.dynamic_update_slice_in_dim(placed, final[k][:, :, None], z ^ k, 2)
    placed = placed.reshape(2, own_rows, width).astype(jnp.float32)
    own_bits = lax.dynamic_slice_in_dim(out_bits, u * own_rows, own_rows, 0)
    return (placed[0] + signed(own_bits) * placed[1]).astype(bf)


def body(*arrays):
    heads = arrays[2].shape[3] // HEAD
    depth = lax.axis_size("blk") // 2
    if depth == heads - 1 and depth & (depth - 1) == 0 and lax.axis_size("uly") == 4:
        return stationary_plan(*arrays)
    return gather_plan(*arrays)


def solution(mesh):
    return jax.shard_map(
        body,
        mesh=mesh,
        in_specs=(
            P(("blk", "uly"), None),
            P(("blk", "uly"), None),
            P(None, None, "blk", "uly"),
            P("blk", None, "uly"),
            P("uly"),
            P("uly"),
            P(None, "uly", "blk"),
            P("blk", "uly"),
            P("blk", None),
        ),
        out_specs=P(("blk", "uly"), None),
        check_vma=False,
    )
```

```python
import math

import jax
import jax.numpy as jnp
from jax import lax
from jax.sharding import PartitionSpec as P

HEAD = 128


epsilon = 1e-06


def signed(bit_values):
    return (2 * bit_values - 1).astype(jnp.float32)


def normalize(values, gain_vector):
    row_count = values.shape[0]
    by_head = values.astype(jnp.float32).reshape(row_count, -1, HEAD)
    inverse_rms = lax.rsqrt(jnp.mean(by_head * by_head, axis=-1, keepdims=True) + epsilon)
    return (by_head * inverse_rms * gain_vector.reshape(-1, HEAD)).astype(jnp.bfloat16)


def gather_plan(
    tokens, in_bits, qkv_weights, qkv_bits, gain_query, gain_key, out_weights, mix_bits, out_bits
):
    flipped = (tokens.astype(jnp.float32) * signed(in_bits)).astype(jnp.bfloat16)
    group_rows = lax.all_gather(jnp.stack([tokens, flipped]), "uly", axis=1, tiled=True)
    row_total = group_rows.shape[1]
    projections = jnp.einsum(
        "mrd,mkdc->rmkc",
        group_rows,
        lax.all_gather(qkv_weights, "blk", axis=2, tiled=True),
        preferred_element_type=jnp.float32,
    )
    projected = (projections[:, 0] + signed(qkv_bits) * projections[:, 1]).astype(jnp.bfloat16)
    queries = normalize(projected[:, 0], gain_query)
    head_count = queries.shape[1]
    keys_normed = normalize(projected[:, 1], gain_key).reshape(row_total, -1)
    values_block = projected[:, 2]
    score_scale = 1.0 / math.sqrt(HEAD)

    def attend(running, shard_piece):
        numerator, denominator = running
        key_rows = shard_piece[0].reshape(shard_piece[0].shape[0], head_count, HEAD)
        value_rows = shard_piece[1].reshape(shard_piece[1].shape[0], head_count, HEAD)
        scores = (
            jnp.einsum("rhd,nhd->hrn", queries, key_rows, preferred_element_type=jnp.float32)
            * score_scale
        )
        weights = jnp.exp(scores).astype(jnp.bfloat16)
        numerator = numerator + jnp.einsum(
            "hrn,nhd->rhd", weights, value_rows, preferred_element_type=jnp.float32
        )
        denominator = denominator + jnp.sum(weights.astype(jnp.float32), axis=2).T
        return (numerator, denominator)

    start_state = (
        jnp.zeros((row_total, head_count, HEAD), jnp.float32),
        jnp.zeros((row_total, head_count), jnp.float32),
    )
    all_keys, all_values = (
        lax.all_gather(keys_normed, "blk", axis=0, tiled=True),
        lax.all_gather(values_block, "blk", axis=0, tiled=True),
    )
    group_count = lax.axis_size("blk")
    per_block = 1
    while per_block * row_total < 512 and group_count % (per_block * 2) == 0:
        per_block = per_block * 2
    block_rows = per_block * row_total
    block_count = group_count // per_block
    key_blocks = all_keys.reshape(block_count, block_rows, all_keys.shape[1])
    value_blocks = all_values.reshape(block_count, block_rows, all_values.shape[1])

    def scan_step(running, block_pair):
        return (attend(running, block_pair), None)

    (numerator, denominator), unused = lax.scan(scan_step, start_state, (key_blocks, value_blocks))
    attended = (numerator / denominator[:, :, None]).astype(jnp.bfloat16).reshape(row_total, -1)
    attended_flipped = (attended.astype(jnp.float32) * signed(mix_bits)).astype(jnp.bfloat16)
    attended_pair = jnp.stack([attended, attended_flipped])
    out_signs = signed(out_bits)
    partial_out = jnp.einsum(
        "mrc,mcn->rmn",
        attended_pair,
        lax.all_gather(out_weights, "blk", axis=2, tiled=True),
        preferred_element_type=jnp.float32,
    )
    summed = lax.psum_scatter(
        partial_out.astype(jnp.bfloat16), "uly", scatter_dimension=0, tiled=True
    ).astype(jnp.float32)
    own_rows = summed.shape[0]
    own_signs = lax.dynamic_slice_in_dim(out_signs, lax.axis_index("uly") * own_rows, own_rows, 0)
    result_rows = summed[:, 0] + own_signs * summed[:, 1]
    return result_rows.astype(jnp.bfloat16)


def dot32(a, b):
    return lax.dot_general(
        a, b, (((1,), (0,)), ((), ())), preferred_element_type=jnp.float32
    )


def dot32_t(a, b):
    return lax.dot_general(
        a, b, (((1,), (1,)), ((), ())), preferred_element_type=jnp.float32
    )


def norm_rows(values, gain_row):
    wide = values.astype(jnp.float32)
    inverse_rms = lax.rsqrt(jnp.mean(wide * wide, axis=-1, keepdims=True) + epsilon)
    return (wide * inverse_rms * gain_row).astype(jnp.bfloat16)


def attend(queries, keys, values):
    scores = dot32_t(queries, keys) * (1.0 / math.sqrt(HEAD))
    weights = jnp.exp(scores).astype(jnp.bfloat16)
    totals = jnp.sum(weights.astype(jnp.float32), axis=1, keepdims=True)
    return (dot32(weights, values) / totals).astype(jnp.bfloat16)


def stationary_plan(
    tokens, in_bits, qkv_weights, qkv_bits, gain_query, gain_key, out_weights, mix_bits, out_bits
):
    groups = lax.axis_size("blk")
    team = lax.axis_size("uly")
    depth = groups // 2
    z = lax.axis_index("blk") // 2
    x = lax.axis_index("blk") % 2
    u = lax.axis_index("uly")
    own_rows, width = tokens.shape
    slab = qkv_weights.shape[2]
    columns = qkv_weights.shape[3]
    group_rows = own_rows * team
    heads = columns // HEAD
    half_rows = depth * group_rows
    lines = [[2 * i + j for i in range(depth)] for j in (0, 1)]
    bf = jnp.bfloat16

    def swap_x(value):
        return lax.ppermute(value, "blk", [(i, i ^ 1) for i in range(groups)])

    def swap_u(value, bit):
        return lax.ppermute(value, "uly", [(i, i ^ bit) for i in range(team)])

    def exchange_z(value):
        return lax.all_to_all(value, "blk", 0, 0, axis_index_groups=lines)

    def gather_z(value):
        return lax.all_gather(value, "blk", axis=0, axis_index_groups=lines)

    partner = {part: swap_x(qkv_weights[:, part]) for part in (2, 1, 0)}
    out_t = jnp.transpose(out_weights, (0, 2, 1))
    out_partner = swap_x(out_t)

    flipped = (tokens.astype(jnp.float32) * signed(in_bits)).astype(bf)
    pair = jnp.stack([tokens, flipped]).reshape(2, own_rows, depth, 2 * slab)
    held = exchange_z(jnp.transpose(pair, (2, 0, 1, 3)))
    rows = lax.all_gather(held, "uly", axis=0)
    rows = jnp.transpose(rows, (2, 1, 0, 3, 4)).reshape(2, half_rows, 2 * slab)

    signs_own = jnp.transpose(2 * qkv_bits - 1, (1, 0, 2)).astype(bf)
    signs_all = gather_z(signs_own)
    mix = gather_z((2 * mix_bits - 1).astype(bf)).reshape(half_rows, columns)

    def project(part):
        total = []
        for m in (0, 1):
            own, other = qkv_weights[m, part], partner[part][m]
            full = jnp.where(
                x == 0,
                jnp.concatenate([own, other], axis=0),
                jnp.concatenate([other, own], axis=0),
            )
            total.append(dot32(rows[m], full))
        signs = signs_all[:, part].reshape(half_rows, columns).astype(jnp.float32)
        partial = (total[0] + signs * total[1]).astype(bf)
        shared = partial[:, depth * HEAD :]
        blocks = [
            jnp.concatenate(
                [
                    partial[:, k * HEAD : (k + 1) * HEAD],
                    shared[k * group_rows : (k + 1) * group_rows],
                ],
                axis=0,
            )
            for k in range(depth)
        ]
        got = exchange_z(jnp.stack(blocks)).astype(jnp.float32)
        done = jnp.sum(got, axis=0).astype(bf)
        return done[:half_rows], done[half_rows:]

    gain_q = gain_query.reshape(heads, HEAD)
    gain_k = gain_key.reshape(heads, HEAD)

    def gains(table):
        return lax.dynamic_slice_in_dim(table, z, 1, 0), table[depth : depth + 1]

    value_main, value_rest = project(2)
    key_main, key_rest = project(1)
    gain_main, gain_rest = gains(gain_k)
    key_main, key_rest = norm_rows(key_main, gain_main), norm_rows(key_rest, gain_rest)
    rest_all = gather_z(jnp.concatenate([key_rest, value_rest], axis=1))
    rest_all = rest_all.reshape(half_rows, 2 * HEAD)
    sent = jnp.concatenate([key_main, value_main, rest_all], axis=1)
    taken = swap_x(sent)
    keys_values = jnp.concatenate([sent, taken], axis=0)

    query_main, query_rest = project(0)
    gain_main, gain_rest = gains(gain_q)
    query_main, query_rest = norm_rows(query_main, gain_main), norm_rows(query_rest, gain_rest)

    done_main = attend(query_main, keys_values[:, :HEAD], keys_values[:, HEAD : 2 * HEAD])
    done_rest = attend(
        query_rest, keys_values[:, 2 * HEAD : 3 * HEAD], keys_values[:, 3 * HEAD :]
    )
    done = gather_z(jnp.concatenate([done_main, done_rest], axis=0))
    main = jnp.transpose(done[:, :half_rows], (1, 0, 2)).reshape(half_rows, depth * HEAD)
    attended = jnp.concatenate([main, done[:, half_rows:].reshape(half_rows, HEAD)], axis=1)
    attended_flipped = attended * mix
    first = jnp.where(x == 0, out_t, out_partner)
    second = jnp.where(x == 0, out_partner, out_t)
    out_full = jnp.concatenate([first, second], axis=1)
    partial = jnp.stack(
        [dot32_t(attended, out_full[0]), dot32_t(attended_flipped, out_full[1])]
    ).astype(bf)
    partial = partial.reshape(2, depth, 2, 2, own_rows, 2 * slab)
    core = u % 2
    y = u // 2
    keep = lax.dynamic_index_in_dim(partial, core, 3, keepdims=False)
    send = lax.dynamic_index_in_dim(partial, 1 - core, 3, keepdims=False)
    summed = keep.astype(jnp.float32) + swap_u(send, 1).astype(jnp.float32)
    keep = lax.dynamic_index_in_dim(summed, y, 2, keepdims=False)
    send = lax.dynamic_index_in_dim(summed, 1 - y, 2, keepdims=False).astype(bf)
    summed = (keep + swap_u(send, 2).astype(jnp.float32)).astype(bf)
    final = exchange_z(jnp.transpose(summed, (1, 0, 2, 3)))
    final = jnp.transpose(final, (1, 2, 0, 3)).reshape(2, own_rows, width).astype(jnp.float32)
    own_bits = lax.dynamic_slice_in_dim(out_bits, u * own_rows, own_rows, 0)
    return (final[0] + signed(own_bits) * final[1]).astype(bf)


def body(*arrays):
    heads = arrays[2].shape[3] // HEAD
    depth = lax.axis_size("blk") // 2
    if depth == heads - 1 and depth & (depth - 1) == 0 and lax.axis_size("uly") == 4:
        return stationary_plan(*arrays)
    return gather_plan(*arrays)


def solution(mesh):
    return jax.shard_map(
        body,
        mesh=mesh,
        in_specs=(
            P(("blk", "uly"), None),
            P(("blk", "uly"), None),
            P(None, None, "blk", "uly"),
            P("blk", None, "uly"),
            P("uly"),
            P("uly"),
            P(None, "uly", "blk"),
            P("blk", "uly"),
            P("blk", None),
        ),
        out_specs=P(("blk", "uly"), None),
        check_vma=False,
    )
```

```python
import math

import jax
import jax.numpy as jnp
from jax import lax
from jax.sharding import PartitionSpec as P

HEAD = 128


epsilon = 1e-06


def signed(bit_values):
    return (2 * bit_values - 1).astype(jnp.float32)


def normalize(values, gain_vector):
    row_count = values.shape[0]
    by_head = values.astype(jnp.float32).reshape(row_count, -1, HEAD)
    inverse_rms = lax.rsqrt(jnp.mean(by_head * by_head, axis=-1, keepdims=True) + epsilon)
    return (by_head * inverse_rms * gain_vector.reshape(-1, HEAD)).astype(jnp.bfloat16)


def gather_plan(
    tokens, in_bits, qkv_weights, qkv_bits, gain_query, gain_key, out_weights, mix_bits, out_bits
):
    flipped = (tokens.astype(jnp.float32) * signed(in_bits)).astype(jnp.bfloat16)
    group_rows = lax.all_gather(jnp.stack([tokens, flipped]), "uly", axis=1, tiled=True)
    row_total = group_rows.shape[1]
    projections = jnp.einsum(
        "mrd,mkdc->rmkc",
        group_rows,
        lax.all_gather(qkv_weights, "blk", axis=2, tiled=True),
        preferred_element_type=jnp.float32,
    )
    projected = (projections[:, 0] + signed(qkv_bits) * projections[:, 1]).astype(jnp.bfloat16)
    queries = normalize(projected[:, 0], gain_query)
    head_count = queries.shape[1]
    keys_normed = normalize(projected[:, 1], gain_key).reshape(row_total, -1)
    values_block = projected[:, 2]
    score_scale = 1.0 / math.sqrt(HEAD)

    def attend(running, shard_piece):
        numerator, denominator = running
        key_rows = shard_piece[0].reshape(shard_piece[0].shape[0], head_count, HEAD)
        value_rows = shard_piece[1].reshape(shard_piece[1].shape[0], head_count, HEAD)
        scores = (
            jnp.einsum("rhd,nhd->hrn", queries, key_rows, preferred_element_type=jnp.float32)
            * score_scale
        )
        weights = jnp.exp(scores).astype(jnp.bfloat16)
        numerator = numerator + jnp.einsum(
            "hrn,nhd->rhd", weights, value_rows, preferred_element_type=jnp.float32
        )
        denominator = denominator + jnp.sum(weights.astype(jnp.float32), axis=2).T
        return (numerator, denominator)

    start_state = (
        jnp.zeros((row_total, head_count, HEAD), jnp.float32),
        jnp.zeros((row_total, head_count), jnp.float32),
    )
    all_keys, all_values = (
        lax.all_gather(keys_normed, "blk", axis=0, tiled=True),
        lax.all_gather(values_block, "blk", axis=0, tiled=True),
    )
    group_count = lax.axis_size("blk")
    per_block = 1
    while per_block * row_total < 512 and group_count % (per_block * 2) == 0:
        per_block = per_block * 2
    block_rows = per_block * row_total
    block_count = group_count // per_block
    key_blocks = all_keys.reshape(block_count, block_rows, all_keys.shape[1])
    value_blocks = all_values.reshape(block_count, block_rows, all_values.shape[1])

    def scan_step(running, block_pair):
        return (attend(running, block_pair), None)

    (numerator, denominator), unused = lax.scan(scan_step, start_state, (key_blocks, value_blocks))
    attended = (numerator / denominator[:, :, None]).astype(jnp.bfloat16).reshape(row_total, -1)
    attended_flipped = (attended.astype(jnp.float32) * signed(mix_bits)).astype(jnp.bfloat16)
    attended_pair = jnp.stack([attended, attended_flipped])
    out_signs = signed(out_bits)
    partial_out = jnp.einsum(
        "mrc,mcn->rmn",
        attended_pair,
        lax.all_gather(out_weights, "blk", axis=2, tiled=True),
        preferred_element_type=jnp.float32,
    )
    summed = lax.psum_scatter(
        partial_out.astype(jnp.bfloat16), "uly", scatter_dimension=0, tiled=True
    ).astype(jnp.float32)
    own_rows = summed.shape[0]
    own_signs = lax.dynamic_slice_in_dim(out_signs, lax.axis_index("uly") * own_rows, own_rows, 0)
    result_rows = summed[:, 0] + own_signs * summed[:, 1]
    return result_rows.astype(jnp.bfloat16)


def dot32(a, b):
    return lax.dot_general(
        a, b, (((1,), (0,)), ((), ())), preferred_element_type=jnp.float32
    )


def dot32_t(a, b):
    return lax.dot_general(
        a, b, (((1,), (1,)), ((), ())), preferred_element_type=jnp.float32
    )


def norm_rows(values, gain_row):
    wide = values.astype(jnp.float32)
    inverse_rms = lax.rsqrt(jnp.mean(wide * wide, axis=-1, keepdims=True) + epsilon)
    return (wide * inverse_rms * gain_row).astype(jnp.bfloat16)


def attend(queries, keys, values):
    scores = dot32_t(queries, keys) * (1.0 / math.sqrt(HEAD))
    weights = jnp.exp(scores).astype(jnp.bfloat16)
    totals = jnp.sum(weights.astype(jnp.float32), axis=1, keepdims=True)
    return (dot32(weights, values) / totals).astype(jnp.bfloat16)


def stationary_plan(
    tokens, in_bits, qkv_weights, qkv_bits, gain_query, gain_key, out_weights, mix_bits, out_bits
):
    groups = lax.axis_size("blk")
    team = lax.axis_size("uly")
    depth = groups // 2
    z = lax.axis_index("blk") // 2
    x = lax.axis_index("blk") % 2
    u = lax.axis_index("uly")
    own_rows, width = tokens.shape
    slab = qkv_weights.shape[2]
    columns = qkv_weights.shape[3]
    group_rows = own_rows * team
    heads = columns // HEAD
    half_rows = depth * group_rows
    lines = [[2 * i + j for i in range(depth)] for j in (0, 1)]
    bf = jnp.bfloat16

    def swap_x(value):
        return lax.ppermute(value, "blk", [(i, i ^ 1) for i in range(groups)])

    def swap_u(value, bit):
        return lax.ppermute(value, "uly", [(i, i ^ bit) for i in range(team)])

    def exchange_z(value):
        return lax.all_to_all(value, "blk", 0, 0, axis_index_groups=lines)

    def spread_z(value):
        return exchange_z(jnp.broadcast_to(value[None], (depth,) + value.shape))

    def after(value, earlier):
        return lax.optimization_barrier((value, earlier))[0]

    signs_own = jnp.transpose(2 * qkv_bits - 1, (1, 0, 2)).astype(bf)
    signs_all = lax.all_gather(signs_own, "blk", axis=0, axis_index_groups=lines)

    partner = {2: swap_x(qkv_weights[:, 2])}
    partner[1] = swap_x(after(qkv_weights[:, 1], partner[2]))
    partner[0] = swap_x(after(qkv_weights[:, 0], partner[1]))
    out_t = jnp.transpose(out_weights, (0, 2, 1))
    out_partner = swap_x(after(out_t, partner[0]))

    flipped = (tokens.astype(jnp.float32) * signed(in_bits)).astype(bf)
    pair = jnp.stack([tokens, flipped]).reshape(2, own_rows, depth, 2 * slab)
    held = exchange_z(jnp.transpose(pair, (2, 0, 1, 3)))
    rows = lax.all_gather(held, "uly", axis=0)
    rows = jnp.transpose(rows, (2, 1, 0, 3, 4)).reshape(2, half_rows, 2 * slab)

    def project(part):
        total = []
        for m in (0, 1):
            own, other = qkv_weights[m, part], partner[part][m]
            full = jnp.where(
                x == 0,
                jnp.concatenate([own, other], axis=0),
                jnp.concatenate([other, own], axis=0),
            )
            total.append(dot32(rows[m], full))
        signs = signs_all[:, part].reshape(half_rows, columns).astype(jnp.float32)
        partial = (total[0] + signs * total[1]).astype(bf)
        shared = partial[:, depth * HEAD :]
        blocks = [
            jnp.concatenate(
                [
                    partial[:, k * HEAD : (k + 1) * HEAD],
                    shared[k * group_rows : (k + 1) * group_rows],
                ],
                axis=0,
            )
            for k in range(depth)
        ]
        got = exchange_z(jnp.stack(blocks)).astype(jnp.float32)
        done = jnp.sum(got, axis=0).astype(bf)
        return done[:half_rows], done[half_rows:]

    gain_q = gain_query.reshape(heads, HEAD)
    gain_k = gain_key.reshape(heads, HEAD)

    def gains(table):
        return lax.dynamic_slice_in_dim(table, z, 1, 0), table[depth : depth + 1]

    value_main, value_rest = project(2)
    key_main, key_rest = project(1)
    gain_main, gain_rest = gains(gain_k)
    key_main, key_rest = norm_rows(key_main, gain_main), norm_rows(key_rest, gain_rest)
    rest_all = spread_z(jnp.concatenate([key_rest, value_rest], axis=1))
    rest_all = rest_all.reshape(half_rows, 2 * HEAD)
    sent = jnp.concatenate([key_main, value_main, rest_all], axis=1)
    taken = swap_x(sent)
    keys_values = jnp.concatenate([sent, taken], axis=0)

    mix = spread_z(after((2 * mix_bits - 1).astype(bf), key_rest)).reshape(half_rows, columns)
    query_main, query_rest = project(0)
    gain_main, gain_rest = gains(gain_q)
    query_main, query_rest = norm_rows(query_main, gain_main), norm_rows(query_rest, gain_rest)

    done_main = attend(query_main, keys_values[:, :HEAD], keys_values[:, HEAD : 2 * HEAD])
    done_rest = attend(
        query_rest, keys_values[:, 2 * HEAD : 3 * HEAD], keys_values[:, 3 * HEAD :]
    )
    done = spread_z(jnp.concatenate([done_main, done_rest], axis=0))
    main = jnp.transpose(done[:, :half_rows], (1, 0, 2)).reshape(half_rows, depth * HEAD)
    attended = jnp.concatenate([main, done[:, half_rows:].reshape(half_rows, HEAD)], axis=1)
    attended_flipped = attended * mix
    first = jnp.where(x == 0, out_t, out_partner)
    second = jnp.where(x == 0, out_partner, out_t)
    out_full = jnp.concatenate([first, second], axis=1)
    partial = jnp.stack(
        [dot32_t(attended, out_full[0]), dot32_t(attended_flipped, out_full[1])]
    ).astype(bf)
    partial = partial.reshape(2, depth, 2, 2, own_rows, 2 * slab)
    core = u % 2
    y = u // 2
    keep = lax.dynamic_index_in_dim(partial, core, 3, keepdims=False)
    send = lax.dynamic_index_in_dim(partial, 1 - core, 3, keepdims=False)
    summed = keep.astype(jnp.float32) + swap_u(send, 1).astype(jnp.float32)
    keep = lax.dynamic_index_in_dim(summed, y, 2, keepdims=False)
    send = lax.dynamic_index_in_dim(summed, 1 - y, 2, keepdims=False).astype(bf)
    summed = (keep + swap_u(send, 2).astype(jnp.float32)).astype(bf)
    final = exchange_z(jnp.transpose(summed, (1, 0, 2, 3)))
    final = jnp.transpose(final, (1, 2, 0, 3)).reshape(2, own_rows, width).astype(jnp.float32)
    own_bits = lax.dynamic_slice_in_dim(out_bits, u * own_rows, own_rows, 0)
    return (final[0] + signed(own_bits) * final[1]).astype(bf)


def body(*arrays):
    heads = arrays[2].shape[3] // HEAD
    depth = lax.axis_size("blk") // 2
    if depth == heads - 1 and depth & (depth - 1) == 0 and lax.axis_size("uly") == 4:
        return stationary_plan(*arrays)
    return gather_plan(*arrays)


def solution(mesh):
    return jax.shard_map(
        body,
        mesh=mesh,
        in_specs=(
            P(("blk", "uly"), None),
            P(("blk", "uly"), None),
            P(None, None, "blk", "uly"),
            P("blk", None, "uly"),
            P("uly"),
            P("uly"),
            P(None, "uly", "blk"),
            P("blk", "uly"),
            P("blk", None),
        ),
        out_specs=P(("blk", "uly"), None),
        check_vma=False,
    )
```

```python
import functools
import math

import jax
import jax.numpy as jnp
from jax import lax
from jax.experimental import pallas as pl
from jax.experimental.pallas import tpu as pltpu
from jax.sharding import PartitionSpec as P

HEAD = 128


epsilon = 1e-06


def signed(bit_values):
    return (2 * bit_values - 1).astype(jnp.float32)


def normalize(values, gain_vector):
    row_count = values.shape[0]
    by_head = values.astype(jnp.float32).reshape(row_count, -1, HEAD)
    inverse_rms = lax.rsqrt(jnp.mean(by_head * by_head, axis=-1, keepdims=True) + epsilon)
    return (by_head * inverse_rms * gain_vector.reshape(-1, HEAD)).astype(jnp.bfloat16)


def gather_plan(
    tokens, in_bits, qkv_weights, qkv_bits, gain_query, gain_key, out_weights, mix_bits, out_bits
):
    flipped = (tokens.astype(jnp.float32) * signed(in_bits)).astype(jnp.bfloat16)
    group_rows = lax.all_gather(jnp.stack([tokens, flipped]), "uly", axis=1, tiled=True)
    row_total = group_rows.shape[1]
    projections = jnp.einsum(
        "mrd,mkdc->rmkc",
        group_rows,
        lax.all_gather(qkv_weights, "blk", axis=2, tiled=True),
        preferred_element_type=jnp.float32,
    )
    projected = (projections[:, 0] + signed(qkv_bits) * projections[:, 1]).astype(jnp.bfloat16)
    queries = normalize(projected[:, 0], gain_query)
    head_count = queries.shape[1]
    keys_normed = normalize(projected[:, 1], gain_key).reshape(row_total, -1)
    values_block = projected[:, 2]
    score_scale = 1.0 / math.sqrt(HEAD)

    def attend(running, shard_piece):
        numerator, denominator = running
        key_rows = shard_piece[0].reshape(shard_piece[0].shape[0], head_count, HEAD)
        value_rows = shard_piece[1].reshape(shard_piece[1].shape[0], head_count, HEAD)
        scores = (
            jnp.einsum("rhd,nhd->hrn", queries, key_rows, preferred_element_type=jnp.float32)
            * score_scale
        )
        weights = jnp.exp(scores).astype(jnp.bfloat16)
        numerator = numerator + jnp.einsum(
            "hrn,nhd->rhd", weights, value_rows, preferred_element_type=jnp.float32
        )
        denominator = denominator + jnp.sum(weights.astype(jnp.float32), axis=2).T
        return (numerator, denominator)

    start_state = (
        jnp.zeros((row_total, head_count, HEAD), jnp.float32),
        jnp.zeros((row_total, head_count), jnp.float32),
    )
    all_keys, all_values = (
        lax.all_gather(keys_normed, "blk", axis=0, tiled=True),
        lax.all_gather(values_block, "blk", axis=0, tiled=True),
    )
    group_count = lax.axis_size("blk")
    per_block = 1
    while per_block * row_total < 512 and group_count % (per_block * 2) == 0:
        per_block = per_block * 2
    block_rows = per_block * row_total
    block_count = group_count // per_block
    key_blocks = all_keys.reshape(block_count, block_rows, all_keys.shape[1])
    value_blocks = all_values.reshape(block_count, block_rows, all_values.shape[1])

    def scan_step(running, block_pair):
        return (attend(running, block_pair), None)

    (numerator, denominator), unused = lax.scan(scan_step, start_state, (key_blocks, value_blocks))
    attended = (numerator / denominator[:, :, None]).astype(jnp.bfloat16).reshape(row_total, -1)
    attended_flipped = (attended.astype(jnp.float32) * signed(mix_bits)).astype(jnp.bfloat16)
    attended_pair = jnp.stack([attended, attended_flipped])
    out_signs = signed(out_bits)
    partial_out = jnp.einsum(
        "mrc,mcn->rmn",
        attended_pair,
        lax.all_gather(out_weights, "blk", axis=2, tiled=True),
        preferred_element_type=jnp.float32,
    )
    summed = lax.psum_scatter(
        partial_out.astype(jnp.bfloat16), "uly", scatter_dimension=0, tiled=True
    ).astype(jnp.float32)
    own_rows = summed.shape[0]
    own_signs = lax.dynamic_slice_in_dim(out_signs, lax.axis_index("uly") * own_rows, own_rows, 0)
    result_rows = summed[:, 0] + own_signs * summed[:, 1]
    return result_rows.astype(jnp.bfloat16)


def dot32(a, b):
    return lax.dot_general(
        a, b, (((1,), (0,)), ((), ())), preferred_element_type=jnp.float32
    )


def dot32_t(a, b):
    return lax.dot_general(
        a, b, (((1,), (1,)), ((), ())), preferred_element_type=jnp.float32
    )


bf = jnp.bfloat16
VMEM = pl.BlockSpec(memory_space=pltpu.VMEM)
SMEM = pl.BlockSpec(memory_space=pltpu.SMEM)
ANY = pl.BlockSpec(memory_space=pl.ANY)


def call(kernel, outs, out_specs, in_specs, scratch=(), flops=0, moved=0):
    return pl.pallas_call(
        kernel,
        out_shape=outs,
        in_specs=in_specs,
        out_specs=out_specs,
        scratch_shapes=list(scratch),
        compiler_params=pltpu.CompilerParams(vmem_limit_bytes=40 * 1024 * 1024),
        cost_estimate=pl.CostEstimate(flops=flops, bytes_accessed=moved, transcendentals=0),
    )


def shape(*dims, dtype=bf):
    return jax.ShapeDtypeStruct(dims, dtype)


def lanes(index, size):
    return pl.ds(pl.multiple_of(index * size, 128), size)


def prepare_kernel(place, tokens, in_bits, sign_bits, weights, value_weights, signs, *blocks):
    copies = [
        pltpu.make_async_copy(weights.at[m, 2], value_weights.at[m], blocks[-1].at[m])
        for m in (0, 1)
    ]
    for copy in copies:
        copy.start()
    z = place[0]
    depth = len(blocks) - 1
    wide = tokens.shape[1] // depth
    for k in range(depth):
        cut = lanes(z ^ k, wide)
        plain = tokens[:, cut]
        sign = (2 * in_bits[:, cut] - 1).astype(jnp.float32)
        blocks[k][0] = plain
        blocks[k][1] = (plain.astype(jnp.float32) * sign).astype(bf)
    signs[...] = (2 * sign_bits[2] - 1).astype(jnp.float32).astype(bf)
    for copy in copies:
        copy.wait()


def rest_kernel(sign_bits, mix_bits, weights, key_weights, query_a, query_b, signs, mix, sems):
    pieces = ((1, 0, key_weights.at[0]), (1, 1, key_weights.at[1]), (0, 0, query_a), (0, 1, query_b))
    copies = [
        pltpu.make_async_copy(weights.at[m, part], out, sems.at[part, m])
        for part, m, out in pieces
    ]
    for copy in copies:
        copy.start()
    for part in (0, 1):
        signs[part] = (2 * sign_bits[part] - 1).astype(jnp.float32).astype(bf)
    mix[...] = (2 * mix_bits[...] - 1).astype(jnp.float32).astype(bf)
    for copy in copies:
        copy.wait()


def project_kernel(
    part, whole, place, rows, weights, partner_0, partner_1, sign_0, sign_2, sign_13,
    send, keep_own, keep_two, held, total, sems,
):
    z, x = place[0], place[1]
    slab, columns = weights.shape[2], weights.shape[3]
    partner = (partner_0, partner_1)
    if len(partner_0.shape) == 3:
        partner = (partner_0.at[0], partner_0.at[1])
    own = pl.ds(pl.multiple_of(x * slab, 64), slab)
    other = pl.ds(pl.multiple_of((1 - x) * slab, 64), slab)
    copies = []
    for m in (0, 1):
        copies.append(
            pltpu.make_async_copy(weights.at[m, part], held.at[m, own], sems.at[m, 0])
        )
        copies.append(pltpu.make_async_copy(partner[m], held.at[m, other], sems.at[m, 1]))
    for copy in copies:
        copy.start()
    for copy in copies:
        copy.wait()
    size = sign_0.shape[0]
    depth = rows.shape[1] // size
    total[...] = dot32(rows[1], held[1])
    plain = dot32(rows[0], held[0])
    for j in range(depth):
        cut = slice(j * size, (j + 1) * size)
        sign = (sign_0[...], sign_13[0], sign_2[...], sign_13[1])[j].astype(jnp.float32)
        total[cut] = plain[cut] + sign * total[cut]

    def block(j, head):
        return total[j * size : (j + 1) * size, lanes(head, HEAD)]

    def main(target, start, k):
        for j in range(depth):
            at = start + (j ^ k) * size
            target[at : at + size] = block(j, z ^ k).astype(target.dtype)

    def rest(target, start, j):
        target[start : start + size] = block(j, depth).astype(target.dtype)

    half = depth * size
    if whole:
        main(send, 0, 1)
        main(send, half, 3)
        for j in range(depth):
            rest(send, 2 * half + (j ^ 1) * size, j)
            rest(keep_own, half + j * size, j)
    else:
        main(send, 0, 1)
        rest(send, half, 1)
        main(send, half + size, 3)
        rest(send, 2 * half + size, 3)
        rest(keep_own, half, 0)
        rest(keep_two, half, 2)
    main(keep_own, 0, 0)
    main(keep_two, 0, 2)


def middle_kernel(size, keep_own, keep_two, taken, send, total):
    half = 4 * size
    if taken.shape[0] == 3 * half:
        total[:half] = keep_own[:half] + taken[:half].astype(jnp.float32)
        send[:half] = (keep_two[...] + taken[half : 2 * half].astype(jnp.float32)).astype(bf)
        for j in range(4):
            cut = slice(half + j * size, half + (j + 1) * size)
            got = taken[half + cut.start : half + cut.stop].astype(jnp.float32)
            value = keep_own[cut] + got
            total[cut] = value
            at = half + (j ^ 2) * size
            send[at : at + size] = value.astype(bf)
    else:
        count = half + size
        total[...] = keep_own[...] + taken[:count].astype(jnp.float32)
        send[...] = (keep_two[...] + taken[count:].astype(jnp.float32)).astype(bf)


def norm_rows(values, gain_row):
    wide = values.astype(jnp.float32)
    inverse_rms = lax.rsqrt(jnp.mean(wide * wide, axis=-1, keepdims=True) + epsilon)
    return (wide * inverse_rms * gain_row).astype(bf)


def key_kernel(half, place, total, taken, gain, keys):
    keep = (total[...] + taken[...].astype(jnp.float32)).astype(bf)
    heads = gain.shape[0]
    keys[:half] = norm_rows(keep[:half], gain[pl.ds(place[0], 1), :])
    keys[half:] = norm_rows(keep[half:], gain[heads - 1 : heads, :])


def attend_kernel(half, place, total, taken, gain, keys_a, keys_b, values_a, values_b, out):
    keep = (total[...] + taken[...].astype(jnp.float32)).astype(bf)
    heads = gain.shape[0]

    def attend(queries, cut):
        score_scale = 1.0 / math.sqrt(HEAD)
        totals, sums = 0.0, 0.0
        for keys, values in ((keys_a, values_a), (keys_b, values_b)):
            scores = dot32_t(queries, keys[cut]) * score_scale
            weights = jnp.exp(scores).astype(bf)
            totals = totals + jnp.sum(weights.astype(jnp.float32), axis=1, keepdims=True)
            sums = sums + dot32(weights, values[cut])
        return (sums / totals).astype(bf)

    first = norm_rows(keep[:half], gain[pl.ds(place[0], 1), :])
    out[:half] = attend(first, slice(0, half))
    last = norm_rows(keep[half:], gain[heads - 1 : heads, :])
    out[half:] = attend(last, slice(half, 2 * half))


def stationary_plan(
    tokens, in_bits, qkv_weights, qkv_bits, gain_query, gain_key, out_weights, mix_bits, out_bits
):
    groups = lax.axis_size("blk")
    team = lax.axis_size("uly")
    depth = groups // 2
    z = lax.axis_index("blk") // 2
    x = lax.axis_index("blk") % 2
    u = lax.axis_index("uly")
    own_rows, width = tokens.shape
    slab = qkv_weights.shape[2]
    columns = qkv_weights.shape[3]
    size = own_rows * team
    heads = columns // HEAD
    half = depth * size
    steps = range(depth)
    place = jnp.stack([z, x]).astype(jnp.int32)

    def swap_x(value):
        return lax.ppermute(value, "blk", [(i, i ^ 1) for i in range(groups)])

    def swap_z(value, step):
        return lax.ppermute(value, "blk", [(i, i ^ (2 * step)) for i in range(groups)])

    def swap_u(value, bit):
        return lax.ppermute(value, "uly", [(i, i ^ bit) for i in range(team)])

    def after(value, *earlier):
        return lax.optimization_barrier((value,) + earlier)[0]

    def gather_z(value):
        two = swap_z(value, 2)
        return value, two, swap_z(jnp.stack([value, two]), 1)

    sign_bits = jnp.transpose(qkv_bits, (1, 0, 2))
    weights_shape = shape(2, slab, columns)
    prepared = call(
        prepare_kernel,
        [weights_shape, shape(size, columns)] + [shape(2, own_rows, 2 * slab)] * depth,
        [ANY] + [VMEM] * (depth + 1),
        [SMEM] + [VMEM] * 3 + [ANY],
        [pltpu.SemaphoreType.DMA((2,))],
    )(place, tokens, in_bits, sign_bits, qkv_weights)
    value_weights, sign_value, blocks = prepared[0], prepared[1], prepared[2:]
    partner = {2: [swap_x(value_weights)] * 2}
    held = [blocks[0]] + [swap_z(blocks[k], k) for k in steps if k]
    signs = {2: gather_z(sign_value)}

    piece_shape = shape(slab, columns)
    key_weights, query_a, query_b, sign_pair, mix_own = call(
        rest_kernel,
        [weights_shape, piece_shape, piece_shape, shape(2, size, columns), shape(size, columns)],
        [ANY, ANY, ANY, VMEM, VMEM],
        [VMEM, VMEM, ANY],
        [pltpu.SemaphoreType.DMA((2, 2))],
    )(after(sign_bits, value_weights), mix_bits, qkv_weights)
    rows = lax.all_gather(jnp.stack(held), "uly", axis=0)
    rows = jnp.transpose(rows, (2, 1, 0, 3, 4)).reshape(2, half, 2 * slab)

    partner[1] = [swap_x(after(key_weights, partner[2][0], rows))] * 2
    query_a = swap_x(after(query_a, partner[1][0]))
    query_b = swap_x(after(query_b, query_a))
    partner[0] = [query_a, query_b]
    out_t = jnp.transpose(out_weights, (0, 2, 1))
    out_partner = swap_x(after(out_t, query_b))

    pair_0, pair_2, pair_13 = gather_z(after(sign_pair, signs[2][2]))
    for part in (0, 1):
        signs[part] = (pair_0[part], pair_2[part], pair_13[:, part])

    def project(part, whole, rows, beside=()):
        count = 2 * half if whole else half + size
        f32 = jnp.float32
        send, keep_own, keep_two = call(
            functools.partial(project_kernel, part, whole),
            [
                shape(3 * half if whole else 2 * count, HEAD),
                shape(count, HEAD, dtype=f32),
                shape(half if whole else count, HEAD, dtype=f32),
            ],
            [VMEM] * 3,
            [SMEM, VMEM, ANY, ANY, ANY, VMEM, VMEM, VMEM],
            [
                pltpu.VMEM((2, 2 * slab, columns), bf),
                pltpu.VMEM((half, columns), f32),
                pltpu.SemaphoreType.DMA((2, 2)),
            ],
        )(place, rows, qkv_weights, *partner[part], *signs[part])
        taken = after(swap_z(send, 1), *beside)
        send, total = call(
            functools.partial(middle_kernel, size),
            [shape(count, HEAD), shape(count, HEAD, dtype=f32)],
            [VMEM] * 2,
            [VMEM] * 3,
        )(keep_own, keep_two, taken)
        return total, swap_z(send, 2)

    total, taken = project(2, True, rows)
    values = (total + taken.astype(jnp.float32)).astype(bf)
    rows_next = after(rows, values)
    values_partner = swap_x(values)
    total, taken = project(1, True, rows_next, (query_a,))
    rows_next = after(rows, total)
    taken = after(taken, query_b)
    keys = call(
        functools.partial(key_kernel, half), shape(2 * half, HEAD), VMEM, [SMEM] + [VMEM] * 3
    )(place, total, taken, gain_key.reshape(heads, HEAD))
    keys_partner = swap_x(keys)
    mix_0, mix_2, mix_13 = gather_z(after(mix_own, keys))
    total, taken = project(0, False, rows_next)
    done = call(
        functools.partial(attend_kernel, half),
        shape(half + size, HEAD),
        VMEM,
        [SMEM] + [VMEM] * 7,
    )(
        place, total, taken, gain_query.reshape(heads, HEAD),
        keys, keys_partner, values, values_partner,
    )
    done_0, done_2, done_13 = gather_z(done)

    by_head, last_head = [], []
    for k, block in enumerate((done_0, done_13[0], done_2, done_13[1])):
        main = block[:half].reshape(depth, size, HEAD)
        by_head.append(jnp.concatenate([main[j ^ k] for j in steps], axis=0))
        last_head.append(block[half:])
    attended = jnp.concatenate(by_head + [jnp.concatenate(last_head, axis=0)], axis=1)

    def relative(value, axis):
        parts = [
            lax.dynamic_slice_in_dim(value, (z ^ k) * HEAD, HEAD, axis) for k in steps
        ] + [lax.slice_in_dim(value, depth * HEAD, heads * HEAD, axis=axis)]
        return jnp.concatenate(parts, axis=axis)

    mix = relative(jnp.concatenate([mix_0, mix_13[0], mix_2, mix_13[1]], axis=0), 1)
    attended_flipped = attended * mix
    first = jnp.where(x == 0, out_t, out_partner)
    second = jnp.where(x == 0, out_partner, out_t)
    out_full = relative(jnp.concatenate([first, second], axis=1), 2)
    partial = jnp.stack(
        [dot32_t(attended, out_full[0]), dot32_t(attended_flipped, out_full[1])]
    ).astype(bf)
    partial = partial.reshape(2, depth, 2, 2, own_rows, 2 * slab)
    core = u % 2
    y = u // 2
    keep = lax.dynamic_index_in_dim(partial, core, 3, keepdims=False)
    send = lax.dynamic_index_in_dim(partial, 1 - core, 3, keepdims=False)
    summed = keep.astype(jnp.float32) + swap_u(send, 1).astype(jnp.float32)
    keep = lax.dynamic_index_in_dim(summed, y, 2, keepdims=False)
    send = lax.dynamic_index_in_dim(summed, 1 - y, 2, keepdims=False).astype(bf)
    summed = (keep + swap_u(send, 2).astype(jnp.float32)).astype(bf)
    final = [summed[:, 0]] + [swap_z(summed[:, k], k) for k in steps if k]
    placed = jnp.zeros((2, own_rows, depth, 2 * slab), bf)
    for k in steps:
        placed = lax.dynamic_update_slice_in_dim(placed, final[k][:, :, None], z ^ k, 2)
    placed = placed.reshape(2, own_rows, width).astype(jnp.float32)
    own_bits = lax.dynamic_slice_in_dim(out_bits, u * own_rows, own_rows, 0)
    return (placed[0] + signed(own_bits) * placed[1]).astype(bf)


def body(*arrays):
    heads = arrays[2].shape[3] // HEAD
    depth = lax.axis_size("blk") // 2
    if depth == heads - 1 and depth == 4 and lax.axis_size("uly") == 4:
        return stationary_plan(*arrays)
    return gather_plan(*arrays)


def solution(mesh):
    return jax.shard_map(
        body,
        mesh=mesh,
        in_specs=(
            P(("blk", "uly"), None),
            P(("blk", "uly"), None),
            P(None, None, "blk", "uly"),
            P("blk", None, "uly"),
            P("uly"),
            P("uly"),
            P(None, "uly", "blk"),
            P("blk", "uly"),
            P("blk", None),
        ),
        out_specs=P(("blk", "uly"), None),
        check_vma=False,
    )
```

```python
import functools
import math

import jax
import jax.numpy as jnp
from jax import lax
from jax.experimental import pallas as pl
from jax.experimental.pallas import tpu as pltpu
from jax.sharding import PartitionSpec as P

HEAD = 128


epsilon = 1e-06


def signed(bit_values):
    return (2 * bit_values - 1).astype(jnp.float32)


def normalize(values, gain_vector):
    row_count = values.shape[0]
    by_head = values.astype(jnp.float32).reshape(row_count, -1, HEAD)
    inverse_rms = lax.rsqrt(jnp.mean(by_head * by_head, axis=-1, keepdims=True) + epsilon)
    return (by_head * inverse_rms * gain_vector.reshape(-1, HEAD)).astype(jnp.bfloat16)


def gather_plan(
    tokens, in_bits, qkv_weights, qkv_bits, gain_query, gain_key, out_weights, mix_bits, out_bits
):
    flipped = (tokens.astype(jnp.float32) * signed(in_bits)).astype(jnp.bfloat16)
    group_rows = lax.all_gather(jnp.stack([tokens, flipped]), "uly", axis=1, tiled=True)
    row_total = group_rows.shape[1]
    projections = jnp.einsum(
        "mrd,mkdc->rmkc",
        group_rows,
        lax.all_gather(qkv_weights, "blk", axis=2, tiled=True),
        preferred_element_type=jnp.float32,
    )
    projected = (projections[:, 0] + signed(qkv_bits) * projections[:, 1]).astype(jnp.bfloat16)
    queries = normalize(projected[:, 0], gain_query)
    head_count = queries.shape[1]
    keys_normed = normalize(projected[:, 1], gain_key).reshape(row_total, -1)
    values_block = projected[:, 2]
    score_scale = 1.0 / math.sqrt(HEAD)

    def attend(running, shard_piece):
        numerator, denominator = running
        key_rows = shard_piece[0].reshape(shard_piece[0].shape[0], head_count, HEAD)
        value_rows = shard_piece[1].reshape(shard_piece[1].shape[0], head_count, HEAD)
        scores = (
            jnp.einsum("rhd,nhd->hrn", queries, key_rows, preferred_element_type=jnp.float32)
            * score_scale
        )
        weights = jnp.exp(scores).astype(jnp.bfloat16)
        numerator = numerator + jnp.einsum(
            "hrn,nhd->rhd", weights, value_rows, preferred_element_type=jnp.float32
        )
        denominator = denominator + jnp.sum(weights.astype(jnp.float32), axis=2).T
        return (numerator, denominator)

    start_state = (
        jnp.zeros((row_total, head_count, HEAD), jnp.float32),
        jnp.zeros((row_total, head_count), jnp.float32),
    )
    all_keys, all_values = (
        lax.all_gather(keys_normed, "blk", axis=0, tiled=True),
        lax.all_gather(values_block, "blk", axis=0, tiled=True),
    )
    group_count = lax.axis_size("blk")
    per_block = 1
    while per_block * row_total < 512 and group_count % (per_block * 2) == 0:
        per_block = per_block * 2
    block_rows = per_block * row_total
    block_count = group_count // per_block
    key_blocks = all_keys.reshape(block_count, block_rows, all_keys.shape[1])
    value_blocks = all_values.reshape(block_count, block_rows, all_values.shape[1])

    def scan_step(running, block_pair):
        return (attend(running, block_pair), None)

    (numerator, denominator), unused = lax.scan(scan_step, start_state, (key_blocks, value_blocks))
    attended = (numerator / denominator[:, :, None]).astype(jnp.bfloat16).reshape(row_total, -1)
    attended_flipped = (attended.astype(jnp.float32) * signed(mix_bits)).astype(jnp.bfloat16)
    attended_pair = jnp.stack([attended, attended_flipped])
    out_signs = signed(out_bits)
    partial_out = jnp.einsum(
        "mrc,mcn->rmn",
        attended_pair,
        lax.all_gather(out_weights, "blk", axis=2, tiled=True),
        preferred_element_type=jnp.float32,
    )
    summed = lax.psum_scatter(
        partial_out.astype(jnp.bfloat16), "uly", scatter_dimension=0, tiled=True
    ).astype(jnp.float32)
    own_rows = summed.shape[0]
    own_signs = lax.dynamic_slice_in_dim(out_signs, lax.axis_index("uly") * own_rows, own_rows, 0)
    result_rows = summed[:, 0] + own_signs * summed[:, 1]
    return result_rows.astype(jnp.bfloat16)


def dot32(a, b):
    return lax.dot_general(
        a, b, (((1,), (0,)), ((), ())), preferred_element_type=jnp.float32
    )


def dot32_t(a, b):
    return lax.dot_general(
        a, b, (((1,), (1,)), ((), ())), preferred_element_type=jnp.float32
    )


bf = jnp.bfloat16
VMEM = pl.BlockSpec(memory_space=pltpu.VMEM)
SMEM = pl.BlockSpec(memory_space=pltpu.SMEM)
ANY = pl.BlockSpec(memory_space=pl.ANY)


def call(kernel, outs, out_specs, in_specs, scratch=(), flops=0, moved=0):
    return pl.pallas_call(
        kernel,
        out_shape=outs,
        in_specs=in_specs,
        out_specs=out_specs,
        scratch_shapes=list(scratch),
        compiler_params=pltpu.CompilerParams(vmem_limit_bytes=40 * 1024 * 1024),
        cost_estimate=pl.CostEstimate(flops=flops, bytes_accessed=moved, transcendentals=0),
    )


def shape(*dims, dtype=bf):
    return jax.ShapeDtypeStruct(dims, dtype)


def lanes(index, size):
    return pl.ds(pl.multiple_of(index * size, 128), size)


def copy_kernel(part, weights, out, sems):
    copies = [
        pltpu.make_async_copy(weights.at[m, part], out.at[m], sems.at[m]) for m in (0, 1)
    ]
    for copy in copies:
        copy.start()
    for copy in copies:
        copy.wait()


def prepare_kernel(place, tokens, in_bits, *blocks):
    z = place[0]
    wide = tokens.shape[1] // len(blocks)
    for k, block in enumerate(blocks):
        cut = lanes(z ^ k, wide)
        plain = tokens[:, cut]
        sign = (2 * in_bits[:, cut] - 1).astype(jnp.float32)
        block[0] = plain
        block[1] = (plain.astype(jnp.float32) * sign).astype(bf)


def relative_signs(bits, u, team):
    piece = bits.shape[0] // team
    parts = [bits[pl.ds(pl.multiple_of((u ^ r) * piece, 8), piece), :] for r in range(team)]
    return (2 * jnp.concatenate(parts, axis=0) - 1).astype(jnp.float32).astype(bf)


def sign_kernel(team, place, sign_bits, signs):
    signs[...] = relative_signs(sign_bits.at[2], place[2], team)


def rest_kernel(
    team, place, sign_bits, mix_bits, weights, key_weights, query_a, query_b, signs, mix, sems
):
    pieces = ((1, 0, key_weights.at[0]), (1, 1, key_weights.at[1]), (0, 0, query_a), (0, 1, query_b))
    copies = [
        pltpu.make_async_copy(weights.at[m, part], out, sems.at[part, m])
        for part, m, out in pieces
    ]
    for copy in copies:
        copy.start()
    for part in (0, 1):
        signs[part] = relative_signs(sign_bits.at[part], place[2], team)
    mix[...] = relative_signs(mix_bits, place[2], team)
    for copy in copies:
        copy.wait()


def project_kernel(part, size, place, rows, weights, partner_0, partner_1, *refs):
    held, total, sems = refs[-3:]
    z, x = place[0], place[1]
    slab = weights.shape[2]
    partner = (partner_0, partner_1)
    if len(partner_0.shape) == 3:
        partner = (partner_0.at[0], partner_0.at[1])
    own = pl.ds(pl.multiple_of(x * slab, 64), slab)
    other = pl.ds(pl.multiple_of((1 - x) * slab, 64), slab)
    copies = []
    for m in (0, 1):
        copies.append(
            pltpu.make_async_copy(weights.at[m, part], held.at[m, own], sems.at[m, 0])
        )
        copies.append(pltpu.make_async_copy(partner[m], held.at[m, other], sems.at[m, 1]))
    for copy in copies:
        copy.start()
    for copy in copies:
        copy.wait()
    if part == 2:
        outs = refs[4:-3]
        signs = [ref[...] for ref in refs[:4]]
    else:
        outs = refs[3:-3]
        pair_0, pair_2, pair_13 = refs[:3]
        signs = [pair_0[part], pair_13[0, part], pair_2[part], pair_13[1, part]]
    depth = rows.shape[1] // size
    total[...] = dot32(rows[1], held[1])
    plain = dot32(rows[0], held[0])
    for j in range(depth):
        cut = slice(j * size, (j + 1) * size)
        total[cut] = plain[cut] + signs[j].astype(jnp.float32) * total[cut]

    def block(j, head):
        return total[j * size : (j + 1) * size, lanes(head, HEAD)]

    def main(target, start, k):
        for j in range(depth):
            at = start + (j ^ k) * size
            target[at : at + size] = block(j, z ^ k).astype(target.dtype)

    def rest(target, start, j):
        target[start : start + size] = block(j, depth).astype(target.dtype)

    half = depth * size
    if part:
        send, keep_own, keep_two = outs
        main(send, 0, 1)
        main(send, half, 3)
        for j in range(depth):
            rest(send, 2 * half + (j ^ 1) * size, j)
            rest(keep_own, half + j * size, j)
        main(keep_own, 0, 0)
        main(keep_two, 0, 2)
    else:
        for k in range(depth):
            main(outs[k], 0, k)
            rest(outs[k], half, k)


def middle_kernel(size, keep_own, keep_two, taken, send, total):
    half = keep_two.shape[0]
    total[:half] = keep_own[:half] + taken[:half].astype(jnp.float32)
    send[:half] = (keep_two[...] + taken[half : 2 * half].astype(jnp.float32)).astype(bf)
    for j in range(half // size):
        cut = slice(half + j * size, half + (j + 1) * size)
        got = taken[half + cut.start : half + cut.stop].astype(jnp.float32)
        value = keep_own[cut] + got
        total[cut] = value
        at = half + (j ^ 2) * size
        send[at : at + size] = value.astype(bf)


def norm_rows(values, gain_row):
    wide = values.astype(jnp.float32)
    inverse_rms = lax.rsqrt(jnp.mean(wide * wide, axis=-1, keepdims=True) + epsilon)
    return (wide * inverse_rms * gain_row).astype(bf)


def key_kernel(half, place, total, taken, gain, keys):
    keep = (total[...] + taken[...].astype(jnp.float32)).astype(bf)
    heads = gain.shape[0]
    keys[:half] = norm_rows(keep[:half], gain[pl.ds(place[0], 1), :])
    keys[half:] = norm_rows(keep[half:], gain[heads - 1 : heads, :])


def attend_kernel(
    half, place, total, taken_1, taken_2, taken_3, gain, keys_a, keys_b, values_a, values_b, out
):
    keep = total[...]
    for taken in (taken_1, taken_2, taken_3):
        keep = keep + taken[...].astype(jnp.float32)
    keep = keep.astype(bf)
    heads = gain.shape[0]

    def attend(queries, cut):
        score_scale = 1.0 / math.sqrt(HEAD)
        totals, sums = 0.0, 0.0
        for keys, values in ((keys_a, values_a), (keys_b, values_b)):
            scores = dot32_t(queries, keys[cut]) * score_scale
            weights = jnp.exp(scores).astype(bf)
            totals = totals + jnp.sum(weights.astype(jnp.float32), axis=1, keepdims=True)
            sums = sums + dot32(weights, values[cut])
        return (sums / totals).astype(bf)

    first = norm_rows(keep[:half], gain[pl.ds(place[0], 1), :])
    out[:half] = attend(first, slice(0, half))
    last = norm_rows(keep[half:], gain[heads - 1 : heads, :])
    out[half:] = attend(last, slice(half, 2 * half))


def final_kernel(place, bits, *refs):
    out = refs[-1]
    for k, block in enumerate(refs[:-1]):
        cut = lanes(place[0] ^ k, block.shape[2])
        sign = (2 * bits[:, cut] - 1).astype(jnp.float32)
        out[:, cut] = (block[0].astype(jnp.float32) + sign * block[1].astype(jnp.float32)).astype(bf)


def stationary_plan(
    tokens, in_bits, qkv_weights, qkv_bits, gain_query, gain_key, out_weights, mix_bits, out_bits
):
    groups = lax.axis_size("blk")
    team = lax.axis_size("uly")
    depth = groups // 2
    z = lax.axis_index("blk") // 2
    x = lax.axis_index("blk") % 2
    u = lax.axis_index("uly")
    own_rows, width = tokens.shape
    slab = qkv_weights.shape[2]
    columns = qkv_weights.shape[3]
    size = own_rows * team
    heads = columns // HEAD
    half = depth * size
    steps = range(depth)
    f32 = jnp.float32
    place = jnp.stack([z, x, u]).astype(jnp.int32)

    def swap_x(value):
        return lax.ppermute(value, "blk", [(i, i ^ 1) for i in range(groups)])

    def swap_z(value, step):
        return lax.ppermute(value, "blk", [(i, i ^ (2 * step)) for i in range(groups)])

    def swap_u(value, bit):
        return lax.ppermute(value, "uly", [(i, i ^ bit) for i in range(team)])

    def after(value, *earlier):
        return lax.optimization_barrier((value,) + earlier)[0]

    weights_shape = shape(2, slab, columns)
    piece_shape = shape(slab, columns)
    value_weights = call(
        functools.partial(copy_kernel, 2),
        weights_shape, ANY, [ANY], [pltpu.SemaphoreType.DMA((2,))],
    )(qkv_weights)
    partner = {2: [swap_x(value_weights)] * 2}

    blocks = call(
        prepare_kernel,
        [shape(2, own_rows, 2 * slab)] * depth, [VMEM] * depth, [SMEM] + [VMEM] * 2,
    )(place, after(tokens, value_weights), in_bits)
    held = jnp.stack([blocks[0]] + [swap_z(blocks[k], k) for k in steps if k])

    sign_bits = jnp.transpose(qkv_bits, (1, 0, 2))
    sign_value = call(
        functools.partial(sign_kernel, team), shape(size, columns), VMEM, [SMEM, VMEM],
    )(place, after(sign_bits, blocks[0]))
    signs = {2: [sign_value] + [swap_z(sign_value, k) for k in steps if k]}

    key_weights, query_a, query_b, sign_pair, mix_own = call(
        functools.partial(rest_kernel, team),
        [weights_shape, piece_shape, piece_shape, shape(2, size, columns), shape(size, columns)],
        [ANY, ANY, ANY, VMEM, VMEM],
        [SMEM, VMEM, VMEM, ANY],
        [pltpu.SemaphoreType.DMA((2, 2))],
    )(place, after(sign_bits, sign_value), mix_bits, qkv_weights)

    held = jnp.stack([held, swap_u(held, 2)])
    rows = jnp.stack([held, swap_u(held, 1)])
    rows = jnp.transpose(rows, (3, 2, 1, 0, 4, 5)).reshape(2, half, 2 * slab)

    partner[1] = [swap_x(after(key_weights, partner[2][0]))] * 2
    query_a = swap_x(after(query_a, partner[1][0]))
    query_b = swap_x(after(query_b, query_a))
    partner[0] = [query_a, query_b]
    out_t = jnp.transpose(out_weights, (0, 2, 1))
    out_partner = swap_x(after(out_t, query_b))

    def project(part, rows, outs):
        return call(
            functools.partial(project_kernel, part, size),
            outs,
            [VMEM] * len(outs),
            [SMEM, VMEM, ANY, ANY, ANY] + [VMEM] * len(signs[part]),
            [
                pltpu.VMEM((2, 2 * slab, columns), bf),
                pltpu.VMEM((half, columns), f32),
                pltpu.SemaphoreType.DMA((2, 2)),
            ],
        )(place, rows, qkv_weights, *partner[part], *signs[part])

    two_step = [
        shape(3 * half, HEAD), shape(2 * half, HEAD, dtype=f32), shape(half, HEAD, dtype=f32)
    ]

    def middle(keep_own, keep_two, taken):
        return call(
            functools.partial(middle_kernel, size),
            [shape(2 * half, HEAD), shape(2 * half, HEAD, dtype=f32)],
            [VMEM] * 2,
            [VMEM] * 3,
        )(keep_own, keep_two, taken)

    pair_two = swap_z(after(sign_pair, *signs[2]), 2)
    send, keep_own, keep_two = project(2, rows, two_step)
    pair_13 = swap_z(after(jnp.stack([sign_pair, pair_two]), send), 1)
    signs[1] = signs[0] = [sign_pair, pair_two, pair_13]
    send, total = middle(keep_own, keep_two, swap_z(send, 1))
    values = (total + swap_z(send, 2).astype(f32)).astype(bf)
    values_partner = swap_x(values)

    send, keep_own, keep_two = project(1, after(rows, total), two_step)
    mix_two = swap_z(after(mix_own, pair_13, total), 2)
    taken = after(swap_z(send, 1), query_a)
    send, total = middle(keep_own, keep_two, taken)
    mix_13 = swap_z(after(jnp.stack([mix_own, mix_two]), send), 1)
    taken = after(swap_z(send, 2), query_b)
    keys = call(
        functools.partial(key_kernel, half), shape(2 * half, HEAD), VMEM, [SMEM] + [VMEM] * 3
    )(place, total, taken, gain_key.reshape(heads, HEAD))
    keys_partner = swap_x(keys)

    own, *sends = project(
        0, after(rows, total), [shape(half + size, HEAD, dtype=f32)] + [shape(half + size, HEAD)] * 3
    )
    done = call(
        functools.partial(attend_kernel, half),
        shape(half + size, HEAD),
        VMEM,
        [SMEM] + [VMEM] * 9,
    )(
        place, own, *[swap_z(sends[k - 1], k) for k in steps if k],
        gain_query.reshape(heads, HEAD), keys, keys_partner, values, values_partner,
    )

    by_head, last_head = [], []
    for k in steps:
        block = swap_z(done, k) if k else done
        main = block[:half].reshape(depth, size, HEAD)
        by_head.append(jnp.concatenate([main[j ^ k] for j in steps], axis=0))
        last_head.append(block[half:])
    attended = jnp.concatenate(by_head + [jnp.concatenate(last_head, axis=0)], axis=1)

    def relative(value, axis):
        parts = [
            lax.dynamic_slice_in_dim(value, (z ^ k) * HEAD, HEAD, axis) for k in steps
        ] + [lax.slice_in_dim(value, depth * HEAD, heads * HEAD, axis=axis)]
        return jnp.concatenate(parts, axis=axis)

    mix = relative(jnp.concatenate([mix_own, mix_13[0], mix_two, mix_13[1]], axis=0), 1)
    attended_flipped = attended * mix
    first = jnp.where(x == 0, out_t, out_partner)
    second = jnp.where(x == 0, out_partner, out_t)
    out_full = relative(jnp.concatenate([first, second], axis=1), 2)
    partial = jnp.stack(
        [dot32_t(attended, out_full[0]), dot32_t(attended_flipped, out_full[1])]
    ).astype(bf)
    partial = partial.reshape(2, depth, team, own_rows, 2 * slab)
    summed = partial[:, :, 0::2].astype(f32) + swap_u(partial[:, :, 1::2], 1).astype(f32)
    summed = (summed[:, :, 0] + swap_u(summed[:, :, 1].astype(bf), 2).astype(f32)).astype(bf)
    final = [summed[:, 0]] + [swap_z(summed[:, k], k) for k in steps if k]
    own_bits = lax.dynamic_slice_in_dim(out_bits, u * own_rows, own_rows, 0)
    return call(
        final_kernel, shape(own_rows, width), VMEM, [SMEM] + [VMEM] * (1 + depth)
    )(place, own_bits, *final)


def body(*arrays):
    heads = arrays[2].shape[3] // HEAD
    depth = lax.axis_size("blk") // 2
    if depth == heads - 1 and depth == 4 and lax.axis_size("uly") == 4:
        return stationary_plan(*arrays)
    return gather_plan(*arrays)


def solution(mesh):
    return jax.shard_map(
        body,
        mesh=mesh,
        in_specs=(
            P(("blk", "uly"), None),
            P(("blk", "uly"), None),
            P(None, None, "blk", "uly"),
            P("blk", None, "uly"),
            P("uly"),
            P("uly"),
            P(None, "uly", "blk"),
            P("blk", "uly"),
            P("blk", None),
        ),
        out_specs=P(("blk", "uly"), None),
        check_vma=False,
    )
```

```python
import functools
import math

import jax
import jax.numpy as jnp
from jax import lax
from jax.experimental import pallas as pl
from jax.experimental.pallas import tpu as pltpu
from jax.sharding import PartitionSpec as P

HEAD = 128


epsilon = 1e-06


def signed(bit_values):
    return (2 * bit_values - 1).astype(jnp.float32)


def normalize(values, gain_vector):
    row_count = values.shape[0]
    by_head = values.astype(jnp.float32).reshape(row_count, -1, HEAD)
    inverse_rms = lax.rsqrt(jnp.mean(by_head * by_head, axis=-1, keepdims=True) + epsilon)
    return (by_head * inverse_rms * gain_vector.reshape(-1, HEAD)).astype(jnp.bfloat16)


def gather_plan(
    tokens, in_bits, qkv_weights, qkv_bits, gain_query, gain_key, out_weights, mix_bits, out_bits
):
    flipped = (tokens.astype(jnp.float32) * signed(in_bits)).astype(jnp.bfloat16)
    group_rows = lax.all_gather(jnp.stack([tokens, flipped]), "uly", axis=1, tiled=True)
    row_total = group_rows.shape[1]
    projections = jnp.einsum(
        "mrd,mkdc->rmkc",
        group_rows,
        lax.all_gather(qkv_weights, "blk", axis=2, tiled=True),
        preferred_element_type=jnp.float32,
    )
    projected = (projections[:, 0] + signed(qkv_bits) * projections[:, 1]).astype(jnp.bfloat16)
    queries = normalize(projected[:, 0], gain_query)
    head_count = queries.shape[1]
    keys_normed = normalize(projected[:, 1], gain_key).reshape(row_total, -1)
    values_block = projected[:, 2]
    score_scale = 1.0 / math.sqrt(HEAD)

    def attend(running, shard_piece):
        numerator, denominator = running
        key_rows = shard_piece[0].reshape(shard_piece[0].shape[0], head_count, HEAD)
        value_rows = shard_piece[1].reshape(shard_piece[1].shape[0], head_count, HEAD)
        scores = (
            jnp.einsum("rhd,nhd->hrn", queries, key_rows, preferred_element_type=jnp.float32)
            * score_scale
        )
        weights = jnp.exp(scores).astype(jnp.bfloat16)
        numerator = numerator + jnp.einsum(
            "hrn,nhd->rhd", weights, value_rows, preferred_element_type=jnp.float32
        )
        denominator = denominator + jnp.sum(weights.astype(jnp.float32), axis=2).T
        return (numerator, denominator)

    start_state = (
        jnp.zeros((row_total, head_count, HEAD), jnp.float32),
        jnp.zeros((row_total, head_count), jnp.float32),
    )
    all_keys, all_values = (
        lax.all_gather(keys_normed, "blk", axis=0, tiled=True),
        lax.all_gather(values_block, "blk", axis=0, tiled=True),
    )
    group_count = lax.axis_size("blk")
    per_block = 1
    while per_block * row_total < 512 and group_count % (per_block * 2) == 0:
        per_block = per_block * 2
    block_rows = per_block * row_total
    block_count = group_count // per_block
    key_blocks = all_keys.reshape(block_count, block_rows, all_keys.shape[1])
    value_blocks = all_values.reshape(block_count, block_rows, all_values.shape[1])

    def scan_step(running, block_pair):
        return (attend(running, block_pair), None)

    (numerator, denominator), unused = lax.scan(scan_step, start_state, (key_blocks, value_blocks))
    attended = (numerator / denominator[:, :, None]).astype(jnp.bfloat16).reshape(row_total, -1)
    attended_flipped = (attended.astype(jnp.float32) * signed(mix_bits)).astype(jnp.bfloat16)
    attended_pair = jnp.stack([attended, attended_flipped])
    out_signs = signed(out_bits)
    partial_out = jnp.einsum(
        "mrc,mcn->rmn",
        attended_pair,
        lax.all_gather(out_weights, "blk", axis=2, tiled=True),
        preferred_element_type=jnp.float32,
    )
    summed = lax.psum_scatter(
        partial_out.astype(jnp.bfloat16), "uly", scatter_dimension=0, tiled=True
    ).astype(jnp.float32)
    own_rows = summed.shape[0]
    own_signs = lax.dynamic_slice_in_dim(out_signs, lax.axis_index("uly") * own_rows, own_rows, 0)
    result_rows = summed[:, 0] + own_signs * summed[:, 1]
    return result_rows.astype(jnp.bfloat16)


def dot32(a, b):
    return lax.dot_general(
        a, b, (((1,), (0,)), ((), ())), preferred_element_type=jnp.float32
    )


def dot32_t(a, b):
    return lax.dot_general(
        a, b, (((1,), (1,)), ((), ())), preferred_element_type=jnp.float32
    )


bf = jnp.bfloat16
VMEM = pl.BlockSpec(memory_space=pltpu.VMEM)
SMEM = pl.BlockSpec(memory_space=pltpu.SMEM)
ANY = pl.BlockSpec(memory_space=pl.ANY)


def call(kernel, outs, out_specs, in_specs, scratch=(), flops=0, moved=0):
    return pl.pallas_call(
        kernel,
        out_shape=outs,
        in_specs=in_specs,
        out_specs=out_specs,
        scratch_shapes=list(scratch),
        compiler_params=pltpu.CompilerParams(vmem_limit_bytes=40 * 1024 * 1024),
        cost_estimate=pl.CostEstimate(flops=flops, bytes_accessed=moved, transcendentals=0),
    )


def shape(*dims, dtype=bf):
    return jax.ShapeDtypeStruct(dims, dtype)


def lanes(index, size):
    return pl.ds(pl.multiple_of(index * size, 128), size)


def copy_kernel(first, count, weights, out, sems):
    copies = [
        pltpu.make_async_copy(weights.at[m, pl.ds(first, count)], out.at[m], sems.at[m])
        for m in (0, 1)
    ]
    for copy in copies:
        copy.start()
    for copy in copies:
        copy.wait()


def sign_pieces(bits, u, team):
    piece = bits.shape[0] // team
    parts = [bits[pl.ds(pl.multiple_of((u ^ r) * piece, 8), piece), :] for r in range(team)]
    return [(2 * part - 1).astype(jnp.float32) for part in parts]


def prepare_kernel(team, place, tokens, in_bits, sign_bits, *blocks):
    z = place[0]
    wide = tokens.shape[1] // len(blocks)
    signs = [part.astype(bf) for part in sign_pieces(sign_bits.at[2], place[2], team)]
    for k, block in enumerate(blocks):
        cut = lanes(z ^ k, wide)
        plain = tokens[:, cut]
        sign = (2 * in_bits[:, cut] - 1).astype(jnp.float32)
        block[0] = plain
        block[1] = (plain.astype(jnp.float32) * sign).astype(bf)
        for r in range(team):
            block[2 + r] = signs[r]


def rest_kernel(team, place, sign_bits, mix_bits, weights, query_a, query_b, signs, mix, sems):
    copies = [
        pltpu.make_async_copy(weights.at[m, 0], out, sems.at[m])
        for m, out in ((0, query_a), (1, query_b))
    ]
    for copy in copies:
        copy.start()
    for part in (0, 1):
        pieces = sign_pieces(sign_bits.at[part], place[2], team)
        signs[part] = jnp.concatenate(pieces, axis=0).astype(bf)
    mix[...] = jnp.concatenate(sign_pieces(mix_bits, place[2], team), axis=0).astype(bf)
    for copy in copies:
        copy.wait()


def stack_kernel(*refs):
    for k, ref in enumerate(refs[:-1]):
        refs[-1][k] = ref[: refs[-1].shape[1]]


def pair_kernel(own, taken, out):
    out[0] = own[...]
    out[1] = taken[...]


def rows_kernel(own, taken, rows):
    depth, kinds, piece = own.shape[1:4]
    for m in range(kinds):
        for j in range(depth):
            parts = [ref[y, j, m].astype(jnp.float32) for y in (0, 1) for ref in (own, taken)]
            at = j * 4 * piece
            rows[m, at : at + 4 * piece] = jnp.concatenate(parts, axis=0).astype(bf)


def sum_kernel(total, taken, out):
    out[...] = (total[...] + taken[...].astype(jnp.float32)).astype(bf)


def project_kernel(part, size, place, rows, weights, partner_0, partner_1, *refs):
    held, total, sems = refs[-3:]
    z, x = place[0], place[1]
    slab = weights.shape[2]
    partner = (partner_0, partner_1)
    if part:
        partner = (partner_0.at[0, part - 1], partner_0.at[1, part - 1])
    own = pl.ds(pl.multiple_of(x * slab, 64), slab)
    other = pl.ds(pl.multiple_of((1 - x) * slab, 64), slab)
    copies = []
    for m in (0, 1):
        copies.append(
            pltpu.make_async_copy(weights.at[m, part], held.at[m, own], sems.at[m, 0])
        )
        copies.append(pltpu.make_async_copy(partner[m], held.at[m, other], sems.at[m, 1]))
    for copy in copies:
        copy.start()
    for copy in copies:
        copy.wait()
    depth = rows.shape[1] // size
    outs = refs[depth:-3]

    def sign(j):
        if part < 2:
            return refs[j][part].astype(jnp.float32)
        pieces = [refs[j][r] for r in range(2, refs[j].shape[0])]
        return jnp.concatenate([piece.astype(jnp.float32) for piece in pieces], axis=0)

    total[...] = dot32(rows[1], held[1])
    plain = dot32(rows[0], held[0])
    for j in range(depth):
        cut = slice(j * size, (j + 1) * size)
        total[cut] = plain[cut] + sign(j) * total[cut]

    def block(j, head):
        return total[j * size : (j + 1) * size, lanes(head, HEAD)]

    def main(target, start, k):
        for j in range(depth):
            at = start + (j ^ k) * size
            target[at : at + size] = block(j, z ^ k).astype(target.dtype)

    def rest(target, start, j):
        target[start : start + size] = block(j, depth).astype(target.dtype)

    half = depth * size
    if part:
        send, keep_own, keep_two = outs
        main(send, 0, 1)
        main(send, half, 3)
        for j in range(depth):
            rest(send, 2 * half + (j ^ 1) * size, j)
            rest(keep_own, half + j * size, j)
        main(keep_own, 0, 0)
        main(keep_two, 0, 2)
    else:
        for k in range(depth):
            main(outs[k], 0, k)
            rest(outs[k], half, k)


def middle_kernel(size, keep_own, keep_two, taken, send, total):
    half = keep_two.shape[0]
    total[:half] = keep_own[:half] + taken[:half].astype(jnp.float32)
    send[:half] = (keep_two[...] + taken[half : 2 * half].astype(jnp.float32)).astype(bf)
    for j in range(half // size):
        cut = slice(half + j * size, half + (j + 1) * size)
        got = taken[half + cut.start : half + cut.stop].astype(jnp.float32)
        value = keep_own[cut] + got
        total[cut] = value
        at = half + (j ^ 2) * size
        send[at : at + size] = value.astype(bf)


def norm_rows(values, gain_row):
    wide = values.astype(jnp.float32)
    inverse_rms = lax.rsqrt(jnp.mean(wide * wide, axis=-1, keepdims=True) + epsilon)
    return (wide * inverse_rms * gain_row).astype(bf)


def key_kernel(half, place, total, taken, gain, keys):
    keep = (total[...] + taken[...].astype(jnp.float32)).astype(bf)
    heads = gain.shape[0]
    keys[:half] = norm_rows(keep[:half], gain[pl.ds(place[0], 1), :])
    keys[half:] = norm_rows(keep[half:], gain[heads - 1 : heads, :])


def attend_kernel(
    half, place, total, taken_1, taken_2, taken_3, gain, keys_a, keys_b, values_a, values_b, out
):
    keep = total[...]
    for taken in (taken_1, taken_2, taken_3):
        keep = keep + taken[...].astype(jnp.float32)
    keep = keep.astype(bf)
    heads = gain.shape[0]

    def attend(queries, cut):
        score_scale = 1.0 / math.sqrt(HEAD)
        totals, sums = 0.0, 0.0
        for keys, values in ((keys_a, values_a), (keys_b, values_b)):
            scores = dot32_t(queries, keys[cut]) * score_scale
            weights = jnp.exp(scores).astype(bf)
            totals = totals + jnp.sum(weights.astype(jnp.float32), axis=1, keepdims=True)
            sums = sums + dot32(weights, values[cut])
        return (sums / totals).astype(bf)

    first = norm_rows(keep[:half], gain[pl.ds(place[0], 1), :])
    out[:half] = attend(first, slice(0, half))
    last = norm_rows(keep[half:], gain[heads - 1 : heads, :])
    out[half:] = attend(last, slice(half, 2 * half))


def final_kernel(place, bits, *refs):
    out = refs[-1]
    for k, block in enumerate(refs[:-1]):
        cut = lanes(place[0] ^ k, block.shape[2])
        sign = (2 * bits[:, cut] - 1).astype(jnp.float32)
        out[:, cut] = (block[0].astype(jnp.float32) + sign * block[1].astype(jnp.float32)).astype(bf)


def stationary_plan(
    tokens, in_bits, qkv_weights, qkv_bits, gain_query, gain_key, out_weights, mix_bits, out_bits
):
    groups = lax.axis_size("blk")
    team = lax.axis_size("uly")
    depth = groups // 2
    z = lax.axis_index("blk") // 2
    x = lax.axis_index("blk") % 2
    u = lax.axis_index("uly")
    own_rows, width = tokens.shape
    slab = qkv_weights.shape[2]
    columns = qkv_weights.shape[3]
    size = own_rows * team
    heads = columns // HEAD
    half = depth * size
    steps = range(depth)
    f32 = jnp.float32
    place = jnp.stack([z, x, u]).astype(jnp.int32)

    def swap_x(value):
        return lax.ppermute(value, "blk", [(i, i ^ 1) for i in range(groups)])

    def swap_z(value, step):
        return lax.ppermute(value, "blk", [(i, i ^ (2 * step)) for i in range(groups)])

    def swap_u(value, bit):
        return lax.ppermute(value, "uly", [(i, i ^ bit) for i in range(team)])

    def after(value, *earlier):
        return lax.optimization_barrier((value,) + earlier)[0]

    early = call(
        functools.partial(copy_kernel, 1, 2),
        shape(2, 2, slab, columns), ANY, [ANY], [pltpu.SemaphoreType.DMA((2,))],
    )(qkv_weights)
    partner_early = swap_x(early)

    sign_bits = jnp.transpose(qkv_bits, (1, 0, 2))
    blocks = call(
        functools.partial(prepare_kernel, team),
        [shape(2 + team, own_rows, 2 * slab)] * depth, [VMEM] * depth, [SMEM] + [VMEM] * 3,
    )(place, after(tokens, early), in_bits, sign_bits)
    got = [blocks[0]] + [swap_z(blocks[k], k) for k in steps if k]
    query_a, query_b, sign_pair, mix_own = call(
        functools.partial(rest_kernel, team),
        [shape(slab, columns), shape(slab, columns), shape(2, size, columns), shape(size, columns)],
        [ANY, ANY, VMEM, VMEM],
        [SMEM, VMEM, VMEM, ANY],
        [pltpu.SemaphoreType.DMA((2,))],
    )(place, after(sign_bits, blocks[0]), mix_bits, qkv_weights)
    sent_pair = after(sign_pair, *got[1:])
    pairs = [sign_pair] + [swap_z(sent_pair, k) for k in steps if k]
    signs = {2: got, 1: pairs, 0: pairs}

    held_shape = (depth, 2, own_rows, 2 * slab)
    held = call(stack_kernel, shape(*held_shape), VMEM, [VMEM] * depth)(*got)
    held = call(pair_kernel, shape(2, *held_shape), VMEM, [VMEM] * 2)(held, swap_u(held, 2))
    rows = call(rows_kernel, shape(2, half, 2 * slab), VMEM, [VMEM] * 2)(held, swap_u(held, 1))

    query_a = swap_x(after(query_a, partner_early, pairs[1]))
    query_b = swap_x(after(query_b, query_a))
    partner = {2: [partner_early] * 2, 1: [partner_early] * 2, 0: [query_a, query_b]}

    def project(part, rows, outs):
        return call(
            functools.partial(project_kernel, part, size),
            outs,
            [VMEM] * len(outs),
            [SMEM, VMEM, ANY, ANY, ANY] + [VMEM] * len(signs[part]),
            [
                pltpu.VMEM((2, 2 * slab, columns), bf),
                pltpu.VMEM((half, columns), f32),
                pltpu.SemaphoreType.DMA((2, 2)),
            ],
        )(place, rows, qkv_weights, *partner[part], *signs[part])

    two_step = [
        shape(3 * half, HEAD), shape(2 * half, HEAD, dtype=f32), shape(half, HEAD, dtype=f32)
    ]

    def middle(keep_own, keep_two, taken):
        return call(
            functools.partial(middle_kernel, size),
            [shape(2 * half, HEAD), shape(2 * half, HEAD, dtype=f32)],
            [VMEM] * 2,
            [VMEM] * 3,
        )(keep_own, keep_two, taken)

    value_send, keep_own, keep_two = project(2, rows, two_step)
    key_send, key_own, key_two = project(1, after(rows, value_send), two_step)
    taken = after(swap_z(value_send, 1), key_send, query_a)
    send, value_total = middle(keep_own, keep_two, taken)
    value_last = swap_z(send, 2)
    taken = after(swap_z(key_send, 1), value_total, query_b)
    send, key_total = middle(key_own, key_two, taken)
    key_last = swap_z(send, 2)
    own, *sends = project(
        0,
        after(rows, key_total),
        [shape(half + size, HEAD, dtype=f32)] + [shape(half + size, HEAD)] * 3,
    )
    taken_q = [swap_z(sends[k - 1], k) for k in steps if k]
    values = call(sum_kernel, shape(2 * half, HEAD), VMEM, [VMEM] * 2)(
        value_total, after(value_last, own)
    )
    values_partner = swap_x(values)
    keys = call(
        functools.partial(key_kernel, half), shape(2 * half, HEAD), VMEM, [SMEM] + [VMEM] * 3
    )(place, key_total, after(key_last, values, taken_q[0]), gain_key.reshape(heads, HEAD))
    keys_partner = swap_x(keys)
    mix_two = swap_z(after(mix_own, taken_q[1]), 2)
    mix_13 = swap_z(
        call(pair_kernel, shape(2, size, columns), VMEM, [VMEM] * 2)(mix_own, mix_two), 1
    )
    out_t = jnp.transpose(out_weights, (0, 2, 1))
    out_partner = swap_x(after(out_t, keys, taken_q[1]))

    done = call(
        functools.partial(attend_kernel, half),
        shape(half + size, HEAD),
        VMEM,
        [SMEM] + [VMEM] * 9,
    )(
        place, own, *taken_q,
        gain_query.reshape(heads, HEAD), keys, keys_partner, values, values_partner,
    )

    by_head, last_head = [], []
    for k in steps:
        block = swap_z(done, k) if k else done
        main = block[:half].reshape(depth, size, HEAD)
        by_head.append(jnp.concatenate([main[j ^ k] for j in steps], axis=0))
        last_head.append(block[half:])
    attended = jnp.concatenate(by_head + [jnp.concatenate(last_head, axis=0)], axis=1)

    def relative(value, axis):
        parts = [
            lax.dynamic_slice_in_dim(value, (z ^ k) * HEAD, HEAD, axis) for k in steps
        ] + [lax.slice_in_dim(value, depth * HEAD, heads * HEAD, axis=axis)]
        return jnp.concatenate(parts, axis=axis)

    mix = relative(jnp.concatenate([mix_own, mix_13[0], mix_two, mix_13[1]], axis=0), 1)
    attended_flipped = attended * mix
    first = jnp.where(x == 0, out_t, out_partner)
    second = jnp.where(x == 0, out_partner, out_t)
    out_full = relative(jnp.concatenate([first, second], axis=1), 2)
    partial = jnp.stack(
        [dot32_t(attended, out_full[0]), dot32_t(attended_flipped, out_full[1])]
    ).astype(bf)
    partial = partial.reshape(2, depth, team, own_rows, 2 * slab)
    summed = partial[:, :, 0::2].astype(f32) + swap_u(partial[:, :, 1::2], 1).astype(f32)
    summed = (summed[:, :, 0] + swap_u(summed[:, :, 1].astype(bf), 2).astype(f32)).astype(bf)
    final = [summed[:, 0]] + [swap_z(summed[:, k], k) for k in steps if k]
    own_bits = lax.dynamic_slice_in_dim(out_bits, u * own_rows, own_rows, 0)
    return call(
        final_kernel, shape(own_rows, width), VMEM, [SMEM] + [VMEM] * (1 + depth)
    )(place, own_bits, *final)


def body(*arrays):
    heads = arrays[2].shape[3] // HEAD
    depth = lax.axis_size("blk") // 2
    if depth == heads - 1 and depth == 4 and lax.axis_size("uly") == 4:
        return stationary_plan(*arrays)
    return gather_plan(*arrays)


def solution(mesh):
    return jax.shard_map(
        body,
        mesh=mesh,
        in_specs=(
            P(("blk", "uly"), None),
            P(("blk", "uly"), None),
            P(None, None, "blk", "uly"),
            P("blk", None, "uly"),
            P("uly"),
            P("uly"),
            P(None, "uly", "blk"),
            P("blk", "uly"),
            P("blk", None),
        ),
        out_specs=P(("blk", "uly"), None),
        check_vma=False,
    )
```

```python
import functools
import math

import jax
import jax.numpy as jnp
from jax import lax
from jax.experimental import pallas as pl
from jax.experimental.pallas import tpu as pltpu
from jax.sharding import PartitionSpec as P

HEAD = 128


epsilon = 1e-06


def signed(bit_values):
    return (2 * bit_values - 1).astype(jnp.float32)


def normalize(values, gain_vector):
    row_count = values.shape[0]
    by_head = values.astype(jnp.float32).reshape(row_count, -1, HEAD)
    inverse_rms = lax.rsqrt(jnp.mean(by_head * by_head, axis=-1, keepdims=True) + epsilon)
    return (by_head * inverse_rms * gain_vector.reshape(-1, HEAD)).astype(jnp.bfloat16)


def gather_plan(
    tokens, in_bits, qkv_weights, qkv_bits, gain_query, gain_key, out_weights, mix_bits, out_bits
):
    flipped = (tokens.astype(jnp.float32) * signed(in_bits)).astype(jnp.bfloat16)
    group_rows = lax.all_gather(jnp.stack([tokens, flipped]), "uly", axis=1, tiled=True)
    row_total = group_rows.shape[1]
    projections = jnp.einsum(
        "mrd,mkdc->rmkc",
        group_rows,
        lax.all_gather(qkv_weights, "blk", axis=2, tiled=True),
        preferred_element_type=jnp.float32,
    )
    projected = (projections[:, 0] + signed(qkv_bits) * projections[:, 1]).astype(jnp.bfloat16)
    queries = normalize(projected[:, 0], gain_query)
    head_count = queries.shape[1]
    keys_normed = normalize(projected[:, 1], gain_key).reshape(row_total, -1)
    values_block = projected[:, 2]
    score_scale = 1.0 / math.sqrt(HEAD)

    def attend(running, shard_piece):
        numerator, denominator = running
        key_rows = shard_piece[0].reshape(shard_piece[0].shape[0], head_count, HEAD)
        value_rows = shard_piece[1].reshape(shard_piece[1].shape[0], head_count, HEAD)
        scores = (
            jnp.einsum("rhd,nhd->hrn", queries, key_rows, preferred_element_type=jnp.float32)
            * score_scale
        )
        weights = jnp.exp(scores).astype(jnp.bfloat16)
        numerator = numerator + jnp.einsum(
            "hrn,nhd->rhd", weights, value_rows, preferred_element_type=jnp.float32
        )
        denominator = denominator + jnp.sum(weights.astype(jnp.float32), axis=2).T
        return (numerator, denominator)

    start_state = (
        jnp.zeros((row_total, head_count, HEAD), jnp.float32),
        jnp.zeros((row_total, head_count), jnp.float32),
    )
    all_keys, all_values = (
        lax.all_gather(keys_normed, "blk", axis=0, tiled=True),
        lax.all_gather(values_block, "blk", axis=0, tiled=True),
    )
    group_count = lax.axis_size("blk")
    per_block = 1
    while per_block * row_total < 512 and group_count % (per_block * 2) == 0:
        per_block = per_block * 2
    block_rows = per_block * row_total
    block_count = group_count // per_block
    key_blocks = all_keys.reshape(block_count, block_rows, all_keys.shape[1])
    value_blocks = all_values.reshape(block_count, block_rows, all_values.shape[1])

    def scan_step(running, block_pair):
        return (attend(running, block_pair), None)

    (numerator, denominator), unused = lax.scan(scan_step, start_state, (key_blocks, value_blocks))
    attended = (numerator / denominator[:, :, None]).astype(jnp.bfloat16).reshape(row_total, -1)
    attended_flipped = (attended.astype(jnp.float32) * signed(mix_bits)).astype(jnp.bfloat16)
    attended_pair = jnp.stack([attended, attended_flipped])
    out_signs = signed(out_bits)
    partial_out = jnp.einsum(
        "mrc,mcn->rmn",
        attended_pair,
        lax.all_gather(out_weights, "blk", axis=2, tiled=True),
        preferred_element_type=jnp.float32,
    )
    summed = lax.psum_scatter(
        partial_out.astype(jnp.bfloat16), "uly", scatter_dimension=0, tiled=True
    ).astype(jnp.float32)
    own_rows = summed.shape[0]
    own_signs = lax.dynamic_slice_in_dim(out_signs, lax.axis_index("uly") * own_rows, own_rows, 0)
    result_rows = summed[:, 0] + own_signs * summed[:, 1]
    return result_rows.astype(jnp.bfloat16)


def dot32(a, b):
    return lax.dot_general(
        a, b, (((1,), (0,)), ((), ())), preferred_element_type=jnp.float32
    )


def dot32_t(a, b):
    return lax.dot_general(
        a, b, (((1,), (1,)), ((), ())), preferred_element_type=jnp.float32
    )


bf = jnp.bfloat16
VMEM = pl.BlockSpec(memory_space=pltpu.VMEM)
SMEM = pl.BlockSpec(memory_space=pltpu.SMEM)
ANY = pl.BlockSpec(memory_space=pl.ANY)


def call(kernel, outs, out_specs, in_specs, scratch=(), flops=0, moved=0):
    return pl.pallas_call(
        kernel,
        out_shape=outs,
        in_specs=in_specs,
        out_specs=out_specs,
        scratch_shapes=list(scratch),
        compiler_params=pltpu.CompilerParams(vmem_limit_bytes=40 * 1024 * 1024),
        cost_estimate=pl.CostEstimate(flops=flops, bytes_accessed=moved, transcendentals=0),
    )


def shape(*dims, dtype=bf):
    return jax.ShapeDtypeStruct(dims, dtype)


def lanes(index, size):
    return pl.ds(pl.multiple_of(index * size, 128), size)


def copy_kernel(first, count, weights, out, sems):
    copies = [
        pltpu.make_async_copy(weights.at[m, pl.ds(first, count)], out.at[m], sems.at[m])
        for m in (0, 1)
    ]
    for copy in copies:
        copy.start()
    for copy in copies:
        copy.wait()


def sign_pieces(bits, u, team):
    piece = bits.shape[0] // team
    parts = [bits[pl.ds(pl.multiple_of((u ^ r) * piece, 8), piece), :] for r in range(team)]
    return [(2 * part - 1).astype(jnp.float32) for part in parts]


def sign_kernel(team, place, sign_bits, signs):
    for part in range(signs.shape[0]):
        pieces = sign_pieces(sign_bits.at[part], place[2], team)
        signs[part] = jnp.concatenate(pieces, axis=0).astype(bf)


def prepare_kernel(
    team, place, tokens, in_bits, out_bits, mix_bits, weights, query_a, query_b, *refs
):
    blocks, sems = refs[:-1], refs[-1]
    copies = [
        pltpu.make_async_copy(weights.at[m, 0], out, sems.at[m])
        for m, out in ((0, query_a), (1, query_b))
    ]
    for copy in copies:
        copy.start()
    z, u = place[0], place[2]
    own_rows = tokens.shape[0]
    wide = tokens.shape[1] // len(blocks)
    mix = [part.astype(bf) for part in sign_pieces(mix_bits, u, team)]
    for k, block in enumerate(blocks):
        cut = lanes(z ^ k, wide)
        plain = tokens[:, cut]
        sign = (2 * in_bits[:, cut] - 1).astype(jnp.float32)
        block[0] = plain
        block[1] = (plain.astype(jnp.float32) * sign).astype(bf)
        for i, r in enumerate((0, 2)):
            bits = out_bits[pl.ds(pl.multiple_of((u ^ r) * own_rows, 8), own_rows), cut]
            block[2 + i] = (2 * bits - 1).astype(jnp.float32).astype(bf)
        for r in range(team):
            block[4 + r] = mix[r]
    for copy in copies:
        copy.wait()


def stack_kernel(*refs):
    for k, ref in enumerate(refs[:-1]):
        refs[-1][k] = ref[: refs[-1].shape[1]]


def pair_kernel(own, taken, out):
    out[0] = own[...]
    out[1] = taken[...]


def rows_kernel(own, taken, rows):
    depth, kinds, piece = own.shape[1:4]
    for m in range(kinds):
        for j in range(depth):
            parts = [ref[y, j, m].astype(jnp.float32) for y in (0, 1) for ref in (own, taken)]
            at = j * 4 * piece
            rows[m, at : at + 4 * piece] = jnp.concatenate(parts, axis=0).astype(bf)


def sum_kernel(total, taken, out):
    out[...] = (total[...] + taken[...].astype(jnp.float32)).astype(bf)


def project_kernel(
    part, size, place, rows, weights, partner_0, partner_1, all_signs,
    send, keep_own, keep_two, held, total, signs, sems, sign_sems,
):
    z, x = place[0], place[1]
    slab = weights.shape[2]
    partner = (partner_0, partner_1)
    if part:
        partner = (partner_0.at[0, part - 1], partner_0.at[1, part - 1])
    own = pl.ds(pl.multiple_of(x * slab, 64), slab)
    other = pl.ds(pl.multiple_of((1 - x) * slab, 64), slab)
    depth = rows.shape[1] // size
    copies = []
    for m in (0, 1):
        copies.append(
            pltpu.make_async_copy(weights.at[m, part], held.at[m, own], sems.at[m, 0])
        )
        copies.append(pltpu.make_async_copy(partner[m], held.at[m, other], sems.at[m, 1]))
    for j in range(depth):
        copies.append(
            pltpu.make_async_copy(all_signs.at[z ^ j, part], signs.at[j], sign_sems.at[j])
        )
    for copy in copies:
        copy.start()
    for copy in copies:
        copy.wait()
    total[...] = dot32(rows[1], held[1])
    plain = dot32(rows[0], held[0])
    for j in range(depth):
        cut = slice(j * size, (j + 1) * size)
        total[cut] = plain[cut] + signs[j].astype(jnp.float32) * total[cut]

    def block(j, head):
        return total[j * size : (j + 1) * size, lanes(head, HEAD)]

    def main(target, start, k):
        for j in range(depth):
            at = start + (j ^ k) * size
            target[at : at + size] = block(j, z ^ k).astype(target.dtype)

    def rest(target, start, j):
        target[start : start + size] = block(j, depth).astype(target.dtype)

    half = depth * size
    main(keep_own, 0, 0)
    main(keep_two, 0, 2)
    main(send, 0, 1)
    if part:
        main(send, half, 3)
        for j in range(depth):
            rest(send, 2 * half + (j ^ 1) * size, j)
            rest(keep_own, half + j * size, j)
    else:
        rest(send, half, 1)
        main(send, half + size, 3)
        rest(send, 2 * half + size, 3)
        rest(keep_own, half, 0)
        rest(keep_two, half, 2)


def middle_kernel(size, keep_own, keep_two, taken, send, total):
    half = keep_two.shape[0]
    if keep_own.shape[0] == half:
        total[...] = keep_own[...] + taken[:half].astype(jnp.float32)
        send[...] = (keep_two[...] + taken[half:].astype(jnp.float32)).astype(bf)
        return
    total[:half] = keep_own[:half] + taken[:half].astype(jnp.float32)
    send[:half] = (keep_two[...] + taken[half : 2 * half].astype(jnp.float32)).astype(bf)
    for j in range(half // size):
        cut = slice(half + j * size, half + (j + 1) * size)
        got = taken[half + cut.start : half + cut.stop].astype(jnp.float32)
        value = keep_own[cut] + got
        total[cut] = value
        at = half + (j ^ 2) * size
        send[at : at + size] = value.astype(bf)


def norm_rows(values, gain_row):
    wide = values.astype(jnp.float32)
    inverse_rms = lax.rsqrt(jnp.mean(wide * wide, axis=-1, keepdims=True) + epsilon)
    return (wide * inverse_rms * gain_row).astype(bf)


def key_kernel(half, place, total, taken, gain, keys):
    keep = (total[...] + taken[...].astype(jnp.float32)).astype(bf)
    heads = gain.shape[0]
    keys[:half] = norm_rows(keep[:half], gain[pl.ds(place[0], 1), :])
    keys[half:] = norm_rows(keep[half:], gain[heads - 1 : heads, :])


def attend_kernel(
    half, place, total, taken, gain, keys_a, keys_b, values_a, values_b, out
):
    keep = (total[...] + taken[...].astype(jnp.float32)).astype(bf)
    heads = gain.shape[0]

    def attend(queries, cut):
        score_scale = 1.0 / math.sqrt(HEAD)
        totals, sums = 0.0, 0.0
        for keys, values in ((keys_a, values_a), (keys_b, values_b)):
            scores = dot32_t(queries, keys[cut]) * score_scale
            weights = jnp.exp(scores).astype(bf)
            totals = totals + jnp.sum(weights.astype(jnp.float32), axis=1, keepdims=True)
            sums = sums + dot32(weights, values[cut])
        return (sums / totals).astype(bf)

    first = norm_rows(keep[:half], gain[pl.ds(place[0], 1), :])
    out[:half] = attend(first, slice(0, half))
    last = norm_rows(keep[half:], gain[heads - 1 : heads, :])
    out[half:] = attend(last, slice(half, 2 * half))


def final_kernel(place, *refs):
    out = refs[-1]
    for k, block in enumerate(refs[:-1]):
        out[:, lanes(place[0] ^ k, block.shape[1])] = block[...]


def stationary_plan(
    tokens, in_bits, qkv_weights, qkv_bits, gain_query, gain_key, out_weights, mix_bits, out_bits
):
    groups = lax.axis_size("blk")
    team = lax.axis_size("uly")
    depth = groups // 2
    z = lax.axis_index("blk") // 2
    x = lax.axis_index("blk") % 2
    u = lax.axis_index("uly")
    own_rows, width = tokens.shape
    slab = qkv_weights.shape[2]
    columns = qkv_weights.shape[3]
    size = own_rows * team
    heads = columns // HEAD
    half = depth * size
    steps = range(depth)
    f32 = jnp.float32
    place = jnp.stack([z, x, u]).astype(jnp.int32)

    def swap_x(value):
        return lax.ppermute(value, "blk", [(i, i ^ 1) for i in range(groups)])

    def swap_z(value, step):
        return lax.ppermute(value, "blk", [(i, i ^ (2 * step)) for i in range(groups)])

    def swap_u(value, bit):
        return lax.ppermute(value, "uly", [(i, i ^ bit) for i in range(team)])

    def after(value, *earlier):
        return lax.optimization_barrier((value,) + earlier)[0]

    early = call(
        functools.partial(copy_kernel, 1, 2),
        shape(2, 2, slab, columns), ANY, [ANY], [pltpu.SemaphoreType.DMA((2,))],
    )(qkv_weights)
    partner_early = swap_x(early)

    sign_bits = jnp.transpose(qkv_bits, (1, 0, 2))
    sign_own = call(
        functools.partial(sign_kernel, team), shape(3, size, columns), VMEM, [SMEM, VMEM]
    )(place, sign_bits)
    all_signs = lax.all_gather(
        sign_own, "blk", axis=0, axis_index_groups=[[2 * i + j for i in steps] for j in (0, 1)]
    )

    query_a, query_b, *blocks = call(
        functools.partial(prepare_kernel, team),
        [shape(slab, columns)] * 2 + [shape(4 + team, own_rows, 2 * slab)] * depth,
        [ANY] * 2 + [VMEM] * depth,
        [SMEM] + [VMEM] * 4 + [ANY],
        [pltpu.SemaphoreType.DMA((2,))],
    )(place, after(tokens, early, sign_own), in_bits, out_bits, mix_bits, qkv_weights)
    got = [blocks[0]] + [swap_z(blocks[k], k) for k in steps if k]
    held_shape = (depth, 2, own_rows, 2 * slab)
    held = call(stack_kernel, shape(*held_shape), VMEM, [VMEM] * depth)(*got)
    held = call(pair_kernel, shape(2, *held_shape), VMEM, [VMEM] * 2)(held, swap_u(held, 2))
    rows = call(rows_kernel, shape(2, half, 2 * slab), VMEM, [VMEM] * 2)(held, swap_u(held, 1))

    query_a = swap_x(after(query_a, partner_early, rows))
    query_b = swap_x(after(query_b, query_a))
    partner = {2: [partner_early] * 2, 1: [partner_early] * 2, 0: [query_a, query_b]}

    def project(part, rows):
        counts = (3 * half, 2 * half, half) if part else (2 * (half + size),) + (half + size,) * 2
        return call(
            functools.partial(project_kernel, part, size),
            [shape(counts[0], HEAD)] + [shape(count, HEAD, dtype=f32) for count in counts[1:]],
            [VMEM] * 3,
            [SMEM, VMEM] + [ANY] * 4,
            [
                pltpu.VMEM((2, 2 * slab, columns), bf),
                pltpu.VMEM((half, columns), f32),
                pltpu.VMEM((depth, size, columns), bf),
                pltpu.SemaphoreType.DMA((2, 2)),
                pltpu.SemaphoreType.DMA((depth,)),
            ],
        )(place, rows, qkv_weights, *partner[part], all_signs)

    def middle(keep_own, keep_two, taken):
        count = keep_own.shape[0]
        return call(
            functools.partial(middle_kernel, size),
            [shape(count, HEAD), shape(count, HEAD, dtype=f32)],
            [VMEM] * 2,
            [VMEM] * 3,
        )(keep_own, keep_two, taken)

    value_send, keep_own, keep_two = project(2, rows)
    key_send, key_own, key_two = project(1, after(rows, value_send))
    taken = after(swap_z(value_send, 1), key_send, query_a)
    send, value_total = middle(keep_own, keep_two, taken)
    value_last = swap_z(send, 2)
    taken = after(swap_z(key_send, 1), value_last, query_b)
    send, key_total = middle(key_own, key_two, taken)
    key_last = swap_z(send, 2)
    query_send, query_own, query_two = project(0, after(rows, key_total))
    taken = swap_z(query_send, 1)
    values = call(sum_kernel, shape(2 * half, HEAD), VMEM, [VMEM] * 2)(
        value_total, after(value_last, query_send)
    )
    values_partner = swap_x(values)
    keys = call(
        functools.partial(key_kernel, half), shape(2 * half, HEAD), VMEM, [SMEM] + [VMEM] * 3
    )(place, key_total, after(key_last, values), gain_key.reshape(heads, HEAD))
    keys_partner = swap_x(keys)
    send, query_total = middle(query_own, query_two, taken)
    out_t = jnp.transpose(out_weights, (0, 2, 1))
    out_partner = swap_x(after(out_t, keys, query_total))

    done = call(
        functools.partial(attend_kernel, half),
        shape(half + size, HEAD),
        VMEM,
        [SMEM] + [VMEM] * 7,
    )(
        place, query_total, swap_z(send, 2), gain_query.reshape(heads, HEAD),
        keys, keys_partner, values, values_partner,
    )

    by_head, last_head = [], []
    for k in steps:
        block = swap_z(done, k) if k else done
        main = block[:half].reshape(depth, size, HEAD)
        by_head.append(jnp.concatenate([main[j ^ k] for j in steps], axis=0))
        last_head.append(block[half:])
    attended = jnp.concatenate(by_head + [jnp.concatenate(last_head, axis=0)], axis=1)

    def relative(value, axis):
        parts = [
            lax.dynamic_slice_in_dim(value, (z ^ k) * HEAD, HEAD, axis) for k in steps
        ] + [lax.slice_in_dim(value, depth * HEAD, heads * HEAD, axis=axis)]
        return jnp.concatenate(parts, axis=axis)

    mix = relative(jnp.concatenate([g[4:].reshape(size, columns) for g in got], axis=0), 1)
    attended_flipped = attended * mix
    first = jnp.where(x == 0, out_t, out_partner)
    second = jnp.where(x == 0, out_partner, out_t)
    out_full = relative(jnp.concatenate([first, second], axis=1), 2)
    partial = jnp.stack(
        [dot32_t(attended, out_full[0]), dot32_t(attended_flipped, out_full[1])]
    ).astype(bf)
    partial = partial.reshape(2, depth, team, own_rows, 2 * slab)
    summed = partial[:, :, 0::2].astype(f32) + swap_u(partial[:, :, 1::2], 1).astype(f32)
    out_signs = jnp.stack([g[2:4] for g in got]).astype(f32)
    summed = summed[0] + out_signs * summed[1]
    summed = (summed[:, 0] + swap_u(summed[:, 1].astype(bf), 2).astype(f32)).astype(bf)
    final = [summed[0]] + [swap_z(summed[k], k) for k in steps if k]
    return call(
        final_kernel, shape(own_rows, width), VMEM, [SMEM] + [VMEM] * depth
    )(place, *final)


def body(*arrays):
    heads = arrays[2].shape[3] // HEAD
    depth = lax.axis_size("blk") // 2
    if depth == heads - 1 and depth == 4 and lax.axis_size("uly") == 4:
        return stationary_plan(*arrays)
    return gather_plan(*arrays)


def solution(mesh):
    return jax.shard_map(
        body,
        mesh=mesh,
        in_specs=(
            P(("blk", "uly"), None),
            P(("blk", "uly"), None),
            P(None, None, "blk", "uly"),
            P("blk", None, "uly"),
            P("uly"),
            P("uly"),
            P(None, "uly", "blk"),
            P("blk", "uly"),
            P("blk", None),
        ),
        out_specs=P(("blk", "uly"), None),
        check_vma=False,
    )
```

```python
import functools
import math

import jax
import jax.numpy as jnp
from jax import lax
from jax.experimental import pallas as pl
from jax.experimental.pallas import tpu as pltpu
from jax.sharding import PartitionSpec as P

HEAD = 128


epsilon = 1e-06


def signed(bit_values):
    return (2 * bit_values - 1).astype(jnp.float32)


def normalize(values, gain_vector):
    row_count = values.shape[0]
    by_head = values.astype(jnp.float32).reshape(row_count, -1, HEAD)
    inverse_rms = lax.rsqrt(jnp.mean(by_head * by_head, axis=-1, keepdims=True) + epsilon)
    return (by_head * inverse_rms * gain_vector.reshape(-1, HEAD)).astype(jnp.bfloat16)


def gather_plan(
    tokens, in_bits, qkv_weights, qkv_bits, gain_query, gain_key, out_weights, mix_bits, out_bits
):
    flipped = (tokens.astype(jnp.float32) * signed(in_bits)).astype(jnp.bfloat16)
    group_rows = lax.all_gather(jnp.stack([tokens, flipped]), "uly", axis=1, tiled=True)
    row_total = group_rows.shape[1]
    projections = jnp.einsum(
        "mrd,mkdc->rmkc",
        group_rows,
        lax.all_gather(qkv_weights, "blk", axis=2, tiled=True),
        preferred_element_type=jnp.float32,
    )
    projected = (projections[:, 0] + signed(qkv_bits) * projections[:, 1]).astype(jnp.bfloat16)
    queries = normalize(projected[:, 0], gain_query)
    head_count = queries.shape[1]
    keys_normed = normalize(projected[:, 1], gain_key).reshape(row_total, -1)
    values_block = projected[:, 2]
    score_scale = 1.0 / math.sqrt(HEAD)

    def attend(running, shard_piece):
        numerator, denominator = running
        key_rows = shard_piece[0].reshape(shard_piece[0].shape[0], head_count, HEAD)
        value_rows = shard_piece[1].reshape(shard_piece[1].shape[0], head_count, HEAD)
        scores = (
            jnp.einsum("rhd,nhd->hrn", queries, key_rows, preferred_element_type=jnp.float32)
            * score_scale
        )
        weights = jnp.exp(scores).astype(jnp.bfloat16)
        numerator = numerator + jnp.einsum(
            "hrn,nhd->rhd", weights, value_rows, preferred_element_type=jnp.float32
        )
        denominator = denominator + jnp.sum(weights.astype(jnp.float32), axis=2).T
        return (numerator, denominator)

    start_state = (
        jnp.zeros((row_total, head_count, HEAD), jnp.float32),
        jnp.zeros((row_total, head_count), jnp.float32),
    )
    all_keys, all_values = (
        lax.all_gather(keys_normed, "blk", axis=0, tiled=True),
        lax.all_gather(values_block, "blk", axis=0, tiled=True),
    )
    group_count = lax.axis_size("blk")
    per_block = 1
    while per_block * row_total < 512 and group_count % (per_block * 2) == 0:
        per_block = per_block * 2
    block_rows = per_block * row_total
    block_count = group_count // per_block
    key_blocks = all_keys.reshape(block_count, block_rows, all_keys.shape[1])
    value_blocks = all_values.reshape(block_count, block_rows, all_values.shape[1])

    def scan_step(running, block_pair):
        return (attend(running, block_pair), None)

    (numerator, denominator), unused = lax.scan(scan_step, start_state, (key_blocks, value_blocks))
    attended = (numerator / denominator[:, :, None]).astype(jnp.bfloat16).reshape(row_total, -1)
    attended_flipped = (attended.astype(jnp.float32) * signed(mix_bits)).astype(jnp.bfloat16)
    attended_pair = jnp.stack([attended, attended_flipped])
    out_signs = signed(out_bits)
    partial_out = jnp.einsum(
        "mrc,mcn->rmn",
        attended_pair,
        lax.all_gather(out_weights, "blk", axis=2, tiled=True),
        preferred_element_type=jnp.float32,
    )
    summed = lax.psum_scatter(
        partial_out.astype(jnp.bfloat16), "uly", scatter_dimension=0, tiled=True
    ).astype(jnp.float32)
    own_rows = summed.shape[0]
    own_signs = lax.dynamic_slice_in_dim(out_signs, lax.axis_index("uly") * own_rows, own_rows, 0)
    result_rows = summed[:, 0] + own_signs * summed[:, 1]
    return result_rows.astype(jnp.bfloat16)


def dot32(a, b):
    return lax.dot_general(
        a, b, (((1,), (0,)), ((), ())), preferred_element_type=jnp.float32
    )


def dot32_t(a, b):
    return lax.dot_general(
        a, b, (((1,), (1,)), ((), ())), preferred_element_type=jnp.float32
    )


bf = jnp.bfloat16
VMEM = pl.BlockSpec(memory_space=pltpu.VMEM)
SMEM = pl.BlockSpec(memory_space=pltpu.SMEM)
ANY = pl.BlockSpec(memory_space=pl.ANY)


def call(kernel, outs, out_specs, in_specs, scratch=(), flops=0, moved=0):
    return pl.pallas_call(
        kernel,
        out_shape=outs,
        in_specs=in_specs,
        out_specs=out_specs,
        scratch_shapes=list(scratch),
        compiler_params=pltpu.CompilerParams(vmem_limit_bytes=40 * 1024 * 1024),
        cost_estimate=pl.CostEstimate(flops=flops, bytes_accessed=moved, transcendentals=0),
    )


def shape(*dims, dtype=bf):
    return jax.ShapeDtypeStruct(dims, dtype)


def lanes(index, size):
    return pl.ds(pl.multiple_of(index * size, 128), size)


def copy_kernel(first, count, weights, out, sems):
    copies = [
        pltpu.make_async_copy(weights.at[m, pl.ds(first, count)], out.at[m], sems.at[m])
        for m in (0, 1)
    ]
    for copy in copies:
        copy.start()
    for copy in copies:
        copy.wait()


def sign_pieces(bits, u, team):
    piece = bits.shape[0] // team
    parts = [bits[pl.ds(pl.multiple_of((u ^ r) * piece, 8), piece), :] for r in range(team)]
    return [(2 * part - 1).astype(jnp.float32) for part in parts]


def sign_kernel(team, place, sign_bits, signs):
    for part in range(signs.shape[0]):
        pieces = sign_pieces(sign_bits.at[part], place[2], team)
        signs[part] = jnp.concatenate(pieces, axis=0).astype(bf)


def prepare_kernel(place, tokens, in_bits, *blocks):
    wide = tokens.shape[1] // len(blocks)
    for k, block in enumerate(blocks):
        cut = lanes(place[0] ^ k, wide)
        plain = tokens[:, cut]
        sign = (2 * in_bits[:, cut] - 1).astype(jnp.float32)
        block[0] = plain
        block[1] = (plain.astype(jnp.float32) * sign).astype(bf)


def late_signs_kernel(team, place, out_bits, mix_bits, weights, query_weights, *refs):
    blocks, sems = refs[:-1], refs[-1]
    copies = [
        pltpu.make_async_copy(weights.at[m, 0], query_weights.at[m], sems.at[m]) for m in (0, 1)
    ]
    for copy in copies:
        copy.start()
    z, u = place[0], place[2]
    wide = out_bits.shape[1] // len(blocks)
    own_rows = blocks[0].shape[1]
    mix = [part.astype(bf) for part in sign_pieces(mix_bits, u, team)]
    for k, block in enumerate(blocks):
        cut = lanes(z ^ k, wide)
        for i, r in enumerate((0, 2)):
            bits = out_bits[pl.ds(pl.multiple_of((u ^ r) * own_rows, 8), own_rows), cut]
            block[i] = (2 * bits - 1).astype(jnp.float32).astype(bf)
        for r in range(team):
            block[2 + r] = mix[r]
    for copy in copies:
        copy.wait()


def stack_kernel(*refs):
    for k, ref in enumerate(refs[:-1]):
        refs[-1][k] = ref[: refs[-1].shape[1]]


def pair_kernel(own, taken, out):
    out[0] = own[...]
    out[1] = taken[...]


def rows_kernel(own, taken, rows):
    depth, kinds, piece = own.shape[1:4]
    for m in range(kinds):
        for j in range(depth):
            parts = [ref[y, j, m].astype(jnp.float32) for y in (0, 1) for ref in (own, taken)]
            at = j * 4 * piece
            rows[m, at : at + 4 * piece] = jnp.concatenate(parts, axis=0).astype(bf)


def project_kernel(
    parts, size, place, rows, weights, partner, signs_0, signs_2, signs_13,
    send, keep_own, keep_two, held, total, sems,
):
    z, x = place[0], place[1]
    slab = weights.shape[2]
    own = pl.ds(pl.multiple_of(x * slab, 64), slab)
    other = pl.ds(pl.multiple_of((1 - x) * slab, 64), slab)
    depth = rows.shape[1] // size
    half = depth * size
    copies = []
    for i, part in enumerate(parts):
        for m in (0, 1):
            near, far = weights.at[m, part], partner.at[m, i]
            copies.append(pltpu.make_async_copy(near, held.at[i, m, own], sems.at[i, m, 0]))
            copies.append(pltpu.make_async_copy(far, held.at[i, m, other], sems.at[i, m, 1]))
    for copy in copies:
        copy.start()

    def block(j, head):
        return total[j * size : (j + 1) * size, lanes(head, HEAD)]

    def main(target, start, k):
        for j in range(depth):
            at = start + (j ^ k) * size
            target[at : at + size] = block(j, z ^ k).astype(target.dtype)

    def rest(target, start, j):
        target[start : start + size] = block(j, depth).astype(target.dtype)

    for i, part in enumerate(parts):
        for copy in copies[4 * i : 4 * i + 4]:
            copy.wait()
        total[...] = dot32(rows[1], held[i, 1])
        plain = dot32(rows[0], held[i, 0])
        signs = (signs_0[part], signs_13[0, part], signs_2[part], signs_13[1, part])
        for j in range(depth):
            cut = slice(j * size, (j + 1) * size)
            total[cut] = plain[cut] + signs[j].astype(jnp.float32) * total[cut]
        if part:
            main(send, 3 * half * i, 1)
            main(send, 3 * half * i + half, 3)
            main(keep_own, 2 * half * i, 0)
            main(keep_two, half * i, 2)
            for j in range(depth):
                rest(send, 3 * half * i + 2 * half + (j ^ 1) * size, j)
                rest(keep_own, 2 * half * i + half + j * size, j)
        else:
            main(send, 0, 1)
            rest(send, half, 1)
            main(send, half + size, 3)
            rest(send, 2 * half + size, 3)
            main(keep_own, 0, 0)
            rest(keep_own, half, 0)
            main(keep_two, 0, 2)
            rest(keep_two, half, 2)


def middle_kernel(size, keep_own, keep_two, taken, send, total):
    count = keep_two.shape[0]
    if keep_own.shape[0] == count:
        total[...] = keep_own[...] + taken[:count].astype(jnp.float32)
        send[...] = (keep_two[...] + taken[count:].astype(jnp.float32)).astype(bf)
        return
    half = count // 2
    for i in (0, 1):
        base, got = 2 * half * i, 3 * half * i
        first = slice(base, base + half)
        total[first] = keep_own[first] + taken[got : got + half].astype(jnp.float32)
        far = keep_two[half * i : half * i + half]
        send[first] = (far + taken[got + half : got + 2 * half].astype(jnp.float32)).astype(bf)
        for j in range(half // size):
            cut = slice(base + half + j * size, base + half + (j + 1) * size)
            at = got + 2 * half + j * size
            value = keep_own[cut] + taken[at : at + size].astype(jnp.float32)
            total[cut] = value
            at = base + half + (j ^ 2) * size
            send[at : at + size] = value.astype(bf)


def norm_rows(values, gain_row):
    wide = values.astype(jnp.float32)
    inverse_rms = lax.rsqrt(jnp.mean(wide * wide, axis=-1, keepdims=True) + epsilon)
    return (wide * inverse_rms * gain_row).astype(bf)


def key_value_kernel(half, place, total, taken, gain, out):
    keep = (total[...] + taken[...].astype(jnp.float32)).astype(bf)
    heads = gain.shape[0]
    out[:half] = norm_rows(keep[:half], gain[pl.ds(place[0], 1), :])
    out[half : 2 * half] = norm_rows(keep[half : 2 * half], gain[heads - 1 : heads, :])
    out[2 * half :] = keep[2 * half :]


def attend_kernel(half, place, total, taken, gain, own, partner, out):
    keep = (total[...] + taken[...].astype(jnp.float32)).astype(bf)
    heads = gain.shape[0]

    def attend(queries, cut):
        score_scale = 1.0 / math.sqrt(HEAD)
        totals, sums = 0.0, 0.0
        for both in (own, partner):
            scores = dot32_t(queries, both[cut]) * score_scale
            weights = jnp.exp(scores).astype(bf)
            totals = totals + jnp.sum(weights.astype(jnp.float32), axis=1, keepdims=True)
            sums = sums + dot32(weights, both[2 * half + cut.start : 2 * half + cut.stop])
        return (sums / totals).astype(bf)

    first = norm_rows(keep[:half], gain[pl.ds(place[0], 1), :])
    out[:half] = attend(first, slice(0, half))
    last = norm_rows(keep[half:], gain[heads - 1 : heads, :])
    out[half:] = attend(last, slice(half, 2 * half))


def final_kernel(place, *refs):
    out = refs[-1]
    for k, block in enumerate(refs[:-1]):
        out[:, lanes(place[0] ^ k, block.shape[1])] = block[...]


def stationary_plan(
    tokens, in_bits, qkv_weights, qkv_bits, gain_query, gain_key, out_weights, mix_bits, out_bits
):
    groups = lax.axis_size("blk")
    team = lax.axis_size("uly")
    depth = groups // 2
    z = lax.axis_index("blk") // 2
    x = lax.axis_index("blk") % 2
    u = lax.axis_index("uly")
    own_rows, width = tokens.shape
    slab = qkv_weights.shape[2]
    columns = qkv_weights.shape[3]
    size = own_rows * team
    heads = columns // HEAD
    half = depth * size
    steps = range(depth)
    f32 = jnp.float32
    place = jnp.stack([z, x, u]).astype(jnp.int32)

    def swap_x(value):
        return lax.ppermute(value, "blk", [(i, i ^ 1) for i in range(groups)])

    def swap_z(value, step):
        return lax.ppermute(value, "blk", [(i, i ^ (2 * step)) for i in range(groups)])

    def swap_u(value, bit):
        return lax.ppermute(value, "uly", [(i, i ^ bit) for i in range(team)])

    def after(value, *earlier):
        return lax.optimization_barrier((value,) + earlier)[0]

    early = call(
        functools.partial(copy_kernel, 1, 2),
        shape(2, 2, slab, columns), ANY, [ANY], [pltpu.SemaphoreType.DMA((2,))],
    )(qkv_weights)
    partner_early = swap_x(early)

    blocks = call(
        prepare_kernel,
        [shape(2, own_rows, 2 * slab)] * depth, [VMEM] * depth, [SMEM] + [VMEM] * 2,
    )(place, after(tokens, early), in_bits)
    got = [blocks[0]] + [swap_z(blocks[k], k) for k in steps if k]

    sign_bits = jnp.transpose(qkv_bits, (1, 0, 2))
    sign_own = call(
        functools.partial(sign_kernel, team), shape(3, size, columns), VMEM, [SMEM, VMEM]
    )(place, after(sign_bits, blocks[0]))
    sign_two = swap_z(sign_own, 2)
    sign_pair = call(pair_kernel, shape(2, 3, size, columns), VMEM, [VMEM] * 2)(sign_own, sign_two)
    signs = (sign_own, sign_two, swap_z(sign_pair, 1))

    held_shape = (depth, 2, own_rows, 2 * slab)
    held = call(stack_kernel, shape(*held_shape), VMEM, [VMEM] * depth)(*got)
    held = call(pair_kernel, shape(2, *held_shape), VMEM, [VMEM] * 2)(held, swap_u(held, 2))
    rows = call(rows_kernel, shape(2, half, 2 * slab), VMEM, [VMEM] * 2)(held, swap_u(held, 1))

    query_weights, *late = call(
        functools.partial(late_signs_kernel, team),
        [shape(2, slab, columns)] + [shape(2 + team, own_rows, 2 * slab)] * depth,
        [ANY] + [VMEM] * depth,
        [SMEM] + [VMEM] * 2 + [ANY],
        [pltpu.SemaphoreType.DMA((2,))],
    )(place, after(out_bits, sign_own), mix_bits, qkv_weights)
    partner_query = swap_x(after(query_weights, partner_early, rows, sign_pair))
    out_t = jnp.transpose(out_weights, (0, 2, 1))
    out_partner = swap_x(after(out_t, partner_query))

    def project(parts, rows, partner):
        whole = len(parts)
        count = half + size
        counts = (3 * half * whole, 2 * half * whole, half * whole)
        if parts == (0,):
            counts = (2 * count, count, count)
        return call(
            functools.partial(project_kernel, parts, size),
            [shape(counts[0], HEAD)] + [shape(count, HEAD, dtype=f32) for count in counts[1:]],
            [VMEM] * 3,
            [SMEM, VMEM, ANY, ANY] + [VMEM] * 3,
            [
                pltpu.VMEM((whole, 2, 2 * slab, columns), bf),
                pltpu.VMEM((half, columns), f32),
                pltpu.SemaphoreType.DMA((whole, 2, 2)),
            ],
        )(place, rows, qkv_weights, partner, *signs)

    def middle(keep_own, keep_two, taken):
        count = keep_own.shape[0]
        return call(
            functools.partial(middle_kernel, size),
            [shape(count, HEAD), shape(count, HEAD, dtype=f32)],
            [VMEM] * 2,
            [VMEM] * 3,
        )(keep_own, keep_two, taken)

    both_send, both_own, both_two = project((1, 2), rows, partner_early)
    taken = swap_z(both_send, 1)
    late = [late[0]] + [swap_z(after(late[k], signs[2]), k) for k in steps if k]
    query_send, query_own, query_two = project(
        (0,), after(rows, both_send), partner_query.reshape(2, 1, slab, columns)
    )
    query_taken = swap_z(query_send, 1)
    send, both_total = middle(both_own, both_two, after(taken, query_send, *late[1:]))
    both_last = swap_z(send, 2)
    send, query_total = middle(query_own, query_two, after(query_taken, both_total))
    query_last = swap_z(send, 2)
    both = call(
        functools.partial(key_value_kernel, half),
        shape(4 * half, HEAD), VMEM, [SMEM] + [VMEM] * 3,
    )(place, both_total, after(both_last, query_total), gain_key.reshape(heads, HEAD))
    done = call(
        functools.partial(attend_kernel, half),
        shape(half + size, HEAD), VMEM, [SMEM] + [VMEM] * 5,
    )(place, query_total, query_last, gain_query.reshape(heads, HEAD), both, swap_x(both))

    by_head, last_head = [], []
    for k in steps:
        block = swap_z(done, k) if k else done
        main = block[:half].reshape(depth, size, HEAD)
        by_head.append(jnp.concatenate([main[j ^ k] for j in steps], axis=0))
        last_head.append(block[half:])
    attended = jnp.concatenate(by_head + [jnp.concatenate(last_head, axis=0)], axis=1)

    def relative(value, axis):
        parts = [
            lax.dynamic_slice_in_dim(value, (z ^ k) * HEAD, HEAD, axis) for k in steps
        ] + [lax.slice_in_dim(value, depth * HEAD, heads * HEAD, axis=axis)]
        return jnp.concatenate(parts, axis=axis)

    mix = relative(jnp.concatenate([g[2:].reshape(size, columns) for g in late], axis=0), 1)
    attended_flipped = attended * mix
    first = jnp.where(x == 0, out_t, out_partner)
    second = jnp.where(x == 0, out_partner, out_t)
    out_full = relative(jnp.concatenate([first, second], axis=1), 2)
    partial = jnp.stack(
        [dot32_t(attended, out_full[0]), dot32_t(attended_flipped, out_full[1])]
    ).astype(bf)
    partial = partial.reshape(2, depth, team, own_rows, 2 * slab)
    summed = partial[:, :, 0::2].astype(f32) + swap_u(partial[:, :, 1::2], 1).astype(f32)
    out_signs = jnp.stack([g[:2] for g in late]).astype(f32)
    summed = summed[0] + out_signs * summed[1]
    summed = (summed[:, 0] + swap_u(summed[:, 1].astype(bf), 2).astype(f32)).astype(bf)
    final = [summed[0]] + [swap_z(summed[k], k) for k in steps if k]
    return call(
        final_kernel, shape(own_rows, width), VMEM, [SMEM] + [VMEM] * depth
    )(place, *final)


def body(*arrays):
    heads = arrays[2].shape[3] // HEAD
    depth = lax.axis_size("blk") // 2
    if depth == heads - 1 and depth == 4 and lax.axis_size("uly") == 4:
        return stationary_plan(*arrays)
    return gather_plan(*arrays)


def solution(mesh):
    return jax.shard_map(
        body,
        mesh=mesh,
        in_specs=(
            P(("blk", "uly"), None),
            P(("blk", "uly"), None),
            P(None, None, "blk", "uly"),
            P("blk", None, "uly"),
            P("uly"),
            P("uly"),
            P(None, "uly", "blk"),
            P("blk", "uly"),
            P("blk", None),
        ),
        out_specs=P(("blk", "uly"), None),
        check_vma=False,
    )
```

```python
import functools
import math

import jax
import jax.numpy as jnp
from jax import lax
from jax.experimental import pallas as pl
from jax.experimental.pallas import tpu as pltpu
from jax.sharding import PartitionSpec as P

HEAD = 128


epsilon = 1e-06


def signed(bit_values):
    return (2 * bit_values - 1).astype(jnp.float32)


def normalize(values, gain_vector):
    row_count = values.shape[0]
    by_head = values.astype(jnp.float32).reshape(row_count, -1, HEAD)
    inverse_rms = lax.rsqrt(jnp.mean(by_head * by_head, axis=-1, keepdims=True) + epsilon)
    return (by_head * inverse_rms * gain_vector.reshape(-1, HEAD)).astype(jnp.bfloat16)


def gather_plan(
    tokens, in_bits, qkv_weights, qkv_bits, gain_query, gain_key, out_weights, mix_bits, out_bits
):
    flipped = (tokens.astype(jnp.float32) * signed(in_bits)).astype(jnp.bfloat16)
    group_rows = lax.all_gather(jnp.stack([tokens, flipped]), "uly", axis=1, tiled=True)
    row_total = group_rows.shape[1]
    projections = jnp.einsum(
        "mrd,mkdc->rmkc",
        group_rows,
        lax.all_gather(qkv_weights, "blk", axis=2, tiled=True),
        preferred_element_type=jnp.float32,
    )
    projected = (projections[:, 0] + signed(qkv_bits) * projections[:, 1]).astype(jnp.bfloat16)
    queries = normalize(projected[:, 0], gain_query)
    head_count = queries.shape[1]
    keys_normed = normalize(projected[:, 1], gain_key).reshape(row_total, -1)
    values_block = projected[:, 2]
    score_scale = 1.0 / math.sqrt(HEAD)

    def attend(running, shard_piece):
        numerator, denominator = running
        key_rows = shard_piece[0].reshape(shard_piece[0].shape[0], head_count, HEAD)
        value_rows = shard_piece[1].reshape(shard_piece[1].shape[0], head_count, HEAD)
        scores = (
            jnp.einsum("rhd,nhd->hrn", queries, key_rows, preferred_element_type=jnp.float32)
            * score_scale
        )
        weights = jnp.exp(scores).astype(jnp.bfloat16)
        numerator = numerator + jnp.einsum(
            "hrn,nhd->rhd", weights, value_rows, preferred_element_type=jnp.float32
        )
        denominator = denominator + jnp.sum(weights.astype(jnp.float32), axis=2).T
        return (numerator, denominator)

    start_state = (
        jnp.zeros((row_total, head_count, HEAD), jnp.float32),
        jnp.zeros((row_total, head_count), jnp.float32),
    )
    all_keys, all_values = (
        lax.all_gather(keys_normed, "blk", axis=0, tiled=True),
        lax.all_gather(values_block, "blk", axis=0, tiled=True),
    )
    group_count = lax.axis_size("blk")
    per_block = 1
    while per_block * row_total < 512 and group_count % (per_block * 2) == 0:
        per_block = per_block * 2
    block_rows = per_block * row_total
    block_count = group_count // per_block
    key_blocks = all_keys.reshape(block_count, block_rows, all_keys.shape[1])
    value_blocks = all_values.reshape(block_count, block_rows, all_values.shape[1])

    def scan_step(running, block_pair):
        return (attend(running, block_pair), None)

    (numerator, denominator), unused = lax.scan(scan_step, start_state, (key_blocks, value_blocks))
    attended = (numerator / denominator[:, :, None]).astype(jnp.bfloat16).reshape(row_total, -1)
    attended_flipped = (attended.astype(jnp.float32) * signed(mix_bits)).astype(jnp.bfloat16)
    attended_pair = jnp.stack([attended, attended_flipped])
    out_signs = signed(out_bits)
    partial_out = jnp.einsum(
        "mrc,mcn->rmn",
        attended_pair,
        lax.all_gather(out_weights, "blk", axis=2, tiled=True),
        preferred_element_type=jnp.float32,
    )
    summed = lax.psum_scatter(
        partial_out.astype(jnp.bfloat16), "uly", scatter_dimension=0, tiled=True
    ).astype(jnp.float32)
    own_rows = summed.shape[0]
    own_signs = lax.dynamic_slice_in_dim(out_signs, lax.axis_index("uly") * own_rows, own_rows, 0)
    result_rows = summed[:, 0] + own_signs * summed[:, 1]
    return result_rows.astype(jnp.bfloat16)


def dot32(a, b):
    return lax.dot_general(
        a, b, (((1,), (0,)), ((), ())), preferred_element_type=jnp.float32
    )


def dot32_t(a, b):
    return lax.dot_general(
        a, b, (((1,), (1,)), ((), ())), preferred_element_type=jnp.float32
    )


bf = jnp.bfloat16
VMEM = pl.BlockSpec(memory_space=pltpu.VMEM)
SMEM = pl.BlockSpec(memory_space=pltpu.SMEM)
ANY = pl.BlockSpec(memory_space=pl.ANY)


def call(kernel, outs, out_specs, in_specs, scratch=(), flops=0, moved=0):
    return pl.pallas_call(
        kernel,
        out_shape=outs,
        in_specs=in_specs,
        out_specs=out_specs,
        scratch_shapes=list(scratch),
        compiler_params=pltpu.CompilerParams(vmem_limit_bytes=40 * 1024 * 1024),
        cost_estimate=pl.CostEstimate(flops=flops, bytes_accessed=moved, transcendentals=0),
    )


def shape(*dims, dtype=bf):
    return jax.ShapeDtypeStruct(dims, dtype)


def lanes(index, size):
    return pl.ds(pl.multiple_of(index * size, 128), size)


def copy_kernel(first, count, weights, out, sems):
    copies = [
        pltpu.make_async_copy(weights.at[m, pl.ds(first, count)], out.at[m], sems.at[m])
        for m in (0, 1)
    ]
    for copy in copies:
        copy.start()
    for copy in copies:
        copy.wait()


def sign_pieces(bits, u, team):
    piece = bits.shape[0] // team
    parts = [bits[pl.ds(pl.multiple_of((u ^ r) * piece, 8), piece), :] for r in range(team)]
    return [(2 * part - 1).astype(jnp.float32) for part in parts]


def sign_kernel(team, place, sign_bits, both_signs, query_signs):
    for part in range(3):
        pieces = sign_pieces(sign_bits.at[part], place[2], team)
        signs = jnp.concatenate(pieces, axis=0).astype(bf)
        if part:
            both_signs[part - 1] = signs
        else:
            query_signs[0] = signs


def prepare_kernel(place, tokens, in_bits, *blocks):
    wide = tokens.shape[1] // len(blocks)
    for k, block in enumerate(blocks):
        cut = lanes(place[0] ^ k, wide)
        plain = tokens[:, cut]
        sign = (2 * in_bits[:, cut] - 1).astype(jnp.float32)
        block[0] = plain
        block[1] = (plain.astype(jnp.float32) * sign).astype(bf)


def late_signs_kernel(team, place, out_bits, mix_bits, weights, query_weights, out, near, far, sems):
    copies = [
        pltpu.make_async_copy(weights.at[m, 0], query_weights.at[m], sems.at[m]) for m in (0, 1)
    ]
    for copy in copies:
        copy.start()
    z, u = place[0], place[2]
    own_rows, wide = out.shape[1:]

    def fill(target, start, k):
        for i, r in enumerate((0, 2)):
            rows = pl.ds(pl.multiple_of((u ^ r) * own_rows, 8), own_rows)
            bits = out_bits[rows, lanes(z ^ k, wide)]
            target[start + i] = (2 * bits - 1).astype(jnp.float32).astype(bf)

    fill(out, 0, 0)
    for r, part in enumerate(sign_pieces(mix_bits, u, team)):
        near[r] = part.astype(bf)
        far[r] = part.astype(bf)
    fill(near, team, 1)
    fill(far, team, 2)
    fill(far, team + 2, 3)
    for copy in copies:
        copy.wait()


def near_kernel(near, far, out):
    team = near.shape[0] - 2
    out[:team] = near[:team]
    out[team : 2 * team] = far[:team]
    out[2 * team : 2 * team + 2] = near[team:]
    out[2 * team + 2 :] = far[team + 2 :]


def late_kernel(place, own, near, far, got, mix, out):
    team, own_rows = near.shape[0] - 2, near.shape[1]
    size = team * own_rows
    out[0] = own[...]
    out[1] = got[2 * team : 2 * team + 2]
    out[2] = far[team : team + 2]
    out[3] = got[2 * team + 2 :]
    for j, (ref, start) in enumerate(((near, 0), (got, 0), (far, 0), (got, team))):
        cut = slice(j * size, (j + 1) * size)
        for k in range(5):
            head = lanes(place[0] ^ k, HEAD) if k < 4 else slice(4 * HEAD, None)
            parts = [ref[start + r, :, head].astype(jnp.float32) for r in range(team)]
            mix[cut, k * HEAD : (k + 1) * HEAD] = jnp.concatenate(parts, axis=0).astype(bf)


def stack_kernel(*refs):
    for k, ref in enumerate(refs[:-1]):
        refs[-1][k] = ref[: refs[-1].shape[1]]


def pair_kernel(own, taken, out):
    out[0] = own[...]
    out[1] = taken[...]


def rows_kernel(own, taken, rows):
    depth, kinds, piece = own.shape[1:4]
    for m in range(kinds):
        for j in range(depth):
            parts = [ref[y, j, m].astype(jnp.float32) for y in (0, 1) for ref in (own, taken)]
            at = j * 4 * piece
            rows[m, at : at + 4 * piece] = jnp.concatenate(parts, axis=0).astype(bf)


def project_kernel(
    parts, size, place, rows, weights, partner, signs_0, signs_2, signs_13,
    send, keep_own, keep_two, held, total, sems,
):
    z, x = place[0], place[1]
    slab = weights.shape[2]
    own = pl.ds(pl.multiple_of(x * slab, 64), slab)
    other = pl.ds(pl.multiple_of((1 - x) * slab, 64), slab)
    depth = rows.shape[1] // size
    half = depth * size
    copies = []
    for i, part in enumerate(parts):
        for m in (0, 1):
            near, far = weights.at[m, part], partner.at[m, i]
            copies.append(pltpu.make_async_copy(near, held.at[i, m, own], sems.at[i, m, 0]))
            copies.append(pltpu.make_async_copy(far, held.at[i, m, other], sems.at[i, m, 1]))
    for copy in copies:
        copy.start()

    def block(j, head):
        return total[j * size : (j + 1) * size, lanes(head, HEAD)]

    def main(target, start, k):
        for j in range(depth):
            at = start + (j ^ k) * size
            target[at : at + size] = block(j, z ^ k).astype(target.dtype)

    def rest(target, start, j):
        target[start : start + size] = block(j, depth).astype(target.dtype)

    for i, part in enumerate(parts):
        for copy in copies[4 * i : 4 * i + 4]:
            copy.wait()
        total[...] = dot32(rows[1], held[i, 1])
        plain = dot32(rows[0], held[i, 0])
        signs = (signs_0[i], signs_13[0, i], signs_2[i], signs_13[1, i])
        for j in range(depth):
            cut = slice(j * size, (j + 1) * size)
            total[cut] = plain[cut] + signs[j].astype(jnp.float32) * total[cut]
        if part:
            main(send, 3 * half * i, 1)
            main(send, 3 * half * i + half, 3)
            main(keep_own, 2 * half * i, 0)
            main(keep_two, half * i, 2)
            for j in range(depth):
                rest(send, 3 * half * i + 2 * half + (j ^ 1) * size, j)
                rest(keep_own, 2 * half * i + half + j * size, j)
        else:
            main(send, 0, 1)
            rest(send, half, 1)
            main(send, half + size, 3)
            rest(send, 2 * half + size, 3)
            main(keep_own, 0, 0)
            rest(keep_own, half, 0)
            main(keep_two, 0, 2)
            rest(keep_two, half, 2)


def middle_kernel(size, keep_own, keep_two, taken, send, total):
    count = keep_two.shape[0]
    if keep_own.shape[0] == count:
        total[...] = keep_own[...] + taken[:count].astype(jnp.float32)
        send[...] = (keep_two[...] + taken[count:].astype(jnp.float32)).astype(bf)
        return
    half = count // 2
    for i in (0, 1):
        base, got = 2 * half * i, 3 * half * i
        first = slice(base, base + half)
        total[first] = keep_own[first] + taken[got : got + half].astype(jnp.float32)
        far = keep_two[half * i : half * i + half]
        send[first] = (far + taken[got + half : got + 2 * half].astype(jnp.float32)).astype(bf)
        for j in range(half // size):
            cut = slice(base + half + j * size, base + half + (j + 1) * size)
            at = got + 2 * half + j * size
            value = keep_own[cut] + taken[at : at + size].astype(jnp.float32)
            total[cut] = value
            at = base + half + (j ^ 2) * size
            send[at : at + size] = value.astype(bf)


def norm_rows(values, gain_row):
    wide = values.astype(jnp.float32)
    inverse_rms = lax.rsqrt(jnp.mean(wide * wide, axis=-1, keepdims=True) + epsilon)
    return (wide * inverse_rms * gain_row).astype(bf)


def key_value_kernel(half, place, total, taken, gain, out):
    keep = (total[...] + taken[...].astype(jnp.float32)).astype(bf)
    heads = gain.shape[0]
    out[:half] = norm_rows(keep[:half], gain[pl.ds(place[0], 1), :])
    out[half : 2 * half] = norm_rows(keep[half : 2 * half], gain[heads - 1 : heads, :])
    out[2 * half :] = keep[2 * half :]


def attend_kernel(half, place, total, taken, gain, own, partner, out):
    keep = (total[...] + taken[...].astype(jnp.float32)).astype(bf)
    heads = gain.shape[0]

    def attend(queries, cut):
        score_scale = 1.0 / math.sqrt(HEAD)
        totals, sums = 0.0, 0.0
        for both in (own, partner):
            scores = dot32_t(queries, both[cut]) * score_scale
            weights = jnp.exp(scores).astype(bf)
            totals = totals + jnp.sum(weights.astype(jnp.float32), axis=1, keepdims=True)
            sums = sums + dot32(weights, both[2 * half + cut.start : 2 * half + cut.stop])
        return (sums / totals).astype(bf)

    first = norm_rows(keep[:half], gain[pl.ds(place[0], 1), :])
    out[:half] = attend(first, slice(0, half))
    last = norm_rows(keep[half:], gain[heads - 1 : heads, :])
    out[half:] = attend(last, slice(half, 2 * half))


def core_kernel(own, taken, signs, kept, sent):
    for i, target in enumerate((kept, sent)):
        for j in range(kept.shape[0]):
            parts = [own[m, j, i].astype(jnp.float32) + taken[m, j, i].astype(jnp.float32) for m in (0, 1)]
            value = parts[0] + signs[j, i].astype(jnp.float32) * parts[1]
            target[j] = value.astype(target.dtype)


def team_kernel(kept, taken, *blocks):
    for j, block in enumerate(blocks):
        block[...] = (kept[j] + taken[j].astype(jnp.float32)).astype(bf)


def final_kernel(place, *refs):
    out = refs[-1]
    for k, block in enumerate(refs[:-1]):
        out[:, lanes(place[0] ^ k, block.shape[1])] = block[...]


def stationary_plan(
    tokens, in_bits, qkv_weights, qkv_bits, gain_query, gain_key, out_weights, mix_bits, out_bits
):
    groups = lax.axis_size("blk")
    team = lax.axis_size("uly")
    depth = groups // 2
    z = lax.axis_index("blk") // 2
    x = lax.axis_index("blk") % 2
    u = lax.axis_index("uly")
    own_rows, width = tokens.shape
    slab = qkv_weights.shape[2]
    columns = qkv_weights.shape[3]
    size = own_rows * team
    heads = columns // HEAD
    half = depth * size
    steps = range(depth)
    f32 = jnp.float32
    place = jnp.stack([z, x, u]).astype(jnp.int32)

    def swap_x(value):
        return lax.ppermute(value, "blk", [(i, i ^ 1) for i in range(groups)])

    def swap_z(value, step):
        return lax.ppermute(value, "blk", [(i, i ^ (2 * step)) for i in range(groups)])

    def swap_u(value, bit):
        return lax.ppermute(value, "uly", [(i, i ^ bit) for i in range(team)])

    def after(value, *earlier):
        return lax.optimization_barrier((value,) + earlier)[0]

    early = call(
        functools.partial(copy_kernel, 1, 2),
        shape(2, 2, slab, columns), ANY, [ANY], [pltpu.SemaphoreType.DMA((2,))],
    )(qkv_weights)
    partner_early = swap_x(early)

    blocks = call(
        prepare_kernel,
        [shape(2, own_rows, 2 * slab)] * depth, [VMEM] * depth, [SMEM] + [VMEM] * 2,
    )(place, after(tokens, early), in_bits)
    got = [blocks[0]] + [swap_z(blocks[k], k) for k in steps if k]

    sign_bits = jnp.transpose(qkv_bits, (1, 0, 2))
    both_signs, query_signs = call(
        functools.partial(sign_kernel, team),
        [shape(2, size, columns), shape(1, size, columns)], [VMEM] * 2, [SMEM, VMEM],
    )(place, after(sign_bits, blocks[0]))

    def pair(first, second):
        return call(pair_kernel, shape(2, *first.shape), VMEM, [VMEM] * 2)(first, second)

    both_far = swap_z(both_signs, 2)
    both_pair = pair(both_signs, both_far)
    both_near = swap_z(both_pair, 1)
    query_far = swap_z(after(query_signs, both_far), 2)
    query_near = swap_z(after(pair(query_signs, query_far), both_near), 1)

    held_shape = (depth, 2, own_rows, 2 * slab)
    held = call(stack_kernel, shape(*held_shape), VMEM, [VMEM] * depth)(*got)
    held = pair(held, swap_u(after(held, both_far), 2))
    rows = call(rows_kernel, shape(2, half, 2 * slab), VMEM, [VMEM] * 2)(
        held, after(swap_u(after(held, both_near), 1), query_far)
    )

    query_weights, late_own, late_near, late_far = call(
        functools.partial(late_signs_kernel, team),
        [shape(2, slab, columns)]
        + [shape(count, own_rows, 2 * slab) for count in (2, team + 2, team + 4)],
        [ANY] + [VMEM] * 3,
        [SMEM] + [VMEM] * 2 + [ANY],
        [pltpu.SemaphoreType.DMA((2,))],
    )(place, after(out_bits, both_signs), mix_bits, qkv_weights)
    late_far = swap_z(after(late_far, query_far), 2)
    partner_query = swap_x(after(query_weights, partner_early, both_pair))
    out_t = jnp.transpose(out_weights, (0, 2, 1))
    out_partner = swap_x(after(out_t, partner_query))

    def project(parts, rows, partner, signs):
        whole = len(parts)
        count = half + size
        counts = (3 * half * whole, 2 * half * whole, half * whole)
        if parts == (0,):
            counts = (2 * count, count, count)
        return call(
            functools.partial(project_kernel, parts, size),
            [shape(counts[0], HEAD)] + [shape(count, HEAD, dtype=f32) for count in counts[1:]],
            [VMEM] * 3,
            [SMEM, VMEM, ANY, ANY] + [VMEM] * 3,
            [
                pltpu.VMEM((whole, 2, 2 * slab, columns), bf),
                pltpu.VMEM((half, columns), f32),
                pltpu.SemaphoreType.DMA((whole, 2, 2)),
            ],
        )(place, rows, qkv_weights, partner, *signs)

    def middle(keep_own, keep_two, taken):
        count = keep_own.shape[0]
        return call(
            functools.partial(middle_kernel, size),
            [shape(count, HEAD), shape(count, HEAD, dtype=f32)],
            [VMEM] * 2,
            [VMEM] * 3,
        )(keep_own, keep_two, taken)

    both_send, both_own, both_two = project(
        (1, 2), rows, partner_early, (both_signs, both_far, both_near)
    )
    taken = swap_z(both_send, 1)
    query_send, query_own, query_two = project(
        (0,), after(rows, both_send), partner_query.reshape(2, 1, slab, columns),
        (query_signs, query_far, query_near),
    )
    query_taken = swap_z(query_send, 1)
    send, both_total = middle(both_own, both_two, after(taken, query_send, late_far))
    both_last = swap_z(send, 2)
    late_got = call(near_kernel, shape(2 * team + 4, own_rows, 2 * slab), VMEM, [VMEM] * 2)(
        late_near, late_far
    )
    late_got = swap_z(after(late_got, both_total), 1)
    send, query_total = middle(query_own, query_two, after(query_taken, both_total))
    query_last = swap_z(send, 2)
    both = call(
        functools.partial(key_value_kernel, half),
        shape(4 * half, HEAD), VMEM, [SMEM] + [VMEM] * 3,
    )(place, both_total, after(both_last, query_total, late_got), gain_key.reshape(heads, HEAD))
    done = call(
        functools.partial(attend_kernel, half),
        shape(half + size, HEAD), VMEM, [SMEM] + [VMEM] * 5,
    )(place, query_total, query_last, gain_query.reshape(heads, HEAD), both, swap_x(both))

    by_head, last_head = [], []
    for k in steps:
        block = swap_z(done, k) if k else done
        main = block[:half].reshape(depth, size, HEAD)
        by_head.append(jnp.concatenate([main[j ^ k] for j in steps], axis=0))
        last_head.append(block[half:])
    attended = jnp.concatenate(by_head + [jnp.concatenate(last_head, axis=0)], axis=1)

    def relative(value, axis):
        parts = [
            lax.dynamic_slice_in_dim(value, (z ^ k) * HEAD, HEAD, axis) for k in steps
        ] + [lax.slice_in_dim(value, depth * HEAD, heads * HEAD, axis=axis)]
        return jnp.concatenate(parts, axis=axis)

    mix, out_signs = call(
        late_kernel,
        [shape(half, columns), shape(depth, 2, own_rows, 2 * slab)], [VMEM] * 2,
        [SMEM] + [VMEM] * 4,
    )(place, late_own, late_near, late_far, late_got)
    attended_flipped = attended * mix
    first = jnp.where(x == 0, out_t, out_partner)
    second = jnp.where(x == 0, out_partner, out_t)
    out_full = relative(jnp.concatenate([first, second], axis=1), 2)
    partial = jnp.stack(
        [dot32_t(attended, out_full[0]), dot32_t(attended_flipped, out_full[1])]
    ).astype(bf)
    partial = partial.reshape(2, depth, team, own_rows, 2 * slab)
    kept, sent = call(
        core_kernel,
        [shape(depth, own_rows, 2 * slab, dtype=f32), shape(depth, own_rows, 2 * slab)],
        [VMEM] * 2, [VMEM] * 3,
    )(partial[:, :, 0::2], swap_u(partial[:, :, 1::2], 1), out_signs)
    blocks = call(
        team_kernel, [shape(own_rows, 2 * slab)] * depth, [VMEM] * depth, [VMEM] * 2
    )(kept, swap_u(sent, 2))
    return call(
        final_kernel, shape(own_rows, width), VMEM, [SMEM] + [VMEM] * depth
    )(place, blocks[0], *[swap_z(blocks[k], k) for k in steps if k])


def body(*arrays):
    heads = arrays[2].shape[3] // HEAD
    depth = lax.axis_size("blk") // 2
    if depth == heads - 1 and depth == 4 and lax.axis_size("uly") == 4:
        return stationary_plan(*arrays)
    return gather_plan(*arrays)


def solution(mesh):
    return jax.shard_map(
        body,
        mesh=mesh,
        in_specs=(
            P(("blk", "uly"), None),
            P(("blk", "uly"), None),
            P(None, None, "blk", "uly"),
            P("blk", None, "uly"),
            P("uly"),
            P("uly"),
            P(None, "uly", "blk"),
            P("blk", "uly"),
            P("blk", None),
        ),
        out_specs=P(("blk", "uly"), None),
        check_vma=False,
    )
```

```python
import functools
import math

import jax
import jax.numpy as jnp
from jax import lax
from jax.experimental import pallas as pl
from jax.experimental.pallas import tpu as pltpu
from jax.sharding import PartitionSpec as P

HEAD = 128


epsilon = 1e-06


def signed(bit_values):
    return (2 * bit_values - 1).astype(jnp.float32)


def normalize(values, gain_vector):
    row_count = values.shape[0]
    by_head = values.astype(jnp.float32).reshape(row_count, -1, HEAD)
    inverse_rms = lax.rsqrt(jnp.mean(by_head * by_head, axis=-1, keepdims=True) + epsilon)
    return (by_head * inverse_rms * gain_vector.reshape(-1, HEAD)).astype(jnp.bfloat16)


def gather_plan(
    tokens, in_bits, qkv_weights, qkv_bits, gain_query, gain_key, out_weights, mix_bits, out_bits
):
    flipped = (tokens.astype(jnp.float32) * signed(in_bits)).astype(jnp.bfloat16)
    group_rows = lax.all_gather(jnp.stack([tokens, flipped]), "uly", axis=1, tiled=True)
    row_total = group_rows.shape[1]
    projections = jnp.einsum(
        "mrd,mkdc->rmkc",
        group_rows,
        lax.all_gather(qkv_weights, "blk", axis=2, tiled=True),
        preferred_element_type=jnp.float32,
    )
    projected = (projections[:, 0] + signed(qkv_bits) * projections[:, 1]).astype(jnp.bfloat16)
    queries = normalize(projected[:, 0], gain_query)
    head_count = queries.shape[1]
    keys_normed = normalize(projected[:, 1], gain_key).reshape(row_total, -1)
    values_block = projected[:, 2]
    score_scale = 1.0 / math.sqrt(HEAD)

    def attend(running, shard_piece):
        numerator, denominator = running
        key_rows = shard_piece[0].reshape(shard_piece[0].shape[0], head_count, HEAD)
        value_rows = shard_piece[1].reshape(shard_piece[1].shape[0], head_count, HEAD)
        scores = (
            jnp.einsum("rhd,nhd->hrn", queries, key_rows, preferred_element_type=jnp.float32)
            * score_scale
        )
        weights = jnp.exp(scores).astype(jnp.bfloat16)
        numerator = numerator + jnp.einsum(
            "hrn,nhd->rhd", weights, value_rows, preferred_element_type=jnp.float32
        )
        denominator = denominator + jnp.sum(weights.astype(jnp.float32), axis=2).T
        return (numerator, denominator)

    start_state = (
        jnp.zeros((row_total, head_count, HEAD), jnp.float32),
        jnp.zeros((row_total, head_count), jnp.float32),
    )
    all_keys, all_values = (
        lax.all_gather(keys_normed, "blk", axis=0, tiled=True),
        lax.all_gather(values_block, "blk", axis=0, tiled=True),
    )
    group_count = lax.axis_size("blk")
    per_block = 1
    while per_block * row_total < 512 and group_count % (per_block * 2) == 0:
        per_block = per_block * 2
    block_rows = per_block * row_total
    block_count = group_count // per_block
    key_blocks = all_keys.reshape(block_count, block_rows, all_keys.shape[1])
    value_blocks = all_values.reshape(block_count, block_rows, all_values.shape[1])

    def scan_step(running, block_pair):
        return (attend(running, block_pair), None)

    (numerator, denominator), unused = lax.scan(scan_step, start_state, (key_blocks, value_blocks))
    attended = (numerator / denominator[:, :, None]).astype(jnp.bfloat16).reshape(row_total, -1)
    attended_flipped = (attended.astype(jnp.float32) * signed(mix_bits)).astype(jnp.bfloat16)
    attended_pair = jnp.stack([attended, attended_flipped])
    out_signs = signed(out_bits)
    partial_out = jnp.einsum(
        "mrc,mcn->rmn",
        attended_pair,
        lax.all_gather(out_weights, "blk", axis=2, tiled=True),
        preferred_element_type=jnp.float32,
    )
    summed = lax.psum_scatter(
        partial_out.astype(jnp.bfloat16), "uly", scatter_dimension=0, tiled=True
    ).astype(jnp.float32)
    own_rows = summed.shape[0]
    own_signs = lax.dynamic_slice_in_dim(out_signs, lax.axis_index("uly") * own_rows, own_rows, 0)
    result_rows = summed[:, 0] + own_signs * summed[:, 1]
    return result_rows.astype(jnp.bfloat16)


def dot32(a, b):
    return lax.dot_general(
        a, b, (((1,), (0,)), ((), ())), preferred_element_type=jnp.float32
    )


def dot32_t(a, b):
    return lax.dot_general(
        a, b, (((1,), (1,)), ((), ())), preferred_element_type=jnp.float32
    )


bf = jnp.bfloat16
VMEM = pl.BlockSpec(memory_space=pltpu.VMEM)
SMEM = pl.BlockSpec(memory_space=pltpu.SMEM)
ANY = pl.BlockSpec(memory_space=pl.ANY)


def call(kernel, outs, out_specs, in_specs, scratch=(), flops=0, moved=0):
    return pl.pallas_call(
        kernel,
        out_shape=outs,
        in_specs=in_specs,
        out_specs=out_specs,
        scratch_shapes=list(scratch),
        compiler_params=pltpu.CompilerParams(vmem_limit_bytes=40 * 1024 * 1024),
        cost_estimate=pl.CostEstimate(flops=flops, bytes_accessed=moved, transcendentals=0),
    )


def shape(*dims, dtype=bf):
    return jax.ShapeDtypeStruct(dims, dtype)


def lanes(index, size):
    return pl.ds(pl.multiple_of(index * size, 128), size)


def copy_kernel(first, count, weights, out, sems):
    copies = [
        pltpu.make_async_copy(weights.at[m, pl.ds(first, count)], out.at[m], sems.at[m])
        for m in (0, 1)
    ]
    for copy in copies:
        copy.start()
    for copy in copies:
        copy.wait()


def sign_pieces(bits, u, team):
    piece = bits.shape[0] // team
    parts = [bits[pl.ds(pl.multiple_of((u ^ r) * piece, 8), piece), :] for r in range(team)]
    return [(2 * part - 1).astype(jnp.float32) for part in parts]


def prepare_kernel(team, place, tokens, in_bits, sign_bits, *blocks):
    wide = tokens.shape[1] // len(blocks)
    for k, block in enumerate(blocks):
        cut = lanes(place[0] ^ k, wide)
        plain = tokens[:, cut]
        sign = (2 * in_bits[:, cut] - 1).astype(jnp.float32)
        block[0] = plain
        block[1] = (plain.astype(jnp.float32) * sign).astype(bf)
    for i, part in enumerate((1, 2, 0)):
        for r, piece in enumerate(sign_pieces(sign_bits.at[part], place[2], team)):
            blocks[2][2 + team * i + r] = piece.astype(bf)


def late_signs_kernel(team, place, out_bits, mix_bits, weights, query_weights, out, near, far, sems):
    copies = [
        pltpu.make_async_copy(weights.at[m, 0], query_weights.at[m], sems.at[m]) for m in (0, 1)
    ]
    for copy in copies:
        copy.start()
    z, u = place[0], place[2]
    own_rows, wide = out.shape[1:]

    def fill(target, start, k):
        for i, r in enumerate((0, 2)):
            rows = pl.ds(pl.multiple_of((u ^ r) * own_rows, 8), own_rows)
            bits = out_bits[rows, lanes(z ^ k, wide)]
            target[start + i] = (2 * bits - 1).astype(jnp.float32).astype(bf)

    fill(out, 0, 0)
    for r, part in enumerate(sign_pieces(mix_bits, u, team)):
        near[r] = part.astype(bf)
        far[r] = part.astype(bf)
    fill(near, team, 1)
    fill(far, team, 2)
    fill(far, team + 2, 3)
    for copy in copies:
        copy.wait()


def near_kernel(near, far, out):
    team = near.shape[0] - 2
    out[:team] = near[:team]
    out[team : 2 * team] = far[:team]
    out[2 * team : 2 * team + 2] = near[team:]
    out[2 * team + 2 :] = far[team + 2 :]


def late_kernel(place, own, near, far, got, mix, out):
    team, own_rows = near.shape[0] - 2, near.shape[1]
    size = team * own_rows
    out[0] = own[...]
    out[1] = got[2 * team : 2 * team + 2]
    out[2] = far[team : team + 2]
    out[3] = got[2 * team + 2 :]
    for j, (ref, start) in enumerate(((near, 0), (got, 0), (far, 0), (got, team))):
        cut = slice(j * size, (j + 1) * size)
        for k in range(5):
            head = lanes(place[0] ^ k, HEAD) if k < 4 else slice(4 * HEAD, None)
            parts = [ref[start + r, :, head].astype(jnp.float32) for r in range(team)]
            mix[cut, k * HEAD : (k + 1) * HEAD] = jnp.concatenate(parts, axis=0).astype(bf)


def stack_kernel(*refs):
    for k, ref in enumerate(refs[:-1]):
        refs[-1][k] = ref[: refs[-1].shape[1]]


def pair_kernel(own, taken, out):
    out[0] = own[...]
    out[1] = taken[...]


def sign_pair_kernel(first, own, taken, out):
    team = (own.shape[0] - 2) // 3
    for b, ref in enumerate((own, taken)):
        for i in range(out.shape[1]):
            at = 2 + team * (first + i)
            pieces = [ref[at + r].astype(jnp.float32) for r in range(team)]
            out[b, i] = jnp.concatenate(pieces, axis=0).astype(bf)


def rows_kernel(own, taken, rows):
    depth, kinds, piece = own.shape[1:4]
    for m in range(kinds):
        for j in range(depth):
            parts = [ref[y, j, m].astype(jnp.float32) for y in (0, 1) for ref in (own, taken)]
            at = j * 4 * piece
            rows[m, at : at + 4 * piece] = jnp.concatenate(parts, axis=0).astype(bf)


def project_kernel(
    parts, size, place, rows, weights, partner, signs_02, signs_13,
    send, keep_own, keep_two, held, total, sems,
):
    z, x = place[0], place[1]
    slab = weights.shape[2]
    own = pl.ds(pl.multiple_of(x * slab, 64), slab)
    other = pl.ds(pl.multiple_of((1 - x) * slab, 64), slab)
    depth = rows.shape[1] // size
    half = depth * size
    copies = []
    for i, part in enumerate(parts):
        for m in (0, 1):
            near, far = weights.at[m, part], partner.at[m, i]
            copies.append(pltpu.make_async_copy(near, held.at[i, m, own], sems.at[i, m, 0]))
            copies.append(pltpu.make_async_copy(far, held.at[i, m, other], sems.at[i, m, 1]))
    for copy in copies:
        copy.start()

    def block(j, head):
        return total[j * size : (j + 1) * size, lanes(head, HEAD)]

    def main(target, start, k):
        for j in range(depth):
            at = start + (j ^ k) * size
            target[at : at + size] = block(j, z ^ k).astype(target.dtype)

    def rest(target, start, j):
        target[start : start + size] = block(j, depth).astype(target.dtype)

    for i, part in enumerate(parts):
        for copy in copies[4 * i : 4 * i + 4]:
            copy.wait()
        total[...] = dot32(rows[1], held[i, 1])
        plain = dot32(rows[0], held[i, 0])
        signs = (signs_02[0, i], signs_13[0, i], signs_02[1, i], signs_13[1, i])
        for j in range(depth):
            cut = slice(j * size, (j + 1) * size)
            total[cut] = plain[cut] + signs[j].astype(jnp.float32) * total[cut]
        if part:
            main(send, 3 * half * i, 1)
            main(send, 3 * half * i + half, 3)
            main(keep_own, 2 * half * i, 0)
            main(keep_two, half * i, 2)
            for j in range(depth):
                rest(send, 3 * half * i + 2 * half + (j ^ 1) * size, j)
                rest(keep_own, 2 * half * i + half + j * size, j)
        else:
            main(send, 0, 1)
            rest(send, half, 1)
            main(send, half + size, 3)
            rest(send, 2 * half + size, 3)
            main(keep_own, 0, 0)
            rest(keep_own, half, 0)
            main(keep_two, 0, 2)
            rest(keep_two, half, 2)


def middle_kernel(size, keep_own, keep_two, taken, send, total):
    count = keep_two.shape[0]
    if keep_own.shape[0] == count:
        total[...] = keep_own[...] + taken[:count].astype(jnp.float32)
        send[...] = (keep_two[...] + taken[count:].astype(jnp.float32)).astype(bf)
        return
    half = count // 2
    for i in (0, 1):
        base, got = 2 * half * i, 3 * half * i
        first = slice(base, base + half)
        total[first] = keep_own[first] + taken[got : got + half].astype(jnp.float32)
        far = keep_two[half * i : half * i + half]
        send[first] = (far + taken[got + half : got + 2 * half].astype(jnp.float32)).astype(bf)
        for j in range(half // size):
            cut = slice(base + half + j * size, base + half + (j + 1) * size)
            at = got + 2 * half + j * size
            value = keep_own[cut] + taken[at : at + size].astype(jnp.float32)
            total[cut] = value
            at = base + half + (j ^ 2) * size
            send[at : at + size] = value.astype(bf)


def norm_rows(values, gain_row):
    wide = values.astype(jnp.float32)
    inverse_rms = lax.rsqrt(jnp.mean(wide * wide, axis=-1, keepdims=True) + epsilon)
    return (wide * inverse_rms * gain_row).astype(bf)


def key_value_kernel(half, place, total, taken, gain, out):
    keep = (total[...] + taken[...].astype(jnp.float32)).astype(bf)
    heads = gain.shape[0]
    out[:half] = norm_rows(keep[:half], gain[pl.ds(place[0], 1), :])
    out[half : 2 * half] = norm_rows(keep[half : 2 * half], gain[heads - 1 : heads, :])
    out[2 * half :] = keep[2 * half :]


def attend_kernel(half, place, total, taken, gain, own, partner, out):
    keep = (total[...] + taken[...].astype(jnp.float32)).astype(bf)
    heads = gain.shape[0]

    def attend(queries, cut):
        score_scale = 1.0 / math.sqrt(HEAD)
        totals, sums = 0.0, 0.0
        for both in (own, partner):
            scores = dot32_t(queries, both[cut]) * score_scale
            weights = jnp.exp(scores).astype(bf)
            totals = totals + jnp.sum(weights.astype(jnp.float32), axis=1, keepdims=True)
            sums = sums + dot32(weights, both[2 * half + cut.start : 2 * half + cut.stop])
        return (sums / totals).astype(bf)

    first = norm_rows(keep[:half], gain[pl.ds(place[0], 1), :])
    out[:half] = attend(first, slice(0, half))
    last = norm_rows(keep[half:], gain[heads - 1 : heads, :])
    out[half:] = attend(last, slice(half, 2 * half))


def core_kernel(own, taken, signs, kept, sent):
    for i, target in enumerate((kept, sent)):
        for j in range(kept.shape[0]):
            parts = [own[m, j, i].astype(jnp.float32) + taken[m, j, i].astype(jnp.float32) for m in (0, 1)]
            value = parts[0] + signs[j, i].astype(jnp.float32) * parts[1]
            target[j] = value.astype(target.dtype)


def team_kernel(kept, taken, *blocks):
    for j, block in enumerate(blocks):
        block[...] = (kept[j] + taken[j].astype(jnp.float32)).astype(bf)


def final_kernel(place, *refs):
    out = refs[-1]
    for k, block in enumerate(refs[:-1]):
        out[:, lanes(place[0] ^ k, block.shape[1])] = block[...]


def stationary_plan(
    tokens, in_bits, qkv_weights, qkv_bits, gain_query, gain_key, out_weights, mix_bits, out_bits
):
    groups = lax.axis_size("blk")
    team = lax.axis_size("uly")
    depth = groups // 2
    z = lax.axis_index("blk") // 2
    x = lax.axis_index("blk") % 2
    u = lax.axis_index("uly")
    own_rows, width = tokens.shape
    slab = qkv_weights.shape[2]
    columns = qkv_weights.shape[3]
    size = own_rows * team
    heads = columns // HEAD
    half = depth * size
    steps = range(depth)
    f32 = jnp.float32
    place = jnp.stack([z, x, u]).astype(jnp.int32)

    def swap_x(value):
        return lax.ppermute(value, "blk", [(i, i ^ 1) for i in range(groups)])

    def swap_z(value, step):
        return lax.ppermute(value, "blk", [(i, i ^ (2 * step)) for i in range(groups)])

    def swap_u(value, bit):
        return lax.ppermute(value, "uly", [(i, i ^ bit) for i in range(team)])

    def after(value, *earlier):
        return lax.optimization_barrier((value,) + earlier)[0]

    early = call(
        functools.partial(copy_kernel, 1, 2),
        shape(2, 2, slab, columns), ANY, [ANY], [pltpu.SemaphoreType.DMA((2,))],
    )(qkv_weights)
    partner_early = swap_x(early)

    sign_bits = jnp.transpose(qkv_bits, (1, 0, 2))
    counts = [2 + 3 * team if k == 2 else 2 for k in steps]
    blocks = call(
        functools.partial(prepare_kernel, team),
        [shape(count, own_rows, 2 * slab) for count in counts],
        [VMEM] * depth, [SMEM] + [VMEM] * 3,
    )(place, after(tokens, early), in_bits, sign_bits)
    got = [blocks[0]] + [swap_z(blocks[k], k) for k in steps if k]

    def pair(first, second):
        return call(pair_kernel, shape(2, *first.shape), VMEM, [VMEM] * 2)(first, second)

    def sign_pair(first, count):
        return call(
            functools.partial(sign_pair_kernel, first),
            shape(2, count, size, columns), VMEM, [VMEM] * 2,
        )(blocks[2], got[2])

    both_pair = sign_pair(0, 2)
    both_near = swap_z(both_pair, 1)
    query_pair = sign_pair(2, 1)
    query_near = swap_z(after(query_pair, both_near), 1)

    held_shape = (depth, 2, own_rows, 2 * slab)
    held = call(stack_kernel, shape(*held_shape), VMEM, [VMEM] * depth)(*got)
    held = pair(held, swap_u(held, 2))
    rows = call(rows_kernel, shape(2, half, 2 * slab), VMEM, [VMEM] * 2)(
        held, swap_u(after(held, both_near), 1)
    )

    query_weights, late_own, late_near, late_far = call(
        functools.partial(late_signs_kernel, team),
        [shape(2, slab, columns)]
        + [shape(count, own_rows, 2 * slab) for count in (2, team + 2, team + 4)],
        [ANY] + [VMEM] * 3,
        [SMEM] + [VMEM] * 2 + [ANY],
        [pltpu.SemaphoreType.DMA((2,))],
    )(place, after(out_bits, blocks[0]), mix_bits, qkv_weights)
    partner_query = swap_x(after(query_weights, partner_early, both_pair))
    out_t = jnp.transpose(out_weights, (0, 2, 1))
    out_partner = swap_x(after(out_t, partner_query))

    def project(parts, rows, partner, pair, near):
        whole = len(parts)
        count = half + size
        counts = (3 * half * whole, 2 * half * whole, half * whole)
        if parts == (0,):
            counts = (2 * count, count, count)
        return call(
            functools.partial(project_kernel, parts, size),
            [shape(counts[0], HEAD)] + [shape(count, HEAD, dtype=f32) for count in counts[1:]],
            [VMEM] * 3,
            [SMEM, VMEM, ANY, ANY] + [VMEM] * 2,
            [
                pltpu.VMEM((whole, 2, 2 * slab, columns), bf),
                pltpu.VMEM((half, columns), f32),
                pltpu.SemaphoreType.DMA((whole, 2, 2)),
            ],
        )(place, rows, qkv_weights, partner, pair, near)

    def middle(keep_own, keep_two, taken):
        count = keep_own.shape[0]
        return call(
            functools.partial(middle_kernel, size),
            [shape(count, HEAD), shape(count, HEAD, dtype=f32)],
            [VMEM] * 2,
            [VMEM] * 3,
        )(keep_own, keep_two, taken)

    both_send, both_own, both_two = project(
        (1, 2), rows, partner_early, both_pair, both_near
    )
    taken = swap_z(both_send, 1)
    query_send, query_own, query_two = project(
        (0,), after(rows, both_send), partner_query.reshape(2, 1, slab, columns),
        query_pair, query_near,
    )
    query_taken = swap_z(query_send, 1)
    send, both_total = middle(both_own, both_two, after(taken, query_send))
    both_last = swap_z(send, 2)
    send, query_total = middle(query_own, query_two, after(query_taken, both_total))
    query_last = swap_z(send, 2)
    both = call(
        functools.partial(key_value_kernel, half),
        shape(4 * half, HEAD), VMEM, [SMEM] + [VMEM] * 3,
    )(place, both_total, after(both_last, query_total), gain_key.reshape(heads, HEAD))
    both_partner = swap_x(both)
    late_far = swap_z(after(late_far, both), 2)
    late_got = call(near_kernel, shape(2 * team + 4, own_rows, 2 * slab), VMEM, [VMEM] * 2)(
        late_near, late_far
    )
    late_got = swap_z(late_got, 1)
    done = call(
        functools.partial(attend_kernel, half),
        shape(half + size, HEAD), VMEM, [SMEM] + [VMEM] * 5,
    )(place, query_total, query_last, gain_query.reshape(heads, HEAD), both, both_partner)

    by_head, last_head = [], []
    for k in steps:
        block = swap_z(done, k) if k else done
        main = block[:half].reshape(depth, size, HEAD)
        by_head.append(jnp.concatenate([main[j ^ k] for j in steps], axis=0))
        last_head.append(block[half:])
    attended = jnp.concatenate(by_head + [jnp.concatenate(last_head, axis=0)], axis=1)

    def relative(value, axis):
        parts = [
            lax.dynamic_slice_in_dim(value, (z ^ k) * HEAD, HEAD, axis) for k in steps
        ] + [lax.slice_in_dim(value, depth * HEAD, heads * HEAD, axis=axis)]
        return jnp.concatenate(parts, axis=axis)

    mix, out_signs = call(
        late_kernel,
        [shape(half, columns), shape(depth, 2, own_rows, 2 * slab)], [VMEM] * 2,
        [SMEM] + [VMEM] * 4,
    )(place, late_own, late_near, late_far, late_got)
    attended_flipped = attended * mix
    first = jnp.where(x == 0, out_t, out_partner)
    second = jnp.where(x == 0, out_partner, out_t)
    out_full = relative(jnp.concatenate([first, second], axis=1), 2)
    partial = jnp.stack(
        [dot32_t(attended, out_full[0]), dot32_t(attended_flipped, out_full[1])]
    ).astype(bf)
    partial = partial.reshape(2, depth, team, own_rows, 2 * slab)
    kept, sent = call(
        core_kernel,
        [shape(depth, own_rows, 2 * slab, dtype=f32), shape(depth, own_rows, 2 * slab)],
        [VMEM] * 2, [VMEM] * 3,
    )(partial[:, :, 0::2], swap_u(partial[:, :, 1::2], 1), out_signs)
    blocks = call(
        team_kernel, [shape(own_rows, 2 * slab)] * depth, [VMEM] * depth, [VMEM] * 2
    )(kept, swap_u(sent, 2))
    return call(
        final_kernel, shape(own_rows, width), VMEM, [SMEM] + [VMEM] * depth
    )(place, blocks[0], *[swap_z(blocks[k], k) for k in steps if k])


def body(*arrays):
    heads = arrays[2].shape[3] // HEAD
    depth = lax.axis_size("blk") // 2
    if depth == heads - 1 and depth == 4 and lax.axis_size("uly") == 4:
        return stationary_plan(*arrays)
    return gather_plan(*arrays)


def solution(mesh):
    return jax.shard_map(
        body,
        mesh=mesh,
        in_specs=(
            P(("blk", "uly"), None),
            P(("blk", "uly"), None),
            P(None, None, "blk", "uly"),
            P("blk", None, "uly"),
            P("uly"),
            P("uly"),
            P(None, "uly", "blk"),
            P("blk", "uly"),
            P("blk", None),
        ),
        out_specs=P(("blk", "uly"), None),
        check_vma=False,
    )
```

```python
import functools
import math

import jax
import jax.numpy as jnp
from jax import lax
from jax.experimental import pallas as pl
from jax.experimental.pallas import tpu as pltpu
from jax.sharding import PartitionSpec as P

HEAD = 128


epsilon = 1e-06


def signed(bit_values):
    return (2 * bit_values - 1).astype(jnp.float32)


def normalize(values, gain_vector):
    row_count = values.shape[0]
    by_head = values.astype(jnp.float32).reshape(row_count, -1, HEAD)
    inverse_rms = lax.rsqrt(jnp.mean(by_head * by_head, axis=-1, keepdims=True) + epsilon)
    return (by_head * inverse_rms * gain_vector.reshape(-1, HEAD)).astype(jnp.bfloat16)


def gather_plan(
    tokens, in_bits, qkv_weights, qkv_bits, gain_query, gain_key, out_weights, mix_bits, out_bits
):
    flipped = (tokens.astype(jnp.float32) * signed(in_bits)).astype(jnp.bfloat16)
    group_rows = lax.all_gather(jnp.stack([tokens, flipped]), "uly", axis=1, tiled=True)
    row_total = group_rows.shape[1]
    projections = jnp.einsum(
        "mrd,mkdc->rmkc",
        group_rows,
        lax.all_gather(qkv_weights, "blk", axis=2, tiled=True),
        preferred_element_type=jnp.float32,
    )
    projected = (projections[:, 0] + signed(qkv_bits) * projections[:, 1]).astype(jnp.bfloat16)
    queries = normalize(projected[:, 0], gain_query)
    head_count = queries.shape[1]
    keys_normed = normalize(projected[:, 1], gain_key).reshape(row_total, -1)
    values_block = projected[:, 2]
    score_scale = 1.0 / math.sqrt(HEAD)

    def attend(running, shard_piece):
        numerator, denominator = running
        key_rows = shard_piece[0].reshape(shard_piece[0].shape[0], head_count, HEAD)
        value_rows = shard_piece[1].reshape(shard_piece[1].shape[0], head_count, HEAD)
        scores = (
            jnp.einsum("rhd,nhd->hrn", queries, key_rows, preferred_element_type=jnp.float32)
            * score_scale
        )
        weights = jnp.exp(scores).astype(jnp.bfloat16)
        numerator = numerator + jnp.einsum(
            "hrn,nhd->rhd", weights, value_rows, preferred_element_type=jnp.float32
        )
        denominator = denominator + jnp.sum(weights.astype(jnp.float32), axis=2).T
        return (numerator, denominator)

    start_state = (
        jnp.zeros((row_total, head_count, HEAD), jnp.float32),
        jnp.zeros((row_total, head_count), jnp.float32),
    )
    all_keys, all_values = (
        lax.all_gather(keys_normed, "blk", axis=0, tiled=True),
        lax.all_gather(values_block, "blk", axis=0, tiled=True),
    )
    group_count = lax.axis_size("blk")
    per_block = 1
    while per_block * row_total < 512 and group_count % (per_block * 2) == 0:
        per_block = per_block * 2
    block_rows = per_block * row_total
    block_count = group_count // per_block
    key_blocks = all_keys.reshape(block_count, block_rows, all_keys.shape[1])
    value_blocks = all_values.reshape(block_count, block_rows, all_values.shape[1])

    def scan_step(running, block_pair):
        return (attend(running, block_pair), None)

    (numerator, denominator), unused = lax.scan(scan_step, start_state, (key_blocks, value_blocks))
    attended = (numerator / denominator[:, :, None]).astype(jnp.bfloat16).reshape(row_total, -1)
    attended_flipped = (attended.astype(jnp.float32) * signed(mix_bits)).astype(jnp.bfloat16)
    attended_pair = jnp.stack([attended, attended_flipped])
    out_signs = signed(out_bits)
    partial_out = jnp.einsum(
        "mrc,mcn->rmn",
        attended_pair,
        lax.all_gather(out_weights, "blk", axis=2, tiled=True),
        preferred_element_type=jnp.float32,
    )
    summed = lax.psum_scatter(
        partial_out.astype(jnp.bfloat16), "uly", scatter_dimension=0, tiled=True
    ).astype(jnp.float32)
    own_rows = summed.shape[0]
    own_signs = lax.dynamic_slice_in_dim(out_signs, lax.axis_index("uly") * own_rows, own_rows, 0)
    result_rows = summed[:, 0] + own_signs * summed[:, 1]
    return result_rows.astype(jnp.bfloat16)


def dot32(a, b):
    return lax.dot_general(
        a, b, (((1,), (0,)), ((), ())), preferred_element_type=jnp.float32
    )


def dot32_t(a, b):
    return lax.dot_general(
        a, b, (((1,), (1,)), ((), ())), preferred_element_type=jnp.float32
    )


bf = jnp.bfloat16
VMEM = pl.BlockSpec(memory_space=pltpu.VMEM)
SMEM = pl.BlockSpec(memory_space=pltpu.SMEM)
ANY = pl.BlockSpec(memory_space=pl.ANY)


def call(kernel, outs, out_specs, in_specs, scratch=(), flops=0, moved=0):
    return pl.pallas_call(
        kernel,
        out_shape=outs,
        in_specs=in_specs,
        out_specs=out_specs,
        scratch_shapes=list(scratch),
        compiler_params=pltpu.CompilerParams(vmem_limit_bytes=40 * 1024 * 1024),
        cost_estimate=pl.CostEstimate(flops=flops, bytes_accessed=moved, transcendentals=0),
    )


def shape(*dims, dtype=bf):
    return jax.ShapeDtypeStruct(dims, dtype)


def lanes(index, size):
    return pl.ds(pl.multiple_of(index * size, 128), size)


def copy_kernel(first, count, weights, out, sems):
    copies = [
        pltpu.make_async_copy(weights.at[m, pl.ds(first, count)], out.at[m], sems.at[m])
        for m in (0, 1)
    ]
    for copy in copies:
        copy.start()
    for copy in copies:
        copy.wait()


def sign_pieces(bits, u, team):
    piece = bits.shape[0] // team
    parts = [bits[pl.ds(pl.multiple_of((u ^ r) * piece, 8), piece), :] for r in range(team)]
    return [(2 * part - 1).astype(jnp.float32) for part in parts]


def prepare_kernel(team, place, tokens, in_bits, sign_bits, *blocks):
    wide = tokens.shape[1] // len(blocks)
    for k, block in enumerate(blocks):
        cut = lanes(place[0] ^ k, wide)
        plain = tokens[:, cut]
        sign = (2 * in_bits[:, cut] - 1).astype(jnp.float32)
        block[0] = plain
        block[1] = (plain.astype(jnp.float32) * sign).astype(bf)
    for i, part in enumerate((1, 2, 0)):
        for r, piece in enumerate(sign_pieces(sign_bits.at[part], place[2], team)):
            blocks[2][2 + team * i + r] = piece.astype(bf)


def late_signs_kernel(team, place, out_bits, mix_bits, weights, query_weights, out, near, far, sems):
    copies = [
        pltpu.make_async_copy(weights.at[m, 0], query_weights.at[m], sems.at[m]) for m in (0, 1)
    ]
    for copy in copies:
        copy.start()
    z, u = place[0], place[2]
    own_rows, wide = out.shape[1:]

    def fill(target, start, k):
        for i, r in enumerate((0, 2)):
            rows = pl.ds(pl.multiple_of((u ^ r) * own_rows, 8), own_rows)
            bits = out_bits[rows, lanes(z ^ k, wide)]
            target[start + i] = (2 * bits - 1).astype(jnp.float32).astype(bf)

    fill(out, 0, 0)
    for r, part in enumerate(sign_pieces(mix_bits, u, team)):
        near[r] = part.astype(bf)
        far[r] = part.astype(bf)
    fill(near, team, 1)
    fill(far, team, 2)
    fill(far, team + 2, 3)
    for copy in copies:
        copy.wait()


def near_kernel(near, far, out):
    team = near.shape[0] - 2
    out[:team] = near[:team]
    out[team : 2 * team] = far[:team]
    out[2 * team : 2 * team + 2] = near[team:]
    out[2 * team + 2 :] = far[team + 2 :]


def late_kernel(place, own, near, far, got, mix, out):
    team, own_rows = near.shape[0] - 2, near.shape[1]
    size = team * own_rows
    out[0] = own[...]
    out[1] = got[2 * team : 2 * team + 2]
    out[2] = far[team : team + 2]
    out[3] = got[2 * team + 2 :]
    for j, (ref, start) in enumerate(((near, 0), (got, 0), (far, 0), (got, team))):
        cut = slice(j * size, (j + 1) * size)
        for k in range(5):
            head = lanes(place[0] ^ k, HEAD) if k < 4 else slice(4 * HEAD, None)
            parts = [ref[start + r, :, head].astype(jnp.float32) for r in range(team)]
            mix[cut, k * HEAD : (k + 1) * HEAD] = jnp.concatenate(parts, axis=0).astype(bf)


def stack_kernel(*refs):
    for k, ref in enumerate(refs[:-1]):
        refs[-1][k] = ref[: refs[-1].shape[1]]


def pair_kernel(own, taken, out):
    out[0] = own[...]
    out[1] = taken[...]


def sign_pair_kernel(first, own, taken, out):
    team = (own.shape[0] - 2) // 3
    for b, ref in enumerate((own, taken)):
        for i in range(out.shape[1]):
            at = 2 + team * (first + i)
            pieces = [ref[at + r].astype(jnp.float32) for r in range(team)]
            out[b, i] = jnp.concatenate(pieces, axis=0).astype(bf)


def rows_kernel(own, taken, rows):
    depth, kinds, piece = own.shape[1:4]
    for m in range(kinds):
        for j in range(depth):
            parts = [ref[y, j, m].astype(jnp.float32) for y in (0, 1) for ref in (own, taken)]
            at = j * 4 * piece
            rows[m, at : at + 4 * piece] = jnp.concatenate(parts, axis=0).astype(bf)


def project_kernel(
    parts, size, place, rows, weights, partner, signs_02, signs_13,
    send, keep_own, keep_two, held, total, sems,
):
    z, x = place[0], place[1]
    slab = weights.shape[2]
    own = pl.ds(pl.multiple_of(x * slab, 64), slab)
    other = pl.ds(pl.multiple_of((1 - x) * slab, 64), slab)
    depth = rows.shape[1] // size
    half = depth * size
    copies = []
    for i, part in enumerate(parts):
        for m in (0, 1):
            near, far = weights.at[m, part], partner.at[m, i]
            copies.append(pltpu.make_async_copy(near, held.at[i, m, own], sems.at[i, m, 0]))
            copies.append(pltpu.make_async_copy(far, held.at[i, m, other], sems.at[i, m, 1]))
    for copy in copies:
        copy.start()

    def block(j, head):
        return total[j * size : (j + 1) * size, lanes(head, HEAD)]

    def main(target, start, k):
        for j in range(depth):
            at = start + (j ^ k) * size
            target[at : at + size] = block(j, z ^ k).astype(target.dtype)

    def rest(target, start, j):
        target[start : start + size] = block(j, depth).astype(target.dtype)

    for i, part in enumerate(parts):
        for copy in copies[4 * i : 4 * i + 4]:
            copy.wait()
        total[...] = dot32(rows[1], held[i, 1])
        plain = dot32(rows[0], held[i, 0])
        signs = (signs_02[0, i], signs_13[0, i], signs_02[1, i], signs_13[1, i])
        for j in range(depth):
            cut = slice(j * size, (j + 1) * size)
            total[cut] = plain[cut] + signs[j].astype(jnp.float32) * total[cut]
        if part:
            main(send, 3 * half * i, 1)
            main(send, 3 * half * i + half, 3)
            main(keep_own, 2 * half * i, 0)
            main(keep_two, half * i, 2)
            for j in range(depth):
                rest(send, 3 * half * i + 2 * half + (j ^ 1) * size, j)
                rest(keep_own, 2 * half * i + half + j * size, j)
        else:
            main(send, 0, 1)
            rest(send, half, 1)
            main(send, half + size, 3)
            rest(send, 2 * half + size, 3)
            main(keep_own, 0, 0)
            rest(keep_own, half, 0)
            main(keep_two, 0, 2)
            rest(keep_two, half, 2)


def middle_kernel(size, keep_own, keep_two, taken, send, total):
    count = keep_two.shape[0]
    if keep_own.shape[0] == count:
        total[...] = keep_own[...] + taken[:count].astype(jnp.float32)
        send[...] = (keep_two[...] + taken[count:].astype(jnp.float32)).astype(bf)
        return
    half = count // 2
    for i in (0, 1):
        base, got = 2 * half * i, 3 * half * i
        first = slice(base, base + half)
        total[first] = keep_own[first] + taken[got : got + half].astype(jnp.float32)
        far = keep_two[half * i : half * i + half]
        send[first] = (far + taken[got + half : got + 2 * half].astype(jnp.float32)).astype(bf)
        for j in range(half // size):
            cut = slice(base + half + j * size, base + half + (j + 1) * size)
            at = got + 2 * half + j * size
            value = keep_own[cut] + taken[at : at + size].astype(jnp.float32)
            total[cut] = value
            at = base + half + (j ^ 2) * size
            send[at : at + size] = value.astype(bf)


def norm_rows(values, gain_row):
    wide = values.astype(jnp.float32)
    inverse_rms = lax.rsqrt(jnp.mean(wide * wide, axis=-1, keepdims=True) + epsilon)
    return (wide * inverse_rms * gain_row).astype(bf)


def key_value_kernel(half, place, total, taken, gain, out):
    keep = (total[...] + taken[...].astype(jnp.float32)).astype(bf)
    heads = gain.shape[0]
    out[:half] = norm_rows(keep[:half], gain[pl.ds(place[0], 1), :])
    out[half : 2 * half] = norm_rows(keep[half : 2 * half], gain[heads - 1 : heads, :])
    out[2 * half :] = keep[2 * half :]


def attend_kernel(half, place, total, taken, gain, own, partner, out):
    keep = (total[...] + taken[...].astype(jnp.float32)).astype(bf)
    heads = gain.shape[0]

    def attend(queries, cut):
        score_scale = 1.0 / math.sqrt(HEAD)
        totals, sums = 0.0, 0.0
        for both in (own, partner):
            scores = dot32_t(queries, both[cut]) * score_scale
            weights = jnp.exp(scores).astype(bf)
            totals = totals + jnp.sum(weights.astype(jnp.float32), axis=1, keepdims=True)
            sums = sums + dot32(weights, both[2 * half + cut.start : 2 * half + cut.stop])
        return (sums / totals).astype(bf)

    first = norm_rows(keep[:half], gain[pl.ds(place[0], 1), :])
    out[:half] = attend(first, slice(0, half))
    last = norm_rows(keep[half:], gain[heads - 1 : heads, :])
    out[half:] = attend(last, slice(half, 2 * half))


def core_kernel(own, taken, signs, kept, sent):
    for i, target in enumerate((kept, sent)):
        for j in range(kept.shape[0]):
            parts = [own[m, j, i].astype(jnp.float32) + taken[m, j, i].astype(jnp.float32) for m in (0, 1)]
            value = parts[0] + signs[j, i].astype(jnp.float32) * parts[1]
            target[j] = value.astype(target.dtype)


def team_kernel(kept, taken, *blocks):
    for j, block in enumerate(blocks):
        block[...] = (kept[j] + taken[j].astype(jnp.float32)).astype(bf)


def final_kernel(place, *refs):
    out = refs[-1]
    for k, block in enumerate(refs[:-1]):
        out[:, lanes(place[0] ^ k, block.shape[1])] = block[...]


def stationary_plan(
    tokens, in_bits, qkv_weights, qkv_bits, gain_query, gain_key, out_weights, mix_bits, out_bits
):
    groups = lax.axis_size("blk")
    team = lax.axis_size("uly")
    depth = groups // 2
    z = lax.axis_index("blk") // 2
    x = lax.axis_index("blk") % 2
    u = lax.axis_index("uly")
    own_rows, width = tokens.shape
    slab = qkv_weights.shape[2]
    columns = qkv_weights.shape[3]
    size = own_rows * team
    heads = columns // HEAD
    half = depth * size
    steps = range(depth)
    f32 = jnp.float32
    place = jnp.stack([z, x, u]).astype(jnp.int32)

    def swap_x(value):
        return lax.ppermute(value, "blk", [(i, i ^ 1) for i in range(groups)])

    def swap_z(value, step):
        return lax.ppermute(value, "blk", [(i, i ^ (2 * step)) for i in range(groups)])

    def swap_u(value, bit):
        return lax.ppermute(value, "uly", [(i, i ^ bit) for i in range(team)])

    def after(value, *earlier):
        return lax.optimization_barrier((value,) + earlier)[0]

    early = call(
        functools.partial(copy_kernel, 1, 2),
        shape(2, 2, slab, columns), ANY, [ANY], [pltpu.SemaphoreType.DMA((2,))],
    )(qkv_weights)
    partner_early = swap_x(early)

    sign_bits = jnp.transpose(qkv_bits, (1, 0, 2))
    counts = [2 + 3 * team if k == 2 else 2 for k in steps]
    blocks = call(
        functools.partial(prepare_kernel, team),
        [shape(count, own_rows, 2 * slab) for count in counts],
        [VMEM] * depth, [SMEM] + [VMEM] * 3,
    )(place, after(tokens, early), in_bits, sign_bits)
    got = [blocks[0]] + [swap_z(blocks[k], k) for k in steps if k]

    def pair(first, second):
        return call(pair_kernel, shape(2, *first.shape), VMEM, [VMEM] * 2)(first, second)

    def sign_pair(first, count):
        return call(
            functools.partial(sign_pair_kernel, first),
            shape(2, count, size, columns), VMEM, [VMEM] * 2,
        )(blocks[2], got[2])

    held_shape = (depth, 2, own_rows, 2 * slab)
    held = call(stack_kernel, shape(*held_shape), VMEM, [VMEM] * depth)(*got)
    both_pair = sign_pair(0, 2)
    both_near = swap_z(after(both_pair, held), 1)
    held = pair(held, swap_u(held, 2))
    rows = call(rows_kernel, shape(2, half, 2 * slab), VMEM, [VMEM] * 2)(
        held, swap_u(after(held, both_near), 1)
    )

    query_weights, late_own, late_near, late_far = call(
        functools.partial(late_signs_kernel, team),
        [shape(2, slab, columns)]
        + [shape(count, own_rows, 2 * slab) for count in (2, team + 2, team + 4)],
        [ANY] + [VMEM] * 3,
        [SMEM] + [VMEM] * 2 + [ANY],
        [pltpu.SemaphoreType.DMA((2,))],
    )(place, after(out_bits, blocks[0]), mix_bits, qkv_weights)
    late_far = swap_z(after(late_far, held), 2)
    query_pair = sign_pair(2, 1)
    query_near = swap_z(after(query_pair, both_near, late_far), 1)
    partner_query = swap_x(after(query_weights, partner_early, both_pair))
    out_t = jnp.transpose(out_weights, (0, 2, 1))
    out_partner = swap_x(after(out_t, partner_query))

    def project(parts, rows, partner, pair, near):
        whole = len(parts)
        count = half + size
        counts = (3 * half * whole, 2 * half * whole, half * whole)
        if parts == (0,):
            counts = (2 * count, count, count)
        return call(
            functools.partial(project_kernel, parts, size),
            [shape(counts[0], HEAD)] + [shape(count, HEAD, dtype=f32) for count in counts[1:]],
            [VMEM] * 3,
            [SMEM, VMEM, ANY, ANY] + [VMEM] * 2,
            [
                pltpu.VMEM((whole, 2, 2 * slab, columns), bf),
                pltpu.VMEM((half, columns), f32),
                pltpu.SemaphoreType.DMA((whole, 2, 2)),
            ],
        )(place, rows, qkv_weights, partner, pair, near)

    def middle(keep_own, keep_two, taken):
        count = keep_own.shape[0]
        return call(
            functools.partial(middle_kernel, size),
            [shape(count, HEAD), shape(count, HEAD, dtype=f32)],
            [VMEM] * 2,
            [VMEM] * 3,
        )(keep_own, keep_two, taken)

    both_send, both_own, both_two = project(
        (1, 2), rows, partner_early, both_pair, both_near
    )
    taken = swap_z(both_send, 1)
    query_send, query_own, query_two = project(
        (0,), after(rows, both_send), partner_query.reshape(2, 1, slab, columns),
        query_pair, query_near,
    )
    query_taken = swap_z(query_send, 1)
    send, both_total = middle(both_own, both_two, after(taken, query_send))
    both_last = swap_z(send, 2)
    send, query_total = middle(query_own, query_two, after(query_taken, both_total))
    query_last = swap_z(send, 2)
    both = call(
        functools.partial(key_value_kernel, half),
        shape(4 * half, HEAD), VMEM, [SMEM] + [VMEM] * 3,
    )(place, both_total, after(both_last, query_total), gain_key.reshape(heads, HEAD))
    both_partner = swap_x(both)
    late_got = call(near_kernel, shape(2 * team + 4, own_rows, 2 * slab), VMEM, [VMEM] * 2)(
        late_near, late_far
    )
    late_got = swap_z(after(late_got, both), 1)
    done = call(
        functools.partial(attend_kernel, half),
        shape(half + size, HEAD), VMEM, [SMEM] + [VMEM] * 5,
    )(place, query_total, query_last, gain_query.reshape(heads, HEAD), both, both_partner)

    by_head, last_head = [], []
    for k in steps:
        block = swap_z(done, k) if k else done
        main = block[:half].reshape(depth, size, HEAD)
        by_head.append(jnp.concatenate([main[j ^ k] for j in steps], axis=0))
        last_head.append(block[half:])
    attended = jnp.concatenate(by_head + [jnp.concatenate(last_head, axis=0)], axis=1)

    def relative(value, axis):
        parts = [
            lax.dynamic_slice_in_dim(value, (z ^ k) * HEAD, HEAD, axis) for k in steps
        ] + [lax.slice_in_dim(value, depth * HEAD, heads * HEAD, axis=axis)]
        return jnp.concatenate(parts, axis=axis)

    mix, out_signs = call(
        late_kernel,
        [shape(half, columns), shape(depth, 2, own_rows, 2 * slab)], [VMEM] * 2,
        [SMEM] + [VMEM] * 4,
    )(place, late_own, after(late_near, done), late_far, late_got)
    attended_flipped = attended * mix
    first = jnp.where(x == 0, out_t, out_partner)
    second = jnp.where(x == 0, out_partner, out_t)
    out_full = relative(jnp.concatenate([first, second], axis=1), 2)
    partial = jnp.stack(
        [dot32_t(attended, out_full[0]), dot32_t(attended_flipped, out_full[1])]
    ).astype(bf)
    partial = partial.reshape(2, depth, team, own_rows, 2 * slab)
    kept, sent = call(
        core_kernel,
        [shape(depth, own_rows, 2 * slab, dtype=f32), shape(depth, own_rows, 2 * slab)],
        [VMEM] * 2, [VMEM] * 3,
    )(partial[:, :, 0::2], swap_u(partial[:, :, 1::2], 1), out_signs)
    blocks = call(
        team_kernel, [shape(own_rows, 2 * slab)] * depth, [VMEM] * depth, [VMEM] * 2
    )(kept, swap_u(sent, 2))
    return call(
        final_kernel, shape(own_rows, width), VMEM, [SMEM] + [VMEM] * depth
    )(place, blocks[0], *[swap_z(blocks[k], k) for k in steps if k])


def body(*arrays):
    heads = arrays[2].shape[3] // HEAD
    depth = lax.axis_size("blk") // 2
    if depth == heads - 1 and depth == 4 and lax.axis_size("uly") == 4:
        return stationary_plan(*arrays)
    return gather_plan(*arrays)


def solution(mesh):
    return jax.shard_map(
        body,
        mesh=mesh,
        in_specs=(
            P(("blk", "uly"), None),
            P(("blk", "uly"), None),
            P(None, None, "blk", "uly"),
            P("blk", None, "uly"),
            P("uly"),
            P("uly"),
            P(None, "uly", "blk"),
            P("blk", "uly"),
            P("blk", None),
        ),
        out_specs=P(("blk", "uly"), None),
        check_vma=False,
    )
```

```python
import functools
import math

import jax
import jax.numpy as jnp
from jax import lax
from jax.experimental import pallas as pl
from jax.experimental.pallas import tpu as pltpu
from jax.sharding import PartitionSpec as P

HEAD = 128


epsilon = 1e-06


def signed(bit_values):
    return (2 * bit_values - 1).astype(jnp.float32)


def normalize(values, gain_vector):
    row_count = values.shape[0]
    by_head = values.astype(jnp.float32).reshape(row_count, -1, HEAD)
    inverse_rms = lax.rsqrt(jnp.mean(by_head * by_head, axis=-1, keepdims=True) + epsilon)
    return (by_head * inverse_rms * gain_vector.reshape(-1, HEAD)).astype(jnp.bfloat16)


def gather_plan(
    tokens, in_bits, qkv_weights, qkv_bits, gain_query, gain_key, out_weights, mix_bits, out_bits
):
    flipped = (tokens.astype(jnp.float32) * signed(in_bits)).astype(jnp.bfloat16)
    group_rows = lax.all_gather(jnp.stack([tokens, flipped]), "uly", axis=1, tiled=True)
    row_total = group_rows.shape[1]
    projections = jnp.einsum(
        "mrd,mkdc->rmkc",
        group_rows,
        lax.all_gather(qkv_weights, "blk", axis=2, tiled=True),
        preferred_element_type=jnp.float32,
    )
    projected = (projections[:, 0] + signed(qkv_bits) * projections[:, 1]).astype(jnp.bfloat16)
    queries = normalize(projected[:, 0], gain_query)
    head_count = queries.shape[1]
    keys_normed = normalize(projected[:, 1], gain_key).reshape(row_total, -1)
    values_block = projected[:, 2]
    score_scale = 1.0 / math.sqrt(HEAD)

    def attend(running, shard_piece):
        numerator, denominator = running
        key_rows = shard_piece[0].reshape(shard_piece[0].shape[0], head_count, HEAD)
        value_rows = shard_piece[1].reshape(shard_piece[1].shape[0], head_count, HEAD)
        scores = (
            jnp.einsum("rhd,nhd->hrn", queries, key_rows, preferred_element_type=jnp.float32)
            * score_scale
        )
        weights = jnp.exp(scores).astype(jnp.bfloat16)
        numerator = numerator + jnp.einsum(
            "hrn,nhd->rhd", weights, value_rows, preferred_element_type=jnp.float32
        )
        denominator = denominator + jnp.sum(weights.astype(jnp.float32), axis=2).T
        return (numerator, denominator)

    start_state = (
        jnp.zeros((row_total, head_count, HEAD), jnp.float32),
        jnp.zeros((row_total, head_count), jnp.float32),
    )
    all_keys, all_values = (
        lax.all_gather(keys_normed, "blk", axis=0, tiled=True),
        lax.all_gather(values_block, "blk", axis=0, tiled=True),
    )
    group_count = lax.axis_size("blk")
    per_block = 1
    while per_block * row_total < 512 and group_count % (per_block * 2) == 0:
        per_block = per_block * 2
    block_rows = per_block * row_total
    block_count = group_count // per_block
    key_blocks = all_keys.reshape(block_count, block_rows, all_keys.shape[1])
    value_blocks = all_values.reshape(block_count, block_rows, all_values.shape[1])

    def scan_step(running, block_pair):
        return (attend(running, block_pair), None)

    (numerator, denominator), unused = lax.scan(scan_step, start_state, (key_blocks, value_blocks))
    attended = (numerator / denominator[:, :, None]).astype(jnp.bfloat16).reshape(row_total, -1)
    attended_flipped = (attended.astype(jnp.float32) * signed(mix_bits)).astype(jnp.bfloat16)
    attended_pair = jnp.stack([attended, attended_flipped])
    out_signs = signed(out_bits)
    partial_out = jnp.einsum(
        "mrc,mcn->rmn",
        attended_pair,
        lax.all_gather(out_weights, "blk", axis=2, tiled=True),
        preferred_element_type=jnp.float32,
    )
    summed = lax.psum_scatter(
        partial_out.astype(jnp.bfloat16), "uly", scatter_dimension=0, tiled=True
    ).astype(jnp.float32)
    own_rows = summed.shape[0]
    own_signs = lax.dynamic_slice_in_dim(out_signs, lax.axis_index("uly") * own_rows, own_rows, 0)
    result_rows = summed[:, 0] + own_signs * summed[:, 1]
    return result_rows.astype(jnp.bfloat16)


def dot32(a, b):
    return lax.dot_general(
        a, b, (((1,), (0,)), ((), ())), preferred_element_type=jnp.float32
    )


def dot32_t(a, b):
    return lax.dot_general(
        a, b, (((1,), (1,)), ((), ())), preferred_element_type=jnp.float32
    )


bf = jnp.bfloat16
VMEM = pl.BlockSpec(memory_space=pltpu.VMEM)
SMEM = pl.BlockSpec(memory_space=pltpu.SMEM)
ANY = pl.BlockSpec(memory_space=pl.ANY)


def call(kernel, outs, out_specs, in_specs, scratch=(), flops=0, moved=0):
    return pl.pallas_call(
        kernel,
        out_shape=outs,
        in_specs=in_specs,
        out_specs=out_specs,
        scratch_shapes=list(scratch),
        compiler_params=pltpu.CompilerParams(vmem_limit_bytes=40 * 1024 * 1024),
        cost_estimate=pl.CostEstimate(flops=flops, bytes_accessed=moved, transcendentals=0),
    )


def shape(*dims, dtype=bf):
    return jax.ShapeDtypeStruct(dims, dtype)


def lanes(index, size):
    return pl.ds(pl.multiple_of(index * size, 128), size)


def copy_kernel(first, count, weights, out, sems):
    copies = [
        pltpu.make_async_copy(weights.at[m, pl.ds(first, count)], out.at[m], sems.at[m])
        for m in (0, 1)
    ]
    for copy in copies:
        copy.start()
    for copy in copies:
        copy.wait()


def sign_pieces(bits, u, team):
    piece = bits.shape[0] // team
    parts = [bits[pl.ds(pl.multiple_of((u ^ r) * piece, 8), piece), :] for r in range(team)]
    return [(2 * part - 1).astype(jnp.float32) for part in parts]


def prepare_kernel(team, place, tokens, in_bits, sign_bits, *blocks):
    wide = tokens.shape[1] // len(blocks)
    for k, block in enumerate(blocks):
        cut = lanes(place[0] ^ k, wide)
        plain = tokens[:, cut]
        sign = (2 * in_bits[:, cut] - 1).astype(jnp.float32)
        block[0] = plain
        block[1] = (plain.astype(jnp.float32) * sign).astype(bf)
    for i, part in enumerate((1, 2, 0)):
        for r, piece in enumerate(sign_pieces(sign_bits.at[part], place[2], team)):
            blocks[2][2 + team * i + r] = piece.astype(bf)


def late_signs_kernel(team, place, out_bits, mix_bits, weights, query_weights, out, near, far, sems):
    copies = [
        pltpu.make_async_copy(weights.at[m, 0], query_weights.at[m], sems.at[m]) for m in (0, 1)
    ]
    for copy in copies:
        copy.start()
    z, u = place[0], place[2]
    own_rows, wide = out.shape[1:]

    def fill(target, start, k):
        for i, r in enumerate((0, 2)):
            rows = pl.ds(pl.multiple_of((u ^ r) * own_rows, 8), own_rows)
            bits = out_bits[rows, lanes(z ^ k, wide)]
            target[start + i] = (2 * bits - 1).astype(jnp.float32).astype(bf)

    fill(out, 0, 0)
    for r, part in enumerate(sign_pieces(mix_bits, u, team)):
        near[r] = part.astype(bf)
        far[r] = part.astype(bf)
    fill(near, team, 1)
    fill(far, team, 2)
    fill(far, team + 2, 3)
    for copy in copies:
        copy.wait()


def near_kernel(near, far, out):
    team = near.shape[0] - 2
    out[:team] = near[:team]
    out[team : 2 * team] = far[:team]
    out[2 * team : 2 * team + 2] = near[team:]
    out[2 * team + 2 :] = far[team + 2 :]


def late_kernel(place, own, near, far, got, mix, out):
    team, own_rows = near.shape[0] - 2, near.shape[1]
    size = team * own_rows
    out[0] = own[...]
    out[1] = got[2 * team : 2 * team + 2]
    out[2] = far[team : team + 2]
    out[3] = got[2 * team + 2 :]
    for j, (ref, start) in enumerate(((near, 0), (got, 0), (far, 0), (got, team))):
        cut = slice(j * size, (j + 1) * size)
        for k in range(5):
            head = lanes(place[0] ^ k, HEAD) if k < 4 else slice(4 * HEAD, None)
            parts = [ref[start + r, :, head].astype(jnp.float32) for r in range(team)]
            mix[cut, k * HEAD : (k + 1) * HEAD] = jnp.concatenate(parts, axis=0).astype(bf)


def stack_kernel(*refs):
    for k, ref in enumerate(refs[:-1]):
        refs[-1][k] = ref[: refs[-1].shape[1]]


def pair_kernel(own, taken, out):
    out[0] = own[...]
    out[1] = taken[...]


def sign_pair_kernel(own, taken, out):
    team = (own.shape[0] - 2) // 3
    for b, ref in enumerate((own, taken)):
        for i in range(3):
            pieces = [ref[2 + team * i + r].astype(jnp.float32) for r in range(team)]
            out[b, i] = jnp.concatenate(pieces, axis=0).astype(bf)


def rows_kernel(own, taken, rows):
    depth, kinds, piece = own.shape[1:4]
    for m in range(kinds):
        for j in range(depth):
            parts = [ref[y, j, m].astype(jnp.float32) for y in (0, 1) for ref in (own, taken)]
            at = j * 4 * piece
            rows[m, at : at + 4 * piece] = jnp.concatenate(parts, axis=0).astype(bf)


def project_kernel(
    parts, size, place, rows, weights, partner, signs_02, signs_13,
    send, keep_own, keep_two, held, total, sems,
):
    z, x = place[0], place[1]
    slab = weights.shape[2]
    own = pl.ds(pl.multiple_of(x * slab, 64), slab)
    other = pl.ds(pl.multiple_of((1 - x) * slab, 64), slab)
    depth = rows.shape[1] // size
    half = depth * size
    copies = []
    for i, part in enumerate(parts):
        for m in (0, 1):
            near, far = weights.at[m, part], partner.at[m, i]
            copies.append(pltpu.make_async_copy(near, held.at[i, m, own], sems.at[i, m, 0]))
            copies.append(pltpu.make_async_copy(far, held.at[i, m, other], sems.at[i, m, 1]))
    for copy in copies:
        copy.start()

    def block(j, head):
        return total[j * size : (j + 1) * size, lanes(head, HEAD)]

    def main(target, start, k):
        for j in range(depth):
            at = start + (j ^ k) * size
            target[at : at + size] = block(j, z ^ k).astype(target.dtype)

    def rest(target, start, j):
        target[start : start + size] = block(j, depth).astype(target.dtype)

    for i, part in enumerate(parts):
        for copy in copies[4 * i : 4 * i + 4]:
            copy.wait()
        total[...] = dot32(rows[1], held[i, 1])
        plain = dot32(rows[0], held[i, 0])
        at = part - 1 if part else 2
        signs = (signs_02[0, at], signs_13[0, at], signs_02[1, at], signs_13[1, at])
        for j in range(depth):
            cut = slice(j * size, (j + 1) * size)
            total[cut] = plain[cut] + signs[j].astype(jnp.float32) * total[cut]
        if part:
            main(send, 3 * half * i, 1)
            main(send, 3 * half * i + half, 3)
            main(keep_own, 2 * half * i, 0)
            main(keep_two, half * i, 2)
            for j in range(depth):
                rest(send, 3 * half * i + 2 * half + (j ^ 1) * size, j)
                rest(keep_own, 2 * half * i + half + j * size, j)
        else:
            main(send, 0, 1)
            rest(send, half, 1)
            main(send, half + size, 3)
            rest(send, 2 * half + size, 3)
            main(keep_own, 0, 0)
            rest(keep_own, half, 0)
            main(keep_two, 0, 2)
            rest(keep_two, half, 2)


def middle_kernel(size, keep_own, keep_two, taken, send, total):
    count = keep_two.shape[0]
    if keep_own.shape[0] == count:
        total[...] = keep_own[...] + taken[:count].astype(jnp.float32)
        send[...] = (keep_two[...] + taken[count:].astype(jnp.float32)).astype(bf)
        return
    half = count // 2
    for i in (0, 1):
        base, got = 2 * half * i, 3 * half * i
        first = slice(base, base + half)
        total[first] = keep_own[first] + taken[got : got + half].astype(jnp.float32)
        far = keep_two[half * i : half * i + half]
        send[first] = (far + taken[got + half : got + 2 * half].astype(jnp.float32)).astype(bf)
        for j in range(half // size):
            cut = slice(base + half + j * size, base + half + (j + 1) * size)
            at = got + 2 * half + j * size
            value = keep_own[cut] + taken[at : at + size].astype(jnp.float32)
            total[cut] = value
            at = base + half + (j ^ 2) * size
            send[at : at + size] = value.astype(bf)


def norm_rows(values, gain_row):
    wide = values.astype(jnp.float32)
    inverse_rms = lax.rsqrt(jnp.mean(wide * wide, axis=-1, keepdims=True) + epsilon)
    return (wide * inverse_rms * gain_row).astype(bf)


def key_value_kernel(half, place, total, taken, gain, out):
    keep = (total[...] + taken[...].astype(jnp.float32)).astype(bf)
    heads = gain.shape[0]
    out[:half] = norm_rows(keep[:half], gain[pl.ds(place[0], 1), :])
    out[half : 2 * half] = norm_rows(keep[half : 2 * half], gain[heads - 1 : heads, :])
    out[2 * half :] = keep[2 * half :]


def attend_kernel(half, place, total, taken, gain, own, partner, out):
    keep = (total[...] + taken[...].astype(jnp.float32)).astype(bf)
    heads = gain.shape[0]

    def attend(queries, cut):
        score_scale = 1.0 / math.sqrt(HEAD)
        totals, sums = 0.0, 0.0
        for both in (own, partner):
            scores = dot32_t(queries, both[cut]) * score_scale
            weights = jnp.exp(scores).astype(bf)
            totals = totals + jnp.sum(weights.astype(jnp.float32), axis=1, keepdims=True)
            sums = sums + dot32(weights, both[2 * half + cut.start : 2 * half + cut.stop])
        return (sums / totals).astype(bf)

    first = norm_rows(keep[:half], gain[pl.ds(place[0], 1), :])
    out[:half] = attend(first, slice(0, half))
    last = norm_rows(keep[half:], gain[heads - 1 : heads, :])
    out[half:] = attend(last, slice(half, 2 * half))


def core_kernel(own, taken, signs, kept, sent):
    for i, target in enumerate((kept, sent)):
        for j in range(kept.shape[0]):
            parts = [own[m, j, i].astype(jnp.float32) + taken[m, j, i].astype(jnp.float32) for m in (0, 1)]
            value = parts[0] + signs[j, i].astype(jnp.float32) * parts[1]
            target[j] = value.astype(target.dtype)


def team_kernel(kept, taken, *blocks):
    for j, block in enumerate(blocks):
        block[...] = (kept[j] + taken[j].astype(jnp.float32)).astype(bf)


def final_kernel(place, *refs):
    out = refs[-1]
    for k, block in enumerate(refs[:-1]):
        out[:, lanes(place[0] ^ k, block.shape[1])] = block[...]


def stationary_plan(
    tokens, in_bits, qkv_weights, qkv_bits, gain_query, gain_key, out_weights, mix_bits, out_bits
):
    groups = lax.axis_size("blk")
    team = lax.axis_size("uly")
    depth = groups // 2
    z = lax.axis_index("blk") // 2
    x = lax.axis_index("blk") % 2
    u = lax.axis_index("uly")
    own_rows, width = tokens.shape
    slab = qkv_weights.shape[2]
    columns = qkv_weights.shape[3]
    size = own_rows * team
    heads = columns // HEAD
    half = depth * size
    steps = range(depth)
    f32 = jnp.float32
    place = jnp.stack([z, x, u]).astype(jnp.int32)

    def swap_x(value):
        return lax.ppermute(value, "blk", [(i, i ^ 1) for i in range(groups)])

    def swap_z(value, step):
        return lax.ppermute(value, "blk", [(i, i ^ (2 * step)) for i in range(groups)])

    def swap_u(value, bit):
        return lax.ppermute(value, "uly", [(i, i ^ bit) for i in range(team)])

    def after(value, *earlier):
        return lax.optimization_barrier((value,) + earlier)[0]

    early = call(
        functools.partial(copy_kernel, 1, 2),
        shape(2, 2, slab, columns), ANY, [ANY], [pltpu.SemaphoreType.DMA((2,))],
    )(qkv_weights)
    partner_early = swap_x(early)

    sign_bits = jnp.transpose(qkv_bits, (1, 0, 2))
    counts = [2 + 3 * team if k == 2 else 2 for k in steps]
    blocks = call(
        functools.partial(prepare_kernel, team),
        [shape(count, own_rows, 2 * slab) for count in counts],
        [VMEM] * depth, [SMEM] + [VMEM] * 3,
    )(place, after(tokens, early), in_bits, sign_bits)
    got = [blocks[0]] + [swap_z(blocks[k], k) for k in steps if k]

    def pair(first, second):
        return call(pair_kernel, shape(2, *first.shape), VMEM, [VMEM] * 2)(first, second)

    held_shape = (depth, 2, own_rows, 2 * slab)
    held = call(stack_kernel, shape(*held_shape), VMEM, [VMEM] * depth)(*got)
    signs = call(sign_pair_kernel, shape(2, 3, size, columns), VMEM, [VMEM] * 2)(
        blocks[2], got[2]
    )
    signs_near = swap_z(after(signs, held), 1)
    held = pair(held, swap_u(held, 2))
    rows = call(rows_kernel, shape(2, half, 2 * slab), VMEM, [VMEM] * 2)(
        held, swap_u(held, 1)
    )

    query_weights, late_own, late_near, late_far = call(
        functools.partial(late_signs_kernel, team),
        [shape(2, slab, columns)]
        + [shape(count, own_rows, 2 * slab) for count in (2, team + 2, team + 4)],
        [ANY] + [VMEM] * 3,
        [SMEM] + [VMEM] * 2 + [ANY],
        [pltpu.SemaphoreType.DMA((2,))],
    )(place, after(out_bits, blocks[0]), mix_bits, qkv_weights)
    late_far = swap_z(after(late_far, held), 2)
    partner_query = swap_x(after(query_weights, partner_early, rows, signs))
    out_t = jnp.transpose(out_weights, (0, 2, 1))
    out_partner = swap_x(after(out_t, partner_query))

    def project(parts, rows, partner):
        whole = len(parts)
        count = half + size
        counts = (3 * half * whole, 2 * half * whole, half * whole)
        if parts == (0,):
            counts = (2 * count, count, count)
        return call(
            functools.partial(project_kernel, parts, size),
            [shape(counts[0], HEAD)] + [shape(count, HEAD, dtype=f32) for count in counts[1:]],
            [VMEM] * 3,
            [SMEM, VMEM, ANY, ANY] + [VMEM] * 2,
            [
                pltpu.VMEM((whole, 2, 2 * slab, columns), bf),
                pltpu.VMEM((half, columns), f32),
                pltpu.SemaphoreType.DMA((whole, 2, 2)),
            ],
        )(place, rows, qkv_weights, partner, signs, signs_near)

    def middle(keep_own, keep_two, taken):
        count = keep_own.shape[0]
        return call(
            functools.partial(middle_kernel, size),
            [shape(count, HEAD), shape(count, HEAD, dtype=f32)],
            [VMEM] * 2,
            [VMEM] * 3,
        )(keep_own, keep_two, taken)

    both_send, both_own, both_two = project(
        (1, 2), rows, partner_early
    )
    taken = swap_z(both_send, 1)
    query_send, query_own, query_two = project(
        (0,), after(rows, both_send), partner_query.reshape(2, 1, slab, columns),
    )
    query_taken = swap_z(query_send, 1)
    send, both_total = middle(both_own, both_two, after(taken, query_send, late_far))
    both_last = swap_z(send, 2)
    send, query_total = middle(query_own, query_two, after(query_taken, both_total))
    query_last = swap_z(send, 2)
    both = call(
        functools.partial(key_value_kernel, half),
        shape(4 * half, HEAD), VMEM, [SMEM] + [VMEM] * 3,
    )(place, both_total, after(both_last, query_total), gain_key.reshape(heads, HEAD))
    both_partner = swap_x(both)
    late_got = call(near_kernel, shape(2 * team + 4, own_rows, 2 * slab), VMEM, [VMEM] * 2)(
        late_near, late_far
    )
    late_got = swap_z(after(late_got, both), 1)
    done = call(
        functools.partial(attend_kernel, half),
        shape(half + size, HEAD), VMEM, [SMEM] + [VMEM] * 5,
    )(place, query_total, query_last, gain_query.reshape(heads, HEAD), both, both_partner)

    by_head, last_head = [], []
    for k in steps:
        block = swap_z(done, k) if k else done
        main = block[:half].reshape(depth, size, HEAD)
        by_head.append(jnp.concatenate([main[j ^ k] for j in steps], axis=0))
        last_head.append(block[half:])
    attended = jnp.concatenate(by_head + [jnp.concatenate(last_head, axis=0)], axis=1)

    def relative(value, axis):
        parts = [
            lax.dynamic_slice_in_dim(value, (z ^ k) * HEAD, HEAD, axis) for k in steps
        ] + [lax.slice_in_dim(value, depth * HEAD, heads * HEAD, axis=axis)]
        return jnp.concatenate(parts, axis=axis)

    mix, out_signs = call(
        late_kernel,
        [shape(half, columns), shape(depth, 2, own_rows, 2 * slab)], [VMEM] * 2,
        [SMEM] + [VMEM] * 4,
    )(place, late_own, after(late_near, done), late_far, late_got)
    attended_flipped = attended * mix
    first = jnp.where(x == 0, out_t, out_partner)
    second = jnp.where(x == 0, out_partner, out_t)
    out_full = relative(jnp.concatenate([first, second], axis=1), 2)
    partial = jnp.stack(
        [dot32_t(attended, out_full[0]), dot32_t(attended_flipped, out_full[1])]
    ).astype(bf)
    partial = partial.reshape(2, depth, team, own_rows, 2 * slab)
    kept, sent = call(
        core_kernel,
        [shape(depth, own_rows, 2 * slab, dtype=f32), shape(depth, own_rows, 2 * slab)],
        [VMEM] * 2, [VMEM] * 3,
    )(partial[:, :, 0::2], swap_u(partial[:, :, 1::2], 1), out_signs)
    blocks = call(
        team_kernel, [shape(own_rows, 2 * slab)] * depth, [VMEM] * depth, [VMEM] * 2
    )(kept, swap_u(sent, 2))
    return call(
        final_kernel, shape(own_rows, width), VMEM, [SMEM] + [VMEM] * depth
    )(place, blocks[0], *[swap_z(blocks[k], k) for k in steps if k])


def body(*arrays):
    heads = arrays[2].shape[3] // HEAD
    depth = lax.axis_size("blk") // 2
    if depth == heads - 1 and depth == 4 and lax.axis_size("uly") == 4:
        return stationary_plan(*arrays)
    return gather_plan(*arrays)


def solution(mesh):
    return jax.shard_map(
        body,
        mesh=mesh,
        in_specs=(
            P(("blk", "uly"), None),
            P(("blk", "uly"), None),
            P(None, None, "blk", "uly"),
            P("blk", None, "uly"),
            P("uly"),
            P("uly"),
            P(None, "uly", "blk"),
            P("blk", "uly"),
            P("blk", None),
        ),
        out_specs=P(("blk", "uly"), None),
        check_vma=False,
    )
```

```python
import functools
import math

import jax
import jax.numpy as jnp
from jax import lax
from jax.experimental import pallas as pl
from jax.experimental.pallas import tpu as pltpu
from jax.sharding import PartitionSpec as P

HEAD = 128


epsilon = 1e-06


def signed(bit_values):
    return (2 * bit_values - 1).astype(jnp.float32)


def normalize(values, gain_vector):
    row_count = values.shape[0]
    by_head = values.astype(jnp.float32).reshape(row_count, -1, HEAD)
    inverse_rms = lax.rsqrt(jnp.mean(by_head * by_head, axis=-1, keepdims=True) + epsilon)
    return (by_head * inverse_rms * gain_vector.reshape(-1, HEAD)).astype(jnp.bfloat16)


def gather_plan(
    tokens, in_bits, qkv_weights, qkv_bits, gain_query, gain_key, out_weights, mix_bits, out_bits
):
    flipped = (tokens.astype(jnp.float32) * signed(in_bits)).astype(jnp.bfloat16)
    group_rows = lax.all_gather(jnp.stack([tokens, flipped]), "uly", axis=1, tiled=True)
    row_total = group_rows.shape[1]
    projections = jnp.einsum(
        "mrd,mkdc->rmkc",
        group_rows,
        lax.all_gather(qkv_weights, "blk", axis=2, tiled=True),
        preferred_element_type=jnp.float32,
    )
    projected = (projections[:, 0] + signed(qkv_bits) * projections[:, 1]).astype(jnp.bfloat16)
    queries = normalize(projected[:, 0], gain_query)
    head_count = queries.shape[1]
    keys_normed = normalize(projected[:, 1], gain_key).reshape(row_total, -1)
    values_block = projected[:, 2]
    score_scale = 1.0 / math.sqrt(HEAD)

    def attend(running, shard_piece):
        numerator, denominator = running
        key_rows = shard_piece[0].reshape(shard_piece[0].shape[0], head_count, HEAD)
        value_rows = shard_piece[1].reshape(shard_piece[1].shape[0], head_count, HEAD)
        scores = (
            jnp.einsum("rhd,nhd->hrn", queries, key_rows, preferred_element_type=jnp.float32)
            * score_scale
        )
        weights = jnp.exp(scores).astype(jnp.bfloat16)
        numerator = numerator + jnp.einsum(
            "hrn,nhd->rhd", weights, value_rows, preferred_element_type=jnp.float32
        )
        denominator = denominator + jnp.sum(weights.astype(jnp.float32), axis=2).T
        return (numerator, denominator)

    start_state = (
        jnp.zeros((row_total, head_count, HEAD), jnp.float32),
        jnp.zeros((row_total, head_count), jnp.float32),
    )
    all_keys, all_values = (
        lax.all_gather(keys_normed, "blk", axis=0, tiled=True),
        lax.all_gather(values_block, "blk", axis=0, tiled=True),
    )
    group_count = lax.axis_size("blk")
    per_block = 1
    while per_block * row_total < 512 and group_count % (per_block * 2) == 0:
        per_block = per_block * 2
    block_rows = per_block * row_total
    block_count = group_count // per_block
    key_blocks = all_keys.reshape(block_count, block_rows, all_keys.shape[1])
    value_blocks = all_values.reshape(block_count, block_rows, all_values.shape[1])

    def scan_step(running, block_pair):
        return (attend(running, block_pair), None)

    (numerator, denominator), unused = lax.scan(scan_step, start_state, (key_blocks, value_blocks))
    attended = (numerator / denominator[:, :, None]).astype(jnp.bfloat16).reshape(row_total, -1)
    attended_flipped = (attended.astype(jnp.float32) * signed(mix_bits)).astype(jnp.bfloat16)
    attended_pair = jnp.stack([attended, attended_flipped])
    out_signs = signed(out_bits)
    partial_out = jnp.einsum(
        "mrc,mcn->rmn",
        attended_pair,
        lax.all_gather(out_weights, "blk", axis=2, tiled=True),
        preferred_element_type=jnp.float32,
    )
    summed = lax.psum_scatter(
        partial_out.astype(jnp.bfloat16), "uly", scatter_dimension=0, tiled=True
    ).astype(jnp.float32)
    own_rows = summed.shape[0]
    own_signs = lax.dynamic_slice_in_dim(out_signs, lax.axis_index("uly") * own_rows, own_rows, 0)
    result_rows = summed[:, 0] + own_signs * summed[:, 1]
    return result_rows.astype(jnp.bfloat16)


def dot32(a, b):
    return lax.dot_general(
        a, b, (((1,), (0,)), ((), ())), preferred_element_type=jnp.float32
    )


def dot32_t(a, b):
    return lax.dot_general(
        a, b, (((1,), (1,)), ((), ())), preferred_element_type=jnp.float32
    )


bf = jnp.bfloat16
VMEM = pl.BlockSpec(memory_space=pltpu.VMEM)
SMEM = pl.BlockSpec(memory_space=pltpu.SMEM)
ANY = pl.BlockSpec(memory_space=pl.ANY)


def call(kernel, outs, out_specs, in_specs, scratch=(), flops=0, moved=0):
    return pl.pallas_call(
        kernel,
        out_shape=outs,
        in_specs=in_specs,
        out_specs=out_specs,
        scratch_shapes=list(scratch),
        compiler_params=pltpu.CompilerParams(vmem_limit_bytes=40 * 1024 * 1024),
        cost_estimate=pl.CostEstimate(flops=flops, bytes_accessed=moved, transcendentals=0),
    )


def shape(*dims, dtype=bf):
    return jax.ShapeDtypeStruct(dims, dtype)


def lanes(index, size):
    return pl.ds(pl.multiple_of(index * size, 128), size)


def copy_kernel(first, count, weights, out, sems):
    copies = [
        pltpu.make_async_copy(weights.at[m, pl.ds(first, count)], out.at[m], sems.at[m])
        for m in (0, 1)
    ]
    for copy in copies:
        copy.start()
    for copy in copies:
        copy.wait()


def sign_pieces(bits, u, team):
    piece = bits.shape[0] // team
    parts = [bits[pl.ds(pl.multiple_of((u ^ r) * piece, 8), piece), :] for r in range(team)]
    return [(2 * part - 1).astype(jnp.float32) for part in parts]


def prepare_kernel(team, place, tokens, in_bits, sign_bits, *blocks):
    wide = tokens.shape[1] // len(blocks)
    for k, block in enumerate(blocks):
        cut = lanes(place[0] ^ k, wide)
        plain = tokens[:, cut]
        sign = (2 * in_bits[:, cut] - 1).astype(jnp.float32)
        block[0] = plain
        block[1] = (plain.astype(jnp.float32) * sign).astype(bf)
    for i, part in enumerate((1, 2, 0)):
        for r, piece in enumerate(sign_pieces(sign_bits.at[part], place[2], team)):
            for block in blocks[1:3]:
                block[2 + team * i + r] = piece.astype(bf)


def late_signs_kernel(team, place, out_bits, mix_bits, weights, query_weights, out, near, far, sems):
    copies = [
        pltpu.make_async_copy(weights.at[m, 0], query_weights.at[m], sems.at[m]) for m in (0, 1)
    ]
    for copy in copies:
        copy.start()
    z, u = place[0], place[2]
    own_rows, wide = out.shape[1:]

    def fill(target, start, k):
        for i, r in enumerate((0, 2)):
            rows = pl.ds(pl.multiple_of((u ^ r) * own_rows, 8), own_rows)
            bits = out_bits[rows, lanes(z ^ k, wide)]
            target[start + i] = (2 * bits - 1).astype(jnp.float32).astype(bf)

    fill(out, 0, 0)
    for r, part in enumerate(sign_pieces(mix_bits, u, team)):
        near[r] = part.astype(bf)
        far[r] = part.astype(bf)
    fill(near, team, 1)
    fill(far, team, 2)
    fill(far, team + 2, 3)
    for copy in copies:
        copy.wait()


def near_kernel(near, far, out):
    team = near.shape[0] - 2
    out[:team] = near[:team]
    out[team : 2 * team] = far[:team]
    out[2 * team : 2 * team + 2] = near[team:]
    out[2 * team + 2 :] = far[team + 2 :]


def late_kernel(place, own, near, far, got, mix, out):
    team, own_rows = near.shape[0] - 2, near.shape[1]
    size = team * own_rows
    out[0] = own[...]
    out[1] = got[2 * team : 2 * team + 2]
    out[2] = far[team : team + 2]
    out[3] = got[2 * team + 2 :]
    for j, (ref, start) in enumerate(((near, 0), (got, 0), (far, 0), (got, team))):
        cut = slice(j * size, (j + 1) * size)
        for k in range(5):
            head = lanes(place[0] ^ k, HEAD) if k < 4 else slice(4 * HEAD, None)
            parts = [ref[start + r, :, head].astype(jnp.float32) for r in range(team)]
            mix[cut, k * HEAD : (k + 1) * HEAD] = jnp.concatenate(parts, axis=0).astype(bf)


def stack_kernel(*refs):
    for k, ref in enumerate(refs[:-1]):
        refs[-1][k] = ref[: refs[-1].shape[1]]


def pair_kernel(own, taken, out):
    out[0] = own[...]
    out[1] = taken[...]


def forward_kernel(taken, out):
    out[...] = taken[taken.shape[0] - out.shape[0] :]


def rows_kernel(own, taken, rows):
    depth, kinds, piece = own.shape[1:4]
    for m in range(kinds):
        for j in range(depth):
            parts = [ref[y, j, m].astype(jnp.float32) for y in (0, 1) for ref in (own, taken)]
            at = j * 4 * piece
            rows[m, at : at + 4 * piece] = jnp.concatenate(parts, axis=0).astype(bf)


def project_kernel(
    parts, size, place, rows, weights, partner, signs_0, signs_1, signs_2, signs_3,
    send, keep_own, keep_two, held, total, sems,
):
    z, x = place[0], place[1]
    slab = weights.shape[2]
    own = pl.ds(pl.multiple_of(x * slab, 64), slab)
    other = pl.ds(pl.multiple_of((1 - x) * slab, 64), slab)
    depth = rows.shape[1] // size
    half = depth * size
    copies = []
    for i, part in enumerate(parts):
        for m in (0, 1):
            near, far = weights.at[m, part], partner.at[m, i]
            copies.append(pltpu.make_async_copy(near, held.at[i, m, own], sems.at[i, m, 0]))
            copies.append(pltpu.make_async_copy(far, held.at[i, m, other], sems.at[i, m, 1]))
    for copy in copies:
        copy.start()

    def block(j, head):
        return total[j * size : (j + 1) * size, lanes(head, HEAD)]

    def main(target, start, k):
        for j in range(depth):
            at = start + (j ^ k) * size
            target[at : at + size] = block(j, z ^ k).astype(target.dtype)

    def rest(target, start, j):
        target[start : start + size] = block(j, depth).astype(target.dtype)

    for i, part in enumerate(parts):
        for copy in copies[4 * i : 4 * i + 4]:
            copy.wait()
        total[...] = dot32(rows[1], held[i, 1])
        plain = dot32(rows[0], held[i, 0])
        at = part - 1 if part else 2
        team = signs_3.shape[0] // 3
        for j in range(depth):
            cut = slice(j * size, (j + 1) * size)
            ref = (signs_0, signs_1, signs_2, signs_3)[j]
            start = ref.shape[0] - (3 - at) * team
            pieces = [ref[start + r].astype(jnp.float32) for r in range(team)]
            total[cut] = plain[cut] + jnp.concatenate(pieces, axis=0) * total[cut]
        if part:
            main(send, 3 * half * i, 1)
            main(send, 3 * half * i + half, 3)
            main(keep_own, 2 * half * i, 0)
            main(keep_two, half * i, 2)
            for j in range(depth):
                rest(send, 3 * half * i + 2 * half + (j ^ 1) * size, j)
                rest(keep_own, 2 * half * i + half + j * size, j)
        else:
            main(send, 0, 1)
            rest(send, half, 1)
            main(send, half + size, 3)
            rest(send, 2 * half + size, 3)
            main(keep_own, 0, 0)
            rest(keep_own, half, 0)
            main(keep_two, 0, 2)
            rest(keep_two, half, 2)


def middle_kernel(size, keep_own, keep_two, taken, send, total):
    count = keep_two.shape[0]
    if keep_own.shape[0] == count:
        total[...] = keep_own[...] + taken[:count].astype(jnp.float32)
        send[...] = (keep_two[...] + taken[count:].astype(jnp.float32)).astype(bf)
        return
    half = count // 2
    for i in (0, 1):
        base, got = 2 * half * i, 3 * half * i
        first = slice(base, base + half)
        total[first] = keep_own[first] + taken[got : got + half].astype(jnp.float32)
        far = keep_two[half * i : half * i + half]
        send[first] = (far + taken[got + half : got + 2 * half].astype(jnp.float32)).astype(bf)
        for j in range(half // size):
            cut = slice(base + half + j * size, base + half + (j + 1) * size)
            at = got + 2 * half + j * size
            value = keep_own[cut] + taken[at : at + size].astype(jnp.float32)
            total[cut] = value
            at = base + half + (j ^ 2) * size
            send[at : at + size] = value.astype(bf)


def norm_rows(values, gain_row):
    wide = values.astype(jnp.float32)
    inverse_rms = lax.rsqrt(jnp.mean(wide * wide, axis=-1, keepdims=True) + epsilon)
    return (wide * inverse_rms * gain_row).astype(bf)


def key_value_kernel(half, place, total, taken, gain, out):
    keep = (total[...] + taken[...].astype(jnp.float32)).astype(bf)
    heads = gain.shape[0]
    out[:half] = norm_rows(keep[:half], gain[pl.ds(place[0], 1), :])
    out[half : 2 * half] = norm_rows(keep[half : 2 * half], gain[heads - 1 : heads, :])
    out[2 * half :] = keep[2 * half :]


def attend_kernel(half, place, total, taken, gain, own, partner, out):
    keep = (total[...] + taken[...].astype(jnp.float32)).astype(bf)
    heads = gain.shape[0]

    def attend(queries, cut):
        score_scale = 1.0 / math.sqrt(HEAD)
        totals, sums = 0.0, 0.0
        for both in (own, partner):
            scores = dot32_t(queries, both[cut]) * score_scale
            weights = jnp.exp(scores).astype(bf)
            totals = totals + jnp.sum(weights.astype(jnp.float32), axis=1, keepdims=True)
            sums = sums + dot32(weights, both[2 * half + cut.start : 2 * half + cut.stop])
        return (sums / totals).astype(bf)

    first = norm_rows(keep[:half], gain[pl.ds(place[0], 1), :])
    out[:half] = attend(first, slice(0, half))
    last = norm_rows(keep[half:], gain[heads - 1 : heads, :])
    out[half:] = attend(last, slice(half, 2 * half))


def core_kernel(own, taken, signs, kept, sent):
    for i, target in enumerate((kept, sent)):
        for j in range(kept.shape[0]):
            parts = [own[m, j, i].astype(jnp.float32) + taken[m, j, i].astype(jnp.float32) for m in (0, 1)]
            value = parts[0] + signs[j, i].astype(jnp.float32) * parts[1]
            target[j] = value.astype(target.dtype)


def team_kernel(kept, taken, *blocks):
    for j, block in enumerate(blocks):
        block[...] = (kept[j] + taken[j].astype(jnp.float32)).astype(bf)


def final_kernel(place, *refs):
    out = refs[-1]
    for k, block in enumerate(refs[:-1]):
        out[:, lanes(place[0] ^ k, block.shape[1])] = block[...]


def stationary_plan(
    tokens, in_bits, qkv_weights, qkv_bits, gain_query, gain_key, out_weights, mix_bits, out_bits
):
    groups = lax.axis_size("blk")
    team = lax.axis_size("uly")
    depth = groups // 2
    z = lax.axis_index("blk") // 2
    x = lax.axis_index("blk") % 2
    u = lax.axis_index("uly")
    own_rows, width = tokens.shape
    slab = qkv_weights.shape[2]
    columns = qkv_weights.shape[3]
    size = own_rows * team
    heads = columns // HEAD
    half = depth * size
    steps = range(depth)
    f32 = jnp.float32
    place = jnp.stack([z, x, u]).astype(jnp.int32)

    def swap_x(value):
        return lax.ppermute(value, "blk", [(i, i ^ 1) for i in range(groups)])

    def swap_z(value, step):
        return lax.ppermute(value, "blk", [(i, i ^ (2 * step)) for i in range(groups)])

    def swap_u(value, bit):
        return lax.ppermute(value, "uly", [(i, i ^ bit) for i in range(team)])

    def after(value, *earlier):
        return lax.optimization_barrier((value,) + earlier)[0]

    early = call(
        functools.partial(copy_kernel, 1, 2),
        shape(2, 2, slab, columns), ANY, [ANY], [pltpu.SemaphoreType.DMA((2,))],
    )(qkv_weights)
    partner_early = swap_x(early)

    sign_bits = jnp.transpose(qkv_bits, (1, 0, 2))
    counts = [2 + 3 * team if k in (1, 2) else 2 for k in steps]
    blocks = call(
        functools.partial(prepare_kernel, team),
        [shape(count, own_rows, 2 * slab) for count in counts],
        [VMEM] * depth, [SMEM] + [VMEM] * 3,
    )(place, after(tokens, early), in_bits, sign_bits)
    got = [blocks[0]] + [swap_z(blocks[k], k) for k in steps if k]

    def pair(first, second):
        return call(pair_kernel, shape(2, *first.shape), VMEM, [VMEM] * 2)(first, second)

    held_shape = (depth, 2, own_rows, 2 * slab)
    held = call(stack_kernel, shape(*held_shape), VMEM, [VMEM] * depth)(*got)
    forward = call(forward_kernel, shape(3 * team, own_rows, columns), VMEM, [VMEM])(got[2])
    signs = (blocks[2], got[1], got[2], swap_z(after(forward, held), 1))
    held = pair(held, swap_u(held, 2))
    rows = call(rows_kernel, shape(2, half, 2 * slab), VMEM, [VMEM] * 2)(
        held, swap_u(after(held, signs[3]), 1)
    )

    query_weights, late_own, late_near, late_far = call(
        functools.partial(late_signs_kernel, team),
        [shape(2, slab, columns)]
        + [shape(count, own_rows, 2 * slab) for count in (2, team + 2, team + 4)],
        [ANY] + [VMEM] * 3,
        [SMEM] + [VMEM] * 2 + [ANY],
        [pltpu.SemaphoreType.DMA((2,))],
    )(place, after(out_bits, blocks[0]), mix_bits, qkv_weights)
    late_far = swap_z(after(late_far, held), 2)
    partner_query = swap_x(after(query_weights, partner_early, forward))
    out_t = jnp.transpose(out_weights, (0, 2, 1))
    out_partner = swap_x(after(out_t, partner_query))

    def project(parts, rows, partner):
        whole = len(parts)
        count = half + size
        counts = (3 * half * whole, 2 * half * whole, half * whole)
        if parts == (0,):
            counts = (2 * count, count, count)
        return call(
            functools.partial(project_kernel, parts, size),
            [shape(counts[0], HEAD)] + [shape(count, HEAD, dtype=f32) for count in counts[1:]],
            [VMEM] * 3,
            [SMEM, VMEM, ANY, ANY] + [VMEM] * 4,
            [
                pltpu.VMEM((whole, 2, 2 * slab, columns), bf),
                pltpu.VMEM((half, columns), f32),
                pltpu.SemaphoreType.DMA((whole, 2, 2)),
            ],
        )(place, rows, qkv_weights, partner, *signs)

    def middle(keep_own, keep_two, taken):
        count = keep_own.shape[0]
        return call(
            functools.partial(middle_kernel, size),
            [shape(count, HEAD), shape(count, HEAD, dtype=f32)],
            [VMEM] * 2,
            [VMEM] * 3,
        )(keep_own, keep_two, taken)

    both_send, both_own, both_two = project(
        (1, 2), rows, partner_early
    )
    taken = swap_z(both_send, 1)
    query_send, query_own, query_two = project(
        (0,), after(rows, both_send), partner_query.reshape(2, 1, slab, columns),
    )
    query_taken = swap_z(query_send, 1)
    send, both_total = middle(both_own, both_two, after(taken, query_send, late_far))
    both_last = swap_z(send, 2)
    send, query_total = middle(query_own, query_two, after(query_taken, both_total))
    query_last = swap_z(send, 2)
    both = call(
        functools.partial(key_value_kernel, half),
        shape(4 * half, HEAD), VMEM, [SMEM] + [VMEM] * 3,
    )(place, both_total, after(both_last, query_total), gain_key.reshape(heads, HEAD))
    both_partner = swap_x(both)
    late_got = call(near_kernel, shape(2 * team + 4, own_rows, 2 * slab), VMEM, [VMEM] * 2)(
        late_near, late_far
    )
    late_got = swap_z(after(late_got, both), 1)
    done = call(
        functools.partial(attend_kernel, half),
        shape(half + size, HEAD), VMEM, [SMEM] + [VMEM] * 5,
    )(place, query_total, query_last, gain_query.reshape(heads, HEAD), both, both_partner)

    by_head, last_head = [], []
    for k in steps:
        block = swap_z(done, k) if k else done
        main = block[:half].reshape(depth, size, HEAD)
        by_head.append(jnp.concatenate([main[j ^ k] for j in steps], axis=0))
        last_head.append(block[half:])
    attended = jnp.concatenate(by_head + [jnp.concatenate(last_head, axis=0)], axis=1)

    def relative(value, axis):
        parts = [
            lax.dynamic_slice_in_dim(value, (z ^ k) * HEAD, HEAD, axis) for k in steps
        ] + [lax.slice_in_dim(value, depth * HEAD, heads * HEAD, axis=axis)]
        return jnp.concatenate(parts, axis=axis)

    mix, out_signs = call(
        late_kernel,
        [shape(half, columns), shape(depth, 2, own_rows, 2 * slab)], [VMEM] * 2,
        [SMEM] + [VMEM] * 4,
    )(place, late_own, after(late_near, done), late_far, late_got)
    attended_flipped = attended * mix
    first = jnp.where(x == 0, out_t, out_partner)
    second = jnp.where(x == 0, out_partner, out_t)
    out_full = relative(jnp.concatenate([first, second], axis=1), 2)
    partial = jnp.stack(
        [dot32_t(attended, out_full[0]), dot32_t(attended_flipped, out_full[1])]
    ).astype(bf)
    partial = partial.reshape(2, depth, team, own_rows, 2 * slab)
    kept, sent = call(
        core_kernel,
        [shape(depth, own_rows, 2 * slab, dtype=f32), shape(depth, own_rows, 2 * slab)],
        [VMEM] * 2, [VMEM] * 3,
    )(partial[:, :, 0::2], swap_u(partial[:, :, 1::2], 1), out_signs)
    blocks = call(
        team_kernel, [shape(own_rows, 2 * slab)] * depth, [VMEM] * depth, [VMEM] * 2
    )(kept, swap_u(sent, 2))
    return call(
        final_kernel, shape(own_rows, width), VMEM, [SMEM] + [VMEM] * depth
    )(place, blocks[0], *[swap_z(blocks[k], k) for k in steps if k])


def body(*arrays):
    heads = arrays[2].shape[3] // HEAD
    depth = lax.axis_size("blk") // 2
    if depth == heads - 1 and depth == 4 and lax.axis_size("uly") == 4:
        return stationary_plan(*arrays)
    return gather_plan(*arrays)


def solution(mesh):
    return jax.shard_map(
        body,
        mesh=mesh,
        in_specs=(
            P(("blk", "uly"), None),
            P(("blk", "uly"), None),
            P(None, None, "blk", "uly"),
            P("blk", None, "uly"),
            P("uly"),
            P("uly"),
            P(None, "uly", "blk"),
            P("blk", "uly"),
            P("blk", None),
        ),
        out_specs=P(("blk", "uly"), None),
        check_vma=False,
    )
```

```python
import functools
import math

import jax
import jax.numpy as jnp
from jax import lax
from jax.experimental import pallas as pl
from jax.experimental.pallas import tpu as pltpu
from jax.sharding import PartitionSpec as P

HEAD = 128


epsilon = 1e-06


def signed(bit_values):
    return (2 * bit_values - 1).astype(jnp.float32)


def normalize(values, gain_vector):
    row_count = values.shape[0]
    by_head = values.astype(jnp.float32).reshape(row_count, -1, HEAD)
    inverse_rms = lax.rsqrt(jnp.mean(by_head * by_head, axis=-1, keepdims=True) + epsilon)
    return (by_head * inverse_rms * gain_vector.reshape(-1, HEAD)).astype(jnp.bfloat16)


def gather_plan(
    tokens, in_bits, qkv_weights, qkv_bits, gain_query, gain_key, out_weights, mix_bits, out_bits
):
    flipped = (tokens.astype(jnp.float32) * signed(in_bits)).astype(jnp.bfloat16)
    group_rows = lax.all_gather(jnp.stack([tokens, flipped]), "uly", axis=1, tiled=True)
    row_total = group_rows.shape[1]
    projections = jnp.einsum(
        "mrd,mkdc->rmkc",
        group_rows,
        lax.all_gather(qkv_weights, "blk", axis=2, tiled=True),
        preferred_element_type=jnp.float32,
    )
    projected = (projections[:, 0] + signed(qkv_bits) * projections[:, 1]).astype(jnp.bfloat16)
    queries = normalize(projected[:, 0], gain_query)
    head_count = queries.shape[1]
    keys_normed = normalize(projected[:, 1], gain_key).reshape(row_total, -1)
    values_block = projected[:, 2]
    score_scale = 1.0 / math.sqrt(HEAD)

    def attend(running, shard_piece):
        numerator, denominator = running
        key_rows = shard_piece[0].reshape(shard_piece[0].shape[0], head_count, HEAD)
        value_rows = shard_piece[1].reshape(shard_piece[1].shape[0], head_count, HEAD)
        scores = (
            jnp.einsum("rhd,nhd->hrn", queries, key_rows, preferred_element_type=jnp.float32)
            * score_scale
        )
        weights = jnp.exp(scores).astype(jnp.bfloat16)
        numerator = numerator + jnp.einsum(
            "hrn,nhd->rhd", weights, value_rows, preferred_element_type=jnp.float32
        )
        denominator = denominator + jnp.sum(weights.astype(jnp.float32), axis=2).T
        return (numerator, denominator)

    start_state = (
        jnp.zeros((row_total, head_count, HEAD), jnp.float32),
        jnp.zeros((row_total, head_count), jnp.float32),
    )
    all_keys, all_values = (
        lax.all_gather(keys_normed, "blk", axis=0, tiled=True),
        lax.all_gather(values_block, "blk", axis=0, tiled=True),
    )
    group_count = lax.axis_size("blk")
    per_block = 1
    while per_block * row_total < 512 and group_count % (per_block * 2) == 0:
        per_block = per_block * 2
    block_rows = per_block * row_total
    block_count = group_count // per_block
    key_blocks = all_keys.reshape(block_count, block_rows, all_keys.shape[1])
    value_blocks = all_values.reshape(block_count, block_rows, all_values.shape[1])

    def scan_step(running, block_pair):
        return (attend(running, block_pair), None)

    (numerator, denominator), unused = lax.scan(scan_step, start_state, (key_blocks, value_blocks))
    attended = (numerator / denominator[:, :, None]).astype(jnp.bfloat16).reshape(row_total, -1)
    attended_flipped = (attended.astype(jnp.float32) * signed(mix_bits)).astype(jnp.bfloat16)
    attended_pair = jnp.stack([attended, attended_flipped])
    out_signs = signed(out_bits)
    partial_out = jnp.einsum(
        "mrc,mcn->rmn",
        attended_pair,
        lax.all_gather(out_weights, "blk", axis=2, tiled=True),
        preferred_element_type=jnp.float32,
    )
    summed = lax.psum_scatter(
        partial_out.astype(jnp.bfloat16), "uly", scatter_dimension=0, tiled=True
    ).astype(jnp.float32)
    own_rows = summed.shape[0]
    own_signs = lax.dynamic_slice_in_dim(out_signs, lax.axis_index("uly") * own_rows, own_rows, 0)
    result_rows = summed[:, 0] + own_signs * summed[:, 1]
    return result_rows.astype(jnp.bfloat16)


def dot32(a, b):
    return lax.dot_general(
        a, b, (((1,), (0,)), ((), ())), preferred_element_type=jnp.float32
    )


def dot32_t(a, b):
    return lax.dot_general(
        a, b, (((1,), (1,)), ((), ())), preferred_element_type=jnp.float32
    )


bf = jnp.bfloat16
VMEM = pl.BlockSpec(memory_space=pltpu.VMEM)
SMEM = pl.BlockSpec(memory_space=pltpu.SMEM)
ANY = pl.BlockSpec(memory_space=pl.ANY)


def call(kernel, outs, out_specs, in_specs, scratch=(), flops=0, moved=0):
    return pl.pallas_call(
        kernel,
        out_shape=outs,
        in_specs=in_specs,
        out_specs=out_specs,
        scratch_shapes=list(scratch),
        compiler_params=pltpu.CompilerParams(vmem_limit_bytes=40 * 1024 * 1024),
        cost_estimate=pl.CostEstimate(flops=flops, bytes_accessed=moved, transcendentals=0),
    )


def shape(*dims, dtype=bf):
    return jax.ShapeDtypeStruct(dims, dtype)


def lanes(index, size):
    return pl.ds(pl.multiple_of(index * size, 128), size)


def copy_kernel(first, count, weights, out, sems):
    copies = [
        pltpu.make_async_copy(weights.at[m, pl.ds(first, count)], out.at[m], sems.at[m])
        for m in (0, 1)
    ]
    for copy in copies:
        copy.start()
    for copy in copies:
        copy.wait()


def sign_pieces(bits, u, team):
    piece = bits.shape[0] // team
    parts = [bits[pl.ds(pl.multiple_of((u ^ r) * piece, 8), piece), :] for r in range(team)]
    return [(2 * part - 1).astype(jnp.float32) for part in parts]


def prepare_kernel(team, place, tokens, in_bits, sign_bits, *blocks):
    wide = tokens.shape[1] // len(blocks)
    for k, block in enumerate(blocks):
        cut = lanes(place[0] ^ k, wide)
        plain = tokens[:, cut]
        sign = (2 * in_bits[:, cut] - 1).astype(jnp.float32)
        block[0] = plain
        block[1] = (plain.astype(jnp.float32) * sign).astype(bf)
    for i, part in enumerate((1, 2, 0)):
        for r, piece in enumerate(sign_pieces(sign_bits.at[part], place[2], team)):
            for block in blocks[1:3]:
                block[2 + team * i + r] = piece.astype(bf)


def late_signs_kernel(team, place, out_bits, mix_bits, weights, query_weights, out, near, far, sems):
    copies = [
        pltpu.make_async_copy(weights.at[m, 0], query_weights.at[m], sems.at[m]) for m in (0, 1)
    ]
    for copy in copies:
        copy.start()
    z, u = place[0], place[2]
    own_rows, wide = out.shape[1:]

    def fill(target, start, k):
        for i, r in enumerate((0, 2)):
            rows = pl.ds(pl.multiple_of((u ^ r) * own_rows, 8), own_rows)
            bits = out_bits[rows, lanes(z ^ k, wide)]
            target[start + i] = (2 * bits - 1).astype(jnp.float32).astype(bf)

    fill(out, 0, 0)
    for r, part in enumerate(sign_pieces(mix_bits, u, team)):
        near[r] = part.astype(bf)
        far[r] = part.astype(bf)
    fill(near, team, 1)
    fill(far, team, 2)
    fill(far, team + 2, 3)
    for copy in copies:
        copy.wait()


def near_kernel(near, far, out):
    team = near.shape[0] - 2
    out[:team] = near[:team]
    out[team : 2 * team] = far[:team]
    out[2 * team : 2 * team + 2] = near[team:]
    out[2 * team + 2 :] = far[team + 2 :]


def late_kernel(place, own, near, far, got, mix, out):
    team, own_rows = near.shape[0] - 2, near.shape[1]
    size = team * own_rows
    out[0] = own[...]
    out[1] = got[2 * team : 2 * team + 2]
    out[2] = far[team : team + 2]
    out[3] = got[2 * team + 2 :]
    for j, (ref, start) in enumerate(((near, 0), (got, 0), (far, 0), (got, team))):
        cut = slice(j * size, (j + 1) * size)
        for k in range(5):
            head = lanes(place[0] ^ k, HEAD) if k < 4 else slice(4 * HEAD, None)
            parts = [ref[start + r, :, head].astype(jnp.float32) for r in range(team)]
            mix[cut, k * HEAD : (k + 1) * HEAD] = jnp.concatenate(parts, axis=0).astype(bf)


def stack_kernel(*refs):
    for k, ref in enumerate(refs[:-1]):
        refs[-1][k] = ref[: refs[-1].shape[1]]


def pair_kernel(own, taken, out):
    out[0] = own[...]
    out[1] = taken[...]


def forward_kernel(taken, out):
    out[...] = taken[taken.shape[0] - out.shape[0] :]


def rows_kernel(place, own, taken, rows):
    depth, kinds, piece = own.shape[1:4]
    for m in range(kinds):
        for j in range(depth):
            parts = [ref[y, j, m].astype(jnp.float32) for y in (0, 1) for ref in (own, taken)]
            at = j * 4 * piece
            wide = jnp.concatenate(parts, axis=0)
            slab = wide.shape[1] // 2
            low, high = wide[:, :slab], wide[:, slab:]
            first = place[1] == 0
            rows[m, 0, at : at + 4 * piece] = jnp.where(first, low, high).astype(bf)
            rows[m, 1, at : at + 4 * piece] = jnp.where(first, high, low).astype(bf)


def project_kernel(
    parts, size, place, rows, weights, partner, signs_0, signs_1, signs_2, signs_3,
    send, keep_own, keep_two, total,
):
    z = place[0]
    half = rows.shape[2]
    depth = half // size

    def block(j, head):
        return total[j * size : (j + 1) * size, lanes(head, HEAD)]

    def main(target, start, k):
        for j in range(depth):
            at = start + (j ^ k) * size
            target[at : at + size] = block(j, z ^ k).astype(target.dtype)

    def rest(target, start, j):
        target[start : start + size] = block(j, depth).astype(target.dtype)

    for i, part in enumerate(parts):
        near, far = [
            dot32(rows[m, 0], weights[m, part]) + dot32(rows[m, 1], partner[m, i]) for m in (0, 1)
        ]
        total[...] = far
        plain = near
        at = part - 1 if part else 2
        team = signs_3.shape[0] // 3
        for j in range(depth):
            cut = slice(j * size, (j + 1) * size)
            ref = (signs_0, signs_1, signs_2, signs_3)[j]
            start = ref.shape[0] - (3 - at) * team
            pieces = [ref[start + r].astype(jnp.float32) for r in range(team)]
            total[cut] = plain[cut] + jnp.concatenate(pieces, axis=0) * total[cut]
        if part:
            main(send, 3 * half * i, 1)
            main(send, 3 * half * i + half, 3)
            main(keep_own, 2 * half * i, 0)
            main(keep_two, half * i, 2)
            for j in range(depth):
                rest(send, 3 * half * i + 2 * half + (j ^ 1) * size, j)
                rest(keep_own, 2 * half * i + half + j * size, j)
        else:
            main(send, 0, 1)
            rest(send, half, 1)
            main(send, half + size, 3)
            rest(send, 2 * half + size, 3)
            main(keep_own, 0, 0)
            rest(keep_own, half, 0)
            main(keep_two, 0, 2)
            rest(keep_two, half, 2)


def middle_kernel(size, keep_own, keep_two, taken, send, total):
    count = keep_two.shape[0]
    if keep_own.shape[0] == count:
        total[...] = keep_own[...] + taken[:count].astype(jnp.float32)
        send[...] = (keep_two[...] + taken[count:].astype(jnp.float32)).astype(bf)
        return
    half = count // 2
    for i in (0, 1):
        base, got = 2 * half * i, 3 * half * i
        first = slice(base, base + half)
        total[first] = keep_own[first] + taken[got : got + half].astype(jnp.float32)
        far = keep_two[half * i : half * i + half]
        send[first] = (far + taken[got + half : got + 2 * half].astype(jnp.float32)).astype(bf)
        for j in range(half // size):
            cut = slice(base + half + j * size, base + half + (j + 1) * size)
            at = got + 2 * half + j * size
            value = keep_own[cut] + taken[at : at + size].astype(jnp.float32)
            total[cut] = value
            at = base + half + (j ^ 2) * size
            send[at : at + size] = value.astype(bf)


def norm_rows(values, gain_row):
    wide = values.astype(jnp.float32)
    inverse_rms = lax.rsqrt(jnp.mean(wide * wide, axis=-1, keepdims=True) + epsilon)
    return (wide * inverse_rms * gain_row).astype(bf)


def key_value_kernel(half, place, total, taken, gain, out):
    keep = (total[...] + taken[...].astype(jnp.float32)).astype(bf)
    heads = gain.shape[0]
    out[:half] = norm_rows(keep[:half], gain[pl.ds(place[0], 1), :])
    out[half : 2 * half] = norm_rows(keep[half : 2 * half], gain[heads - 1 : heads, :])
    out[2 * half :] = keep[2 * half :]


def attend_kernel(half, place, total, taken, gain, own, partner, out):
    keep = (total[...] + taken[...].astype(jnp.float32)).astype(bf)
    heads = gain.shape[0]

    def attend(queries, cut):
        score_scale = 1.0 / math.sqrt(HEAD)
        totals, sums = 0.0, 0.0
        for both in (own, partner):
            scores = dot32_t(queries, both[cut]) * score_scale
            weights = jnp.exp(scores).astype(bf)
            totals = totals + jnp.sum(weights.astype(jnp.float32), axis=1, keepdims=True)
            sums = sums + dot32(weights, both[2 * half + cut.start : 2 * half + cut.stop])
        return (sums / totals).astype(bf)

    first = norm_rows(keep[:half], gain[pl.ds(place[0], 1), :])
    out[:half] = attend(first, slice(0, half))
    last = norm_rows(keep[half:], gain[heads - 1 : heads, :])
    out[half:] = attend(last, slice(half, 2 * half))


def core_kernel(own, taken, signs, kept, sent):
    for i, target in enumerate((kept, sent)):
        for j in range(kept.shape[0]):
            parts = [own[m, j, i].astype(jnp.float32) + taken[m, j, i].astype(jnp.float32) for m in (0, 1)]
            value = parts[0] + signs[j, i].astype(jnp.float32) * parts[1]
            target[j] = value.astype(target.dtype)


def team_kernel(kept, taken, *blocks):
    for j, block in enumerate(blocks):
        block[...] = (kept[j] + taken[j].astype(jnp.float32)).astype(bf)


def final_kernel(place, *refs):
    out = refs[-1]
    for k, block in enumerate(refs[:-1]):
        out[:, lanes(place[0] ^ k, block.shape[1])] = block[...]


def stationary_plan(
    tokens, in_bits, qkv_weights, qkv_bits, gain_query, gain_key, out_weights, mix_bits, out_bits
):
    groups = lax.axis_size("blk")
    team = lax.axis_size("uly")
    depth = groups // 2
    z = lax.axis_index("blk") // 2
    x = lax.axis_index("blk") % 2
    u = lax.axis_index("uly")
    own_rows, width = tokens.shape
    slab = qkv_weights.shape[2]
    columns = qkv_weights.shape[3]
    size = own_rows * team
    heads = columns // HEAD
    half = depth * size
    steps = range(depth)
    f32 = jnp.float32
    place = jnp.stack([z, x, u]).astype(jnp.int32)

    def swap_x(value):
        return lax.ppermute(value, "blk", [(i, i ^ 1) for i in range(groups)])

    def swap_z(value, step):
        return lax.ppermute(value, "blk", [(i, i ^ (2 * step)) for i in range(groups)])

    def swap_u(value, bit):
        return lax.ppermute(value, "uly", [(i, i ^ bit) for i in range(team)])

    def after(value, *earlier):
        return lax.optimization_barrier((value,) + earlier)[0]

    early = call(
        functools.partial(copy_kernel, 1, 2),
        shape(2, 2, slab, columns), ANY, [ANY], [pltpu.SemaphoreType.DMA((2,))],
    )(qkv_weights)
    partner_early = swap_x(early)

    sign_bits = jnp.transpose(qkv_bits, (1, 0, 2))
    counts = [2 + 3 * team if k in (1, 2) else 2 for k in steps]
    blocks = call(
        functools.partial(prepare_kernel, team),
        [shape(count, own_rows, 2 * slab) for count in counts],
        [VMEM] * depth, [SMEM] + [VMEM] * 3,
    )(place, after(tokens, early), in_bits, sign_bits)
    got = [blocks[0]] + [swap_z(blocks[k], k) for k in steps if k]

    def pair(first, second):
        return call(pair_kernel, shape(2, *first.shape), VMEM, [VMEM] * 2)(first, second)

    held_shape = (depth, 2, own_rows, 2 * slab)
    held = call(stack_kernel, shape(*held_shape), VMEM, [VMEM] * depth)(*got)
    forward = call(forward_kernel, shape(3 * team, own_rows, columns), VMEM, [VMEM])(got[2])
    signs = (blocks[2], got[1], got[2], swap_z(after(forward, held), 1))
    held = pair(held, swap_u(held, 2))
    rows = call(rows_kernel, shape(2, 2, half, slab), VMEM, [SMEM] + [VMEM] * 2)(
        place, held, swap_u(after(held, signs[3]), 1)
    )

    query_weights, late_own, late_near, late_far = call(
        functools.partial(late_signs_kernel, team),
        [shape(2, slab, columns)]
        + [shape(count, own_rows, 2 * slab) for count in (2, team + 2, team + 4)],
        [ANY] + [VMEM] * 3,
        [SMEM] + [VMEM] * 2 + [ANY],
        [pltpu.SemaphoreType.DMA((2,))],
    )(place, after(out_bits, blocks[0]), mix_bits, qkv_weights)
    partner_query = swap_x(after(query_weights, partner_early, forward))
    out_t = jnp.transpose(out_weights, (0, 2, 1))
    out_partner = swap_x(after(out_t, partner_query))

    def project(parts, rows, partner):
        whole = len(parts)
        count = half + size
        counts = (3 * half * whole, 2 * half * whole, half * whole)
        if parts == (0,):
            counts = (2 * count, count, count)
        return call(
            functools.partial(project_kernel, parts, size),
            [shape(counts[0], HEAD)] + [shape(count, HEAD, dtype=f32) for count in counts[1:]],
            [VMEM] * 3,
            [SMEM] + [VMEM] * 7,
            [
                pltpu.VMEM((half, columns), f32),
            ],
        )(place, rows, qkv_weights, partner, *signs)

    def middle(keep_own, keep_two, taken):
        count = keep_own.shape[0]
        return call(
            functools.partial(middle_kernel, size),
            [shape(count, HEAD), shape(count, HEAD, dtype=f32)],
            [VMEM] * 2,
            [VMEM] * 3,
        )(keep_own, keep_two, taken)

    both_send, both_own, both_two = project(
        (1, 2), rows, partner_early
    )
    taken = swap_z(both_send, 1)
    send, both_total = middle(both_own, both_two, taken)
    both_last = swap_z(send, 2)
    query_send, query_own, query_two = project(
        (0,), after(rows, both_total), partner_query.reshape(2, 1, slab, columns),
    )
    query_taken = swap_z(query_send, 1)
    send, query_total = middle(query_own, query_two, after(query_taken, both_total))
    query_last = swap_z(send, 2)
    both = call(
        functools.partial(key_value_kernel, half),
        shape(4 * half, HEAD), VMEM, [SMEM] + [VMEM] * 3,
    )(place, both_total, after(both_last, query_total), gain_key.reshape(heads, HEAD))
    both_partner = swap_x(both)
    late_far = swap_z(after(late_far, both), 2)
    done = call(
        functools.partial(attend_kernel, half),
        shape(half + size, HEAD), VMEM, [SMEM] + [VMEM] * 5,
    )(place, query_total, query_last, gain_query.reshape(heads, HEAD), both, both_partner)

    late_got = call(near_kernel, shape(2 * team + 4, own_rows, 2 * slab), VMEM, [VMEM] * 2)(
        after(late_near, done), late_far
    )
    late_got = swap_z(late_got, 1)

    by_head, last_head = [], []
    for k in steps:
        block = swap_z(done, k) if k else done
        main = block[:half].reshape(depth, size, HEAD)
        by_head.append(jnp.concatenate([main[j ^ k] for j in steps], axis=0))
        last_head.append(block[half:])
    attended = jnp.concatenate(by_head + [jnp.concatenate(last_head, axis=0)], axis=1)

    def relative(value, axis):
        parts = [
            lax.dynamic_slice_in_dim(value, (z ^ k) * HEAD, HEAD, axis) for k in steps
        ] + [lax.slice_in_dim(value, depth * HEAD, heads * HEAD, axis=axis)]
        return jnp.concatenate(parts, axis=axis)

    mix, out_signs = call(
        late_kernel,
        [shape(half, columns), shape(depth, 2, own_rows, 2 * slab)], [VMEM] * 2,
        [SMEM] + [VMEM] * 4,
    )(place, late_own, after(late_near, done), late_far, late_got)
    attended_flipped = attended * mix
    first = jnp.where(x == 0, out_t, out_partner)
    second = jnp.where(x == 0, out_partner, out_t)
    out_full = relative(jnp.concatenate([first, second], axis=1), 2)
    partial = jnp.stack(
        [dot32_t(attended, out_full[0]), dot32_t(attended_flipped, out_full[1])]
    ).astype(bf)
    partial = partial.reshape(2, depth, team, own_rows, 2 * slab)
    kept, sent = call(
        core_kernel,
        [shape(depth, own_rows, 2 * slab, dtype=f32), shape(depth, own_rows, 2 * slab)],
        [VMEM] * 2, [VMEM] * 3,
    )(partial[:, :, 0::2], swap_u(partial[:, :, 1::2], 1), out_signs)
    blocks = call(
        team_kernel, [shape(own_rows, 2 * slab)] * depth, [VMEM] * depth, [VMEM] * 2
    )(kept, swap_u(sent, 2))
    return call(
        final_kernel, shape(own_rows, width), VMEM, [SMEM] + [VMEM] * depth
    )(place, blocks[0], *[swap_z(blocks[k], k) for k in steps if k])


def body(*arrays):
    heads = arrays[2].shape[3] // HEAD
    depth = lax.axis_size("blk") // 2
    if depth == heads - 1 and depth == 4 and lax.axis_size("uly") == 4:
        return stationary_plan(*arrays)
    return gather_plan(*arrays)


def solution(mesh):
    return jax.shard_map(
        body,
        mesh=mesh,
        in_specs=(
            P(("blk", "uly"), None),
            P(("blk", "uly"), None),
            P(None, None, "blk", "uly"),
            P("blk", None, "uly"),
            P("uly"),
            P("uly"),
            P(None, "uly", "blk"),
            P("blk", "uly"),
            P("blk", None),
        ),
        out_specs=P(("blk", "uly"), None),
        check_vma=False,
    )
```

```python
import functools
import math

import jax
import jax.numpy as jnp
from jax import lax
from jax.experimental import pallas as pl
from jax.experimental.pallas import tpu as pltpu
from jax.sharding import PartitionSpec as P

HEAD = 128


epsilon = 1e-06


def signed(bit_values):
    return (2 * bit_values - 1).astype(jnp.float32)


def normalize(values, gain_vector):
    row_count = values.shape[0]
    by_head = values.astype(jnp.float32).reshape(row_count, -1, HEAD)
    inverse_rms = lax.rsqrt(jnp.mean(by_head * by_head, axis=-1, keepdims=True) + epsilon)
    return (by_head * inverse_rms * gain_vector.reshape(-1, HEAD)).astype(jnp.bfloat16)


def gather_plan(
    tokens, in_bits, qkv_weights, qkv_bits, gain_query, gain_key, out_weights, mix_bits, out_bits
):
    flipped = (tokens.astype(jnp.float32) * signed(in_bits)).astype(jnp.bfloat16)
    group_rows = lax.all_gather(jnp.stack([tokens, flipped]), "uly", axis=1, tiled=True)
    row_total = group_rows.shape[1]
    projections = jnp.einsum(
        "mrd,mkdc->rmkc",
        group_rows,
        lax.all_gather(qkv_weights, "blk", axis=2, tiled=True),
        preferred_element_type=jnp.float32,
    )
    projected = (projections[:, 0] + signed(qkv_bits) * projections[:, 1]).astype(jnp.bfloat16)
    queries = normalize(projected[:, 0], gain_query)
    head_count = queries.shape[1]
    keys_normed = normalize(projected[:, 1], gain_key).reshape(row_total, -1)
    values_block = projected[:, 2]
    score_scale = 1.0 / math.sqrt(HEAD)

    def attend(running, shard_piece):
        numerator, denominator = running
        key_rows = shard_piece[0].reshape(shard_piece[0].shape[0], head_count, HEAD)
        value_rows = shard_piece[1].reshape(shard_piece[1].shape[0], head_count, HEAD)
        scores = (
            jnp.einsum("rhd,nhd->hrn", queries, key_rows, preferred_element_type=jnp.float32)
            * score_scale
        )
        weights = jnp.exp(scores).astype(jnp.bfloat16)
        numerator = numerator + jnp.einsum(
            "hrn,nhd->rhd", weights, value_rows, preferred_element_type=jnp.float32
        )
        denominator = denominator + jnp.sum(weights.astype(jnp.float32), axis=2).T
        return (numerator, denominator)

    start_state = (
        jnp.zeros((row_total, head_count, HEAD), jnp.float32),
        jnp.zeros((row_total, head_count), jnp.float32),
    )
    all_keys, all_values = (
        lax.all_gather(keys_normed, "blk", axis=0, tiled=True),
        lax.all_gather(values_block, "blk", axis=0, tiled=True),
    )
    group_count = lax.axis_size("blk")
    per_block = 1
    while per_block * row_total < 512 and group_count % (per_block * 2) == 0:
        per_block = per_block * 2
    block_rows = per_block * row_total
    block_count = group_count // per_block
    key_blocks = all_keys.reshape(block_count, block_rows, all_keys.shape[1])
    value_blocks = all_values.reshape(block_count, block_rows, all_values.shape[1])

    def scan_step(running, block_pair):
        return (attend(running, block_pair), None)

    (numerator, denominator), unused = lax.scan(scan_step, start_state, (key_blocks, value_blocks))
    attended = (numerator / denominator[:, :, None]).astype(jnp.bfloat16).reshape(row_total, -1)
    attended_flipped = (attended.astype(jnp.float32) * signed(mix_bits)).astype(jnp.bfloat16)
    attended_pair = jnp.stack([attended, attended_flipped])
    out_signs = signed(out_bits)
    partial_out = jnp.einsum(
        "mrc,mcn->rmn",
        attended_pair,
        lax.all_gather(out_weights, "blk", axis=2, tiled=True),
        preferred_element_type=jnp.float32,
    )
    summed = lax.psum_scatter(
        partial_out.astype(jnp.bfloat16), "uly", scatter_dimension=0, tiled=True
    ).astype(jnp.float32)
    own_rows = summed.shape[0]
    own_signs = lax.dynamic_slice_in_dim(out_signs, lax.axis_index("uly") * own_rows, own_rows, 0)
    result_rows = summed[:, 0] + own_signs * summed[:, 1]
    return result_rows.astype(jnp.bfloat16)


def dot32(a, b):
    return lax.dot_general(
        a, b, (((1,), (0,)), ((), ())), preferred_element_type=jnp.float32
    )


def dot32_t(a, b):
    return lax.dot_general(
        a, b, (((1,), (1,)), ((), ())), preferred_element_type=jnp.float32
    )


bf = jnp.bfloat16
VMEM = pl.BlockSpec(memory_space=pltpu.VMEM)
SMEM = pl.BlockSpec(memory_space=pltpu.SMEM)
ANY = pl.BlockSpec(memory_space=pl.ANY)


def call(kernel, outs, out_specs, in_specs, scratch=(), flops=0, moved=0):
    return pl.pallas_call(
        kernel,
        out_shape=outs,
        in_specs=in_specs,
        out_specs=out_specs,
        scratch_shapes=list(scratch),
        compiler_params=pltpu.CompilerParams(vmem_limit_bytes=40 * 1024 * 1024),
        cost_estimate=pl.CostEstimate(flops=flops, bytes_accessed=moved, transcendentals=0),
    )


def shape(*dims, dtype=bf):
    return jax.ShapeDtypeStruct(dims, dtype)


def lanes(index, size):
    return pl.ds(pl.multiple_of(index * size, 128), size)


def copy_kernel(first, count, weights, out, sems):
    copies = [
        pltpu.make_async_copy(weights.at[m, pl.ds(first, count)], out.at[m], sems.at[m])
        for m in (0, 1)
    ]
    for copy in copies:
        copy.start()
    for copy in copies:
        copy.wait()


def sign_pieces(bits, u, team):
    piece = bits.shape[0] // team
    parts = [bits[pl.ds(pl.multiple_of((u ^ r) * piece, 8), piece), :] for r in range(team)]
    return [(2 * part - 1).astype(jnp.float32) for part in parts]


def prepare_kernel(team, place, tokens, in_bits, sign_bits, *blocks):
    wide = tokens.shape[1] // len(blocks)
    for k, block in enumerate(blocks):
        cut = lanes(place[0] ^ k, wide)
        plain = tokens[:, cut]
        sign = (2 * in_bits[:, cut] - 1).astype(jnp.float32)
        block[0] = plain
        block[1] = (plain.astype(jnp.float32) * sign).astype(bf)
    for i, part in enumerate((1, 2, 0)):
        for r, piece in enumerate(sign_pieces(sign_bits.at[part], place[2], team)):
            for block in blocks[1:3]:
                block[2 + team * i + r] = piece.astype(bf)


def late_signs_kernel(team, place, out_bits, mix_bits, weights, query_weights, out, near, far, sems):
    copies = [
        pltpu.make_async_copy(weights.at[m, 0], query_weights.at[m], sems.at[m]) for m in (0, 1)
    ]
    for copy in copies:
        copy.start()
    z, u = place[0], place[2]
    own_rows, wide = out.shape[1:]

    def fill(target, start, k):
        for i, r in enumerate((0, 2)):
            rows = pl.ds(pl.multiple_of((u ^ r) * own_rows, 8), own_rows)
            bits = out_bits[rows, lanes(z ^ k, wide)]
            target[start + i] = (2 * bits - 1).astype(jnp.float32).astype(bf)

    fill(out, 0, 0)
    for r, part in enumerate(sign_pieces(mix_bits, u, team)):
        near[r] = part.astype(bf)
        far[r] = part.astype(bf)
    fill(near, team, 1)
    fill(far, team, 2)
    fill(far, team + 2, 3)
    for copy in copies:
        copy.wait()


def near_kernel(near, far, out):
    team = near.shape[0] - 2
    out[:team] = near[:team]
    out[team : 2 * team] = far[:team]
    out[2 * team : 2 * team + 2] = near[team:]
    out[2 * team + 2 :] = far[team + 2 :]


def late_kernel(place, own, near, far, got, mix, out):
    team, own_rows = near.shape[0] - 2, near.shape[1]
    size = team * own_rows
    out[0] = own[...]
    out[1] = got[2 * team : 2 * team + 2]
    out[2] = far[team : team + 2]
    out[3] = got[2 * team + 2 :]
    for j, (ref, start) in enumerate(((near, 0), (got, 0), (far, 0), (got, team))):
        cut = slice(j * size, (j + 1) * size)
        for k in range(5):
            head = lanes(place[0] ^ k, HEAD) if k < 4 else slice(4 * HEAD, None)
            parts = [ref[start + r, :, head].astype(jnp.float32) for r in range(team)]
            mix[cut, k * HEAD : (k + 1) * HEAD] = jnp.concatenate(parts, axis=0).astype(bf)


def stack_kernel(*refs):
    for k, ref in enumerate(refs[:-1]):
        refs[-1][k] = ref[: refs[-1].shape[1]]


def pair_kernel(own, taken, out):
    out[0] = own[...]
    out[1] = taken[...]


def forward_kernel(taken, out):
    out[...] = taken[taken.shape[0] - out.shape[0] :]


def rows_kernel(place, own, taken, rows):
    depth, kinds, piece = own.shape[1:4]
    for m in range(kinds):
        for j in range(depth):
            parts = [ref[y, j, m].astype(jnp.float32) for y in (0, 1) for ref in (own, taken)]
            at = j * 4 * piece
            wide = jnp.concatenate(parts, axis=0)
            slab = wide.shape[1] // 2
            low, high = wide[:, :slab], wide[:, slab:]
            first = place[1] == 0
            rows[m, 0, at : at + 4 * piece] = jnp.where(first, low, high).astype(bf)
            rows[m, 1, at : at + 4 * piece] = jnp.where(first, high, low).astype(bf)


def project_kernel(
    parts, size, place, rows, weights, partner, signs_0, signs_1, signs_2, signs_3,
    send, keep_own, keep_two, total,
):
    z = place[0]
    half = rows.shape[2]
    depth = half // size

    def block(j, head):
        return total[j * size : (j + 1) * size, lanes(head, HEAD)]

    def main(target, start, k):
        for j in range(depth):
            at = start + (j ^ k) * size
            target[at : at + size] = block(j, z ^ k).astype(target.dtype)

    def rest(target, start, j):
        target[start : start + size] = block(j, depth).astype(target.dtype)

    for i, part in enumerate(parts):
        near, far = [
            dot32(rows[m, 0], weights[m, part]) + dot32(rows[m, 1], partner[m, i]) for m in (0, 1)
        ]
        total[...] = far
        plain = near
        at = part - 1 if part else 2
        team = signs_3.shape[0] // 3
        for j in range(depth):
            cut = slice(j * size, (j + 1) * size)
            ref = (signs_0, signs_1, signs_2, signs_3)[j]
            start = ref.shape[0] - (3 - at) * team
            pieces = [ref[start + r].astype(jnp.float32) for r in range(team)]
            total[cut] = plain[cut] + jnp.concatenate(pieces, axis=0) * total[cut]
        if part:
            main(send, 3 * half * i, 1)
            main(send, 3 * half * i + half, 3)
            main(keep_own, 2 * half * i, 0)
            main(keep_two, half * i, 2)
            for j in range(depth):
                rest(send, 3 * half * i + 2 * half + (j ^ 1) * size, j)
                rest(keep_own, 2 * half * i + half + j * size, j)
        else:
            main(send, 0, 1)
            rest(send, half, 1)
            main(send, half + size, 3)
            rest(send, 2 * half + size, 3)
            main(keep_own, 0, 0)
            rest(keep_own, half, 0)
            main(keep_two, 0, 2)
            rest(keep_two, half, 2)


def middle_kernel(size, keep_own, keep_two, taken, send, total):
    count = keep_two.shape[0]
    if keep_own.shape[0] == count:
        total[...] = keep_own[...] + taken[:count].astype(jnp.float32)
        send[...] = (keep_two[...] + taken[count:].astype(jnp.float32)).astype(bf)
        return
    half = count // 2
    for i in (0, 1):
        base, got = 2 * half * i, 3 * half * i
        first = slice(base, base + half)
        total[first] = keep_own[first] + taken[got : got + half].astype(jnp.float32)
        far = keep_two[half * i : half * i + half]
        send[first] = (far + taken[got + half : got + 2 * half].astype(jnp.float32)).astype(bf)
        for j in range(half // size):
            cut = slice(base + half + j * size, base + half + (j + 1) * size)
            at = got + 2 * half + j * size
            value = keep_own[cut] + taken[at : at + size].astype(jnp.float32)
            total[cut] = value
            at = base + half + (j ^ 2) * size
            send[at : at + size] = value.astype(bf)


def norm_rows(values, gain_row):
    wide = values.astype(jnp.float32)
    inverse_rms = lax.rsqrt(jnp.mean(wide * wide, axis=-1, keepdims=True) + epsilon)
    return (wide * inverse_rms * gain_row).astype(bf)


def key_value_kernel(half, place, total, taken, gain, out):
    keep = (total[...] + taken[...].astype(jnp.float32)).astype(bf)
    heads = gain.shape[0]
    out[:half] = norm_rows(keep[:half], gain[pl.ds(place[0], 1), :])
    out[half : 2 * half] = norm_rows(keep[half : 2 * half], gain[heads - 1 : heads, :])
    out[2 * half :] = keep[2 * half :]


def attend_kernel(half, place, total, taken, gain, own, partner, out):
    keep = (total[...] + taken[...].astype(jnp.float32)).astype(bf)
    heads = gain.shape[0]

    def attend(queries, cut):
        score_scale = 1.0 / math.sqrt(HEAD)
        totals, sums = 0.0, 0.0
        for both in (own, partner):
            scores = dot32_t(queries, both[cut]) * score_scale
            weights = jnp.exp(scores).astype(bf)
            totals = totals + jnp.sum(weights.astype(jnp.float32), axis=1, keepdims=True)
            sums = sums + dot32(weights, both[2 * half + cut.start : 2 * half + cut.stop])
        return (sums / totals).astype(bf)

    first = norm_rows(keep[:half], gain[pl.ds(place[0], 1), :])
    out[:half] = attend(first, slice(0, half))
    last = norm_rows(keep[half:], gain[heads - 1 : heads, :])
    out[half:] = attend(last, slice(half, 2 * half))


def core_kernel(own, taken, signs, kept, sent):
    for i, target in enumerate((kept, sent)):
        for j in range(kept.shape[0]):
            parts = [own[m, j, i].astype(jnp.float32) + taken[m, j, i].astype(jnp.float32) for m in (0, 1)]
            value = parts[0] + signs[j, i].astype(jnp.float32) * parts[1]
            target[j] = value.astype(target.dtype)


def team_kernel(kept, taken, *blocks):
    for j, block in enumerate(blocks):
        block[...] = (kept[j] + taken[j].astype(jnp.float32)).astype(bf)


def final_kernel(place, *refs):
    out = refs[-1]
    for k, block in enumerate(refs[:-1]):
        out[:, lanes(place[0] ^ k, block.shape[1])] = block[...]


def stationary_plan(
    tokens, in_bits, qkv_weights, qkv_bits, gain_query, gain_key, out_weights, mix_bits, out_bits
):
    groups = lax.axis_size("blk")
    team = lax.axis_size("uly")
    depth = groups // 2
    z = lax.axis_index("blk") // 2
    x = lax.axis_index("blk") % 2
    u = lax.axis_index("uly")
    own_rows, width = tokens.shape
    slab = qkv_weights.shape[2]
    columns = qkv_weights.shape[3]
    size = own_rows * team
    heads = columns // HEAD
    half = depth * size
    steps = range(depth)
    f32 = jnp.float32
    place = jnp.stack([z, x, u]).astype(jnp.int32)

    def swap_x(value):
        return lax.ppermute(value, "blk", [(i, i ^ 1) for i in range(groups)])

    def swap_z(value, step):
        return lax.ppermute(value, "blk", [(i, i ^ (2 * step)) for i in range(groups)])

    def swap_u(value, bit):
        return lax.ppermute(value, "uly", [(i, i ^ bit) for i in range(team)])

    def after(value, *earlier):
        return lax.optimization_barrier((value,) + earlier)[0]

    early = call(
        functools.partial(copy_kernel, 1, 2),
        shape(2, 2, slab, columns), ANY, [ANY], [pltpu.SemaphoreType.DMA((2,))],
    )(qkv_weights)
    partner_early = swap_x(early)

    sign_bits = jnp.transpose(qkv_bits, (1, 0, 2))
    counts = [2 + 3 * team if k in (1, 2) else 2 for k in steps]
    blocks = call(
        functools.partial(prepare_kernel, team),
        [shape(count, own_rows, 2 * slab) for count in counts],
        [VMEM] * depth, [SMEM] + [VMEM] * 3,
    )(place, after(tokens, early), in_bits, sign_bits)
    got = [blocks[0]] + [swap_z(blocks[k], k) for k in steps if k]

    def pair(first, second):
        return call(pair_kernel, shape(2, *first.shape), VMEM, [VMEM] * 2)(first, second)

    held_shape = (depth, 2, own_rows, 2 * slab)
    held = call(stack_kernel, shape(*held_shape), VMEM, [VMEM] * depth)(*got)
    forward = call(forward_kernel, shape(3 * team, own_rows, columns), VMEM, [VMEM])(got[2])
    signs = (blocks[2], got[1], got[2], swap_z(after(forward, held), 1))
    held = pair(held, swap_u(held, 2))
    rows = call(rows_kernel, shape(2, 2, half, slab), VMEM, [SMEM] + [VMEM] * 2)(
        place, held, swap_u(after(held, signs[3]), 1)
    )

    query_weights, late_own, late_near, late_far = call(
        functools.partial(late_signs_kernel, team),
        [shape(2, slab, columns)]
        + [shape(count, own_rows, 2 * slab) for count in (2, team + 2, team + 4)],
        [ANY] + [VMEM] * 3,
        [SMEM] + [VMEM] * 2 + [ANY],
        [pltpu.SemaphoreType.DMA((2,))],
    )(place, after(out_bits, blocks[0]), mix_bits, qkv_weights)
    late_far = swap_z(after(late_far, held), 2)
    partner_query = swap_x(after(query_weights, partner_early, forward))
    out_t = jnp.transpose(out_weights, (0, 2, 1))
    out_partner = swap_x(after(out_t, partner_query))

    def project(parts, rows, partner):
        whole = len(parts)
        count = half + size
        counts = (3 * half * whole, 2 * half * whole, half * whole)
        if parts == (0,):
            counts = (2 * count, count, count)
        return call(
            functools.partial(project_kernel, parts, size),
            [shape(counts[0], HEAD)] + [shape(count, HEAD, dtype=f32) for count in counts[1:]],
            [VMEM] * 3,
            [SMEM] + [VMEM] * 7,
            [
                pltpu.VMEM((half, columns), f32),
            ],
        )(place, rows, qkv_weights, partner, *signs)

    def middle(keep_own, keep_two, taken):
        count = keep_own.shape[0]
        return call(
            functools.partial(middle_kernel, size),
            [shape(count, HEAD), shape(count, HEAD, dtype=f32)],
            [VMEM] * 2,
            [VMEM] * 3,
        )(keep_own, keep_two, taken)

    both_send, both_own, both_two = project(
        (1, 2), rows, partner_early
    )
    taken = swap_z(both_send, 1)
    send, both_total = middle(both_own, both_two, taken)
    both_last = swap_z(send, 2)
    query_send, query_own, query_two = project(
        (0,), after(rows, both_total, late_far), partner_query.reshape(2, 1, slab, columns),
    )
    query_taken = swap_z(query_send, 1)
    send, query_total = middle(query_own, query_two, after(query_taken, both_total))
    query_last = swap_z(send, 2)
    both = call(
        functools.partial(key_value_kernel, half),
        shape(4 * half, HEAD), VMEM, [SMEM] + [VMEM] * 3,
    )(place, both_total, after(both_last, query_total), gain_key.reshape(heads, HEAD))
    both_partner = swap_x(both)
    late_got = call(near_kernel, shape(2 * team + 4, own_rows, 2 * slab), VMEM, [VMEM] * 2)(
        late_near, late_far
    )
    late_got = swap_z(after(late_got, both), 1)
    done = call(
        functools.partial(attend_kernel, half),
        shape(half + size, HEAD), VMEM, [SMEM] + [VMEM] * 5,
    )(place, query_total, query_last, gain_query.reshape(heads, HEAD), both, both_partner)

    by_head, last_head = [], []
    for k in steps:
        block = swap_z(done, k) if k else done
        main = block[:half].reshape(depth, size, HEAD)
        by_head.append(jnp.concatenate([main[j ^ k] for j in steps], axis=0))
        last_head.append(block[half:])
    attended = jnp.concatenate(by_head + [jnp.concatenate(last_head, axis=0)], axis=1)

    def relative(value, axis):
        parts = [
            lax.dynamic_slice_in_dim(value, (z ^ k) * HEAD, HEAD, axis) for k in steps
        ] + [lax.slice_in_dim(value, depth * HEAD, heads * HEAD, axis=axis)]
        return jnp.concatenate(parts, axis=axis)

    mix, out_signs = call(
        late_kernel,
        [shape(half, columns), shape(depth, 2, own_rows, 2 * slab)], [VMEM] * 2,
        [SMEM] + [VMEM] * 4,
    )(place, late_own, after(late_near, done), late_far, late_got)
    attended_flipped = attended * mix
    first = jnp.where(x == 0, out_t, out_partner)
    second = jnp.where(x == 0, out_partner, out_t)
    out_full = relative(jnp.concatenate([first, second], axis=1), 2)
    partial = jnp.stack(
        [dot32_t(attended, out_full[0]), dot32_t(attended_flipped, out_full[1])]
    ).astype(bf)
    partial = partial.reshape(2, depth, team, own_rows, 2 * slab)
    kept, sent = call(
        core_kernel,
        [shape(depth, own_rows, 2 * slab, dtype=f32), shape(depth, own_rows, 2 * slab)],
        [VMEM] * 2, [VMEM] * 3,
    )(partial[:, :, 0::2], swap_u(partial[:, :, 1::2], 1), out_signs)
    blocks = call(
        team_kernel, [shape(own_rows, 2 * slab)] * depth, [VMEM] * depth, [VMEM] * 2
    )(kept, swap_u(sent, 2))
    return call(
        final_kernel, shape(own_rows, width), VMEM, [SMEM] + [VMEM] * depth
    )(place, blocks[0], *[swap_z(blocks[k], k) for k in steps if k])


def body(*arrays):
    heads = arrays[2].shape[3] // HEAD
    depth = lax.axis_size("blk") // 2
    if depth == heads - 1 and depth == 4 and lax.axis_size("uly") == 4:
        return stationary_plan(*arrays)
    return gather_plan(*arrays)


def solution(mesh):
    return jax.shard_map(
        body,
        mesh=mesh,
        in_specs=(
            P(("blk", "uly"), None),
            P(("blk", "uly"), None),
            P(None, None, "blk", "uly"),
            P("blk", None, "uly"),
            P("uly"),
            P("uly"),
            P(None, "uly", "blk"),
            P("blk", "uly"),
            P("blk", None),
        ),
        out_specs=P(("blk", "uly"), None),
        check_vma=False,
    )
```

```python
import functools
import math

import jax
import jax.numpy as jnp
from jax import lax
from jax.experimental import pallas as pl
from jax.experimental.pallas import tpu as pltpu
from jax.sharding import PartitionSpec as P

HEAD = 128


epsilon = 1e-06


def signed(bit_values):
    return (2 * bit_values - 1).astype(jnp.float32)


def normalize(values, gain_vector):
    row_count = values.shape[0]
    by_head = values.astype(jnp.float32).reshape(row_count, -1, HEAD)
    inverse_rms = lax.rsqrt(jnp.mean(by_head * by_head, axis=-1, keepdims=True) + epsilon)
    return (by_head * inverse_rms * gain_vector.reshape(-1, HEAD)).astype(jnp.bfloat16)


def gather_plan(
    tokens, in_bits, qkv_weights, qkv_bits, gain_query, gain_key, out_weights, mix_bits, out_bits
):
    flipped = (tokens.astype(jnp.float32) * signed(in_bits)).astype(jnp.bfloat16)
    group_rows = lax.all_gather(jnp.stack([tokens, flipped]), "uly", axis=1, tiled=True)
    row_total = group_rows.shape[1]
    projections = jnp.einsum(
        "mrd,mkdc->rmkc",
        group_rows,
        lax.all_gather(qkv_weights, "blk", axis=2, tiled=True),
        preferred_element_type=jnp.float32,
    )
    projected = (projections[:, 0] + signed(qkv_bits) * projections[:, 1]).astype(jnp.bfloat16)
    queries = normalize(projected[:, 0], gain_query)
    head_count = queries.shape[1]
    keys_normed = normalize(projected[:, 1], gain_key).reshape(row_total, -1)
    values_block = projected[:, 2]
    score_scale = 1.0 / math.sqrt(HEAD)

    def attend(running, shard_piece):
        numerator, denominator = running
        key_rows = shard_piece[0].reshape(shard_piece[0].shape[0], head_count, HEAD)
        value_rows = shard_piece[1].reshape(shard_piece[1].shape[0], head_count, HEAD)
        scores = (
            jnp.einsum("rhd,nhd->hrn", queries, key_rows, preferred_element_type=jnp.float32)
            * score_scale
        )
        weights = jnp.exp(scores).astype(jnp.bfloat16)
        numerator = numerator + jnp.einsum(
            "hrn,nhd->rhd", weights, value_rows, preferred_element_type=jnp.float32
        )
        denominator = denominator + jnp.sum(weights.astype(jnp.float32), axis=2).T
        return (numerator, denominator)

    start_state = (
        jnp.zeros((row_total, head_count, HEAD), jnp.float32),
        jnp.zeros((row_total, head_count), jnp.float32),
    )
    all_keys, all_values = (
        lax.all_gather(keys_normed, "blk", axis=0, tiled=True),
        lax.all_gather(values_block, "blk", axis=0, tiled=True),
    )
    group_count = lax.axis_size("blk")
    per_block = 1
    while per_block * row_total < 512 and group_count % (per_block * 2) == 0:
        per_block = per_block * 2
    block_rows = per_block * row_total
    block_count = group_count // per_block
    key_blocks = all_keys.reshape(block_count, block_rows, all_keys.shape[1])
    value_blocks = all_values.reshape(block_count, block_rows, all_values.shape[1])

    def scan_step(running, block_pair):
        return (attend(running, block_pair), None)

    (numerator, denominator), unused = lax.scan(scan_step, start_state, (key_blocks, value_blocks))
    attended = (numerator / denominator[:, :, None]).astype(jnp.bfloat16).reshape(row_total, -1)
    attended_flipped = (attended.astype(jnp.float32) * signed(mix_bits)).astype(jnp.bfloat16)
    attended_pair = jnp.stack([attended, attended_flipped])
    out_signs = signed(out_bits)
    partial_out = jnp.einsum(
        "mrc,mcn->rmn",
        attended_pair,
        lax.all_gather(out_weights, "blk", axis=2, tiled=True),
        preferred_element_type=jnp.float32,
    )
    summed = lax.psum_scatter(
        partial_out.astype(jnp.bfloat16), "uly", scatter_dimension=0, tiled=True
    ).astype(jnp.float32)
    own_rows = summed.shape[0]
    own_signs = lax.dynamic_slice_in_dim(out_signs, lax.axis_index("uly") * own_rows, own_rows, 0)
    result_rows = summed[:, 0] + own_signs * summed[:, 1]
    return result_rows.astype(jnp.bfloat16)


def dot32(a, b):
    return lax.dot_general(
        a, b, (((1,), (0,)), ((), ())), preferred_element_type=jnp.float32
    )


def dot32_t(a, b):
    return lax.dot_general(
        a, b, (((1,), (1,)), ((), ())), preferred_element_type=jnp.float32
    )


bf = jnp.bfloat16
VMEM = pl.BlockSpec(memory_space=pltpu.VMEM)
SMEM = pl.BlockSpec(memory_space=pltpu.SMEM)
ANY = pl.BlockSpec(memory_space=pl.ANY)


def call(kernel, outs, out_specs, in_specs, scratch=(), flops=0, moved=0):
    return pl.pallas_call(
        kernel,
        out_shape=outs,
        in_specs=in_specs,
        out_specs=out_specs,
        scratch_shapes=list(scratch),
        compiler_params=pltpu.CompilerParams(vmem_limit_bytes=40 * 1024 * 1024),
        cost_estimate=pl.CostEstimate(flops=flops, bytes_accessed=moved, transcendentals=0),
    )


def shape(*dims, dtype=bf):
    return jax.ShapeDtypeStruct(dims, dtype)


def lanes(index, size):
    return pl.ds(pl.multiple_of(index * size, 128), size)


def copy_kernel(first, count, weights, out, sems):
    copies = [
        pltpu.make_async_copy(weights.at[m, pl.ds(first, count)], out.at[m], sems.at[m])
        for m in (0, 1)
    ]
    for copy in copies:
        copy.start()
    for copy in copies:
        copy.wait()


def sign_pieces(bits, u, team):
    piece = bits.shape[0] // team
    parts = [bits[pl.ds(pl.multiple_of((u ^ r) * piece, 8), piece), :] for r in range(team)]
    return [(2 * part - 1).astype(jnp.float32) for part in parts]


def prepare_kernel(team, place, tokens, in_bits, sign_bits, *blocks):
    wide = tokens.shape[1] // len(blocks)
    for k, block in enumerate(blocks):
        cut = lanes(place[0] ^ k, wide)
        plain = tokens[:, cut]
        sign = (2 * in_bits[:, cut] - 1).astype(jnp.float32)
        block[0] = plain
        block[1] = (plain.astype(jnp.float32) * sign).astype(bf)
    for i, part in enumerate((1, 2, 0)):
        for r, piece in enumerate(sign_pieces(sign_bits.at[part], place[2], team)):
            for block in blocks[1:3]:
                block[2 + team * i + r] = piece.astype(bf)


def late_signs_kernel(team, place, out_bits, mix_bits, weights, query_weights, out, near, far, sems):
    copies = [
        pltpu.make_async_copy(weights.at[m, 0], query_weights.at[m], sems.at[m]) for m in (0, 1)
    ]
    for copy in copies:
        copy.start()
    z, u = place[0], place[2]
    own_rows, wide = out.shape[1:]

    def fill(target, start, k):
        for i, r in enumerate((0, 2)):
            rows = pl.ds(pl.multiple_of((u ^ r) * own_rows, 8), own_rows)
            bits = out_bits[rows, lanes(z ^ k, wide)]
            target[start + i] = (2 * bits - 1).astype(jnp.float32).astype(bf)

    fill(out, 0, 0)
    for r, part in enumerate(sign_pieces(mix_bits, u, team)):
        near[r] = part.astype(bf)
        far[r] = part.astype(bf)
    fill(near, team, 1)
    fill(far, team, 2)
    fill(far, team + 2, 3)
    for copy in copies:
        copy.wait()


def near_kernel(near, far, out):
    team = near.shape[0] - 2
    out[:team] = near[:team]
    out[team : 2 * team] = far[:team]
    out[2 * team : 2 * team + 2] = near[team:]
    out[2 * team + 2 :] = far[team + 2 :]


def late_kernel(place, own, near, far, got, mix, out):
    team, own_rows = near.shape[0] - 2, near.shape[1]
    size = team * own_rows
    out[0] = own[...]
    out[1] = got[2 * team : 2 * team + 2]
    out[2] = far[team : team + 2]
    out[3] = got[2 * team + 2 :]
    for j, (ref, start) in enumerate(((near, 0), (got, 0), (far, 0), (got, team))):
        cut = slice(j * size, (j + 1) * size)
        for k in range(5):
            head = lanes(place[0] ^ k, HEAD) if k < 4 else slice(4 * HEAD, None)
            parts = [ref[start + r, :, head].astype(jnp.float32) for r in range(team)]
            mix[cut, k * HEAD : (k + 1) * HEAD] = jnp.concatenate(parts, axis=0).astype(bf)


def stack_kernel(*refs):
    for k, ref in enumerate(refs[:-1]):
        refs[-1][k] = ref[: refs[-1].shape[1]]


def pair_kernel(own, taken, out):
    out[0] = own[...]
    out[1] = taken[...]


def forward_kernel(taken, out):
    out[...] = taken[taken.shape[0] - out.shape[0] :]


def rows_kernel(place, own, taken, rows):
    depth, kinds, piece = own.shape[1:4]
    for m in range(kinds):
        for j in range(depth):
            parts = [ref[y, j, m].astype(jnp.float32) for y in (0, 1) for ref in (own, taken)]
            at = j * 4 * piece
            wide = jnp.concatenate(parts, axis=0)
            slab = wide.shape[1] // 2
            low, high = wide[:, :slab], wide[:, slab:]
            first = place[1] == 0
            rows[m, 0, at : at + 4 * piece] = jnp.where(first, low, high).astype(bf)
            rows[m, 1, at : at + 4 * piece] = jnp.where(first, high, low).astype(bf)


def project_kernel(
    parts, size, place, rows, weights, partner, signs_0, signs_1, signs_2, signs_3,
    send, keep_own, keep_two, total,
):
    z = place[0]
    half = rows.shape[2]
    depth = half // size

    def block(j, head):
        return total[j * size : (j + 1) * size, lanes(head, HEAD)]

    def main(target, start, k):
        for j in range(depth):
            at = start + (j ^ k) * size
            target[at : at + size] = block(j, z ^ k).astype(target.dtype)

    def rest(target, start, j):
        target[start : start + size] = block(j, depth).astype(target.dtype)

    for i, part in enumerate(parts):
        near, far = [
            dot32(rows[m, 0], weights[m, part]) + dot32(rows[m, 1], partner[m, i]) for m in (0, 1)
        ]
        total[...] = far
        plain = near
        at = part - 1 if part else 2
        team = signs_3.shape[0] // 3
        for j in range(depth):
            cut = slice(j * size, (j + 1) * size)
            ref = (signs_0, signs_1, signs_2, signs_3)[j]
            start = ref.shape[0] - (3 - at) * team
            pieces = [ref[start + r].astype(jnp.float32) for r in range(team)]
            total[cut] = plain[cut] + jnp.concatenate(pieces, axis=0) * total[cut]
        if part:
            main(send, 3 * half * i, 1)
            main(send, 3 * half * i + half, 3)
            main(keep_own, 2 * half * i, 0)
            main(keep_two, half * i, 2)
            for j in range(depth):
                rest(send, 3 * half * i + 2 * half + (j ^ 1) * size, j)
                rest(keep_own, 2 * half * i + half + j * size, j)
        else:
            main(send, 0, 1)
            rest(send, half, 1)
            main(send, half + size, 3)
            rest(send, 2 * half + size, 3)
            main(keep_own, 0, 0)
            rest(keep_own, half, 0)
            main(keep_two, 0, 2)
            rest(keep_two, half, 2)


def middle_kernel(size, keep_own, keep_two, taken, send, total):
    count = keep_two.shape[0]
    if keep_own.shape[0] == count:
        total[...] = keep_own[...] + taken[:count].astype(jnp.float32)
        send[...] = (keep_two[...] + taken[count:].astype(jnp.float32)).astype(bf)
        return
    half = count // 2
    for i in (0, 1):
        base, got = 2 * half * i, 3 * half * i
        first = slice(base, base + half)
        total[first] = keep_own[first] + taken[got : got + half].astype(jnp.float32)
        far = keep_two[half * i : half * i + half]
        send[first] = (far + taken[got + half : got + 2 * half].astype(jnp.float32)).astype(bf)
        for j in range(half // size):
            cut = slice(base + half + j * size, base + half + (j + 1) * size)
            at = got + 2 * half + j * size
            value = keep_own[cut] + taken[at : at + size].astype(jnp.float32)
            total[cut] = value
            at = base + half + (j ^ 2) * size
            send[at : at + size] = value.astype(bf)


def norm_rows(values, gain_row):
    wide = values.astype(jnp.float32)
    inverse_rms = lax.rsqrt(jnp.mean(wide * wide, axis=-1, keepdims=True) + epsilon)
    return (wide * inverse_rms * gain_row).astype(bf)


def key_value_kernel(half, place, total, taken, gain, out):
    keep = (total[...] + taken[...].astype(jnp.float32)).astype(bf)
    heads = gain.shape[0]
    out[:half] = norm_rows(keep[:half], gain[pl.ds(place[0], 1), :])
    out[half : 2 * half] = norm_rows(keep[half : 2 * half], gain[heads - 1 : heads, :])
    out[2 * half :] = keep[2 * half :]


def attend_kernel(half, place, total, taken, gain, own, partner, out):
    keep = (total[...] + taken[...].astype(jnp.float32)).astype(bf)
    heads = gain.shape[0]

    def attend(queries, cut):
        score_scale = 1.0 / math.sqrt(HEAD)
        totals, sums = 0.0, 0.0
        for both in (own, partner):
            scores = dot32_t(queries, both[cut]) * score_scale
            weights = jnp.exp(scores).astype(bf)
            totals = totals + jnp.sum(weights.astype(jnp.float32), axis=1, keepdims=True)
            sums = sums + dot32(weights, both[2 * half + cut.start : 2 * half + cut.stop])
        return (sums / totals).astype(bf)

    first = norm_rows(keep[:half], gain[pl.ds(place[0], 1), :])
    out[:half] = attend(first, slice(0, half))
    last = norm_rows(keep[half:], gain[heads - 1 : heads, :])
    out[half:] = attend(last, slice(half, 2 * half))


def core_kernel(own, taken, signs, kept, sent):
    for i, target in enumerate((kept, sent)):
        for j in range(kept.shape[0]):
            parts = [own[m, j, i].astype(jnp.float32) + taken[m, j, i].astype(jnp.float32) for m in (0, 1)]
            value = parts[0] + signs[j, i].astype(jnp.float32) * parts[1]
            target[j] = value.astype(target.dtype)


def team_kernel(kept, taken, *blocks):
    for j, block in enumerate(blocks):
        block[...] = (kept[j] + taken[j].astype(jnp.float32)).astype(bf)


def final_kernel(place, *refs):
    out = refs[-1]
    for k, block in enumerate(refs[:-1]):
        out[:, lanes(place[0] ^ k, block.shape[1])] = block[...]


def stationary_plan(
    tokens, in_bits, qkv_weights, qkv_bits, gain_query, gain_key, out_weights, mix_bits, out_bits
):
    groups = lax.axis_size("blk")
    team = lax.axis_size("uly")
    depth = groups // 2
    z = lax.axis_index("blk") // 2
    x = lax.axis_index("blk") % 2
    u = lax.axis_index("uly")
    own_rows, width = tokens.shape
    slab = qkv_weights.shape[2]
    columns = qkv_weights.shape[3]
    size = own_rows * team
    heads = columns // HEAD
    half = depth * size
    steps = range(depth)
    f32 = jnp.float32
    place = jnp.stack([z, x, u]).astype(jnp.int32)

    def swap_x(value):
        return lax.ppermute(value, "blk", [(i, i ^ 1) for i in range(groups)])

    def swap_z(value, step):
        return lax.ppermute(value, "blk", [(i, i ^ (2 * step)) for i in range(groups)])

    def swap_u(value, bit):
        return lax.ppermute(value, "uly", [(i, i ^ bit) for i in range(team)])

    def after(value, *earlier):
        return lax.optimization_barrier((value,) + earlier)[0]

    early = call(
        functools.partial(copy_kernel, 1, 2),
        shape(2, 2, slab, columns), ANY, [ANY], [pltpu.SemaphoreType.DMA((2,))],
    )(qkv_weights)
    partner_early = swap_x(early)

    sign_bits = jnp.transpose(qkv_bits, (1, 0, 2))
    counts = [2 + 3 * team if k in (1, 2) else 2 for k in steps]
    blocks = call(
        functools.partial(prepare_kernel, team),
        [shape(count, own_rows, 2 * slab) for count in counts],
        [VMEM] * depth, [SMEM] + [VMEM] * 3,
    )(place, after(tokens, early), in_bits, sign_bits)
    query_weights, late_own, late_near, late_far = call(
        functools.partial(late_signs_kernel, team),
        [shape(2, slab, columns)]
        + [shape(count, own_rows, 2 * slab) for count in (2, team + 2, team + 4)],
        [ANY] + [VMEM] * 3,
        [SMEM] + [VMEM] * 2 + [ANY],
        [pltpu.SemaphoreType.DMA((2,))],
    )(place, after(out_bits, blocks[0]), mix_bits, qkv_weights)
    blocks = [*blocks[:3], after(blocks[3], query_weights)]
    got = [blocks[0]] + [swap_z(blocks[k], k) for k in steps if k]

    def pair(first, second):
        return call(pair_kernel, shape(2, *first.shape), VMEM, [VMEM] * 2)(first, second)

    held_shape = (depth, 2, own_rows, 2 * slab)
    held = call(stack_kernel, shape(*held_shape), VMEM, [VMEM] * depth)(*got)
    forward = call(forward_kernel, shape(3 * team, own_rows, columns), VMEM, [VMEM])(got[2])
    signs = (blocks[2], got[1], got[2], swap_z(after(forward, held), 1))
    held = pair(held, swap_u(held, 2))
    rows = call(rows_kernel, shape(2, 2, half, slab), VMEM, [SMEM] + [VMEM] * 2)(
        place, held, swap_u(after(held, signs[3]), 1)
    )

    late_far = swap_z(after(late_far, held), 2)
    partner_query = swap_x(after(query_weights, partner_early, forward))
    out_t = jnp.transpose(out_weights, (0, 2, 1))
    out_partner = swap_x(after(out_t, partner_query, late_far))

    def project(parts, rows, partner):
        whole = len(parts)
        count = half + size
        counts = (3 * half * whole, 2 * half * whole, half * whole)
        if parts == (0,):
            counts = (2 * count, count, count)
        return call(
            functools.partial(project_kernel, parts, size),
            [shape(counts[0], HEAD)] + [shape(count, HEAD, dtype=f32) for count in counts[1:]],
            [VMEM] * 3,
            [SMEM] + [VMEM] * 7,
            [
                pltpu.VMEM((half, columns), f32),
            ],
        )(place, rows, qkv_weights, partner, *signs)

    def middle(keep_own, keep_two, taken):
        count = keep_own.shape[0]
        return call(
            functools.partial(middle_kernel, size),
            [shape(count, HEAD), shape(count, HEAD, dtype=f32)],
            [VMEM] * 2,
            [VMEM] * 3,
        )(keep_own, keep_two, taken)

    both_send, both_own, both_two = project(
        (1, 2), rows, partner_early
    )
    taken = swap_z(both_send, 1)
    send, both_total = middle(both_own, both_two, taken)
    both_last = swap_z(send, 2)
    query_send, query_own, query_two = project(
        (0,), after(rows, both_total, late_far), partner_query.reshape(2, 1, slab, columns),
    )
    query_taken = swap_z(query_send, 1)
    send, query_total = middle(query_own, query_two, after(query_taken, both_total))
    query_last = swap_z(send, 2)
    both = call(
        functools.partial(key_value_kernel, half),
        shape(4 * half, HEAD), VMEM, [SMEM] + [VMEM] * 3,
    )(place, both_total, after(both_last, query_total, out_partner), gain_key.reshape(heads, HEAD))
    both_partner = swap_x(both)
    late_got = call(near_kernel, shape(2 * team + 4, own_rows, 2 * slab), VMEM, [VMEM] * 2)(
        late_near, late_far
    )
    late_got = swap_z(after(late_got, both), 1)
    done = call(
        functools.partial(attend_kernel, half),
        shape(half + size, HEAD), VMEM, [SMEM] + [VMEM] * 5,
    )(place, query_total, query_last, gain_query.reshape(heads, HEAD), both, both_partner)

    by_head, last_head = [], []
    for k in steps:
        block = swap_z(done, k) if k else done
        main = block[:half].reshape(depth, size, HEAD)
        by_head.append(jnp.concatenate([main[j ^ k] for j in steps], axis=0))
        last_head.append(block[half:])
    attended = jnp.concatenate(by_head + [jnp.concatenate(last_head, axis=0)], axis=1)

    def relative(value, axis):
        parts = [
            lax.dynamic_slice_in_dim(value, (z ^ k) * HEAD, HEAD, axis) for k in steps
        ] + [lax.slice_in_dim(value, depth * HEAD, heads * HEAD, axis=axis)]
        return jnp.concatenate(parts, axis=axis)

    mix, out_signs = call(
        late_kernel,
        [shape(half, columns), shape(depth, 2, own_rows, 2 * slab)], [VMEM] * 2,
        [SMEM] + [VMEM] * 4,
    )(place, late_own, after(late_near, done), late_far, late_got)
    attended_flipped = attended * mix
    first = jnp.where(x == 0, out_t, out_partner)
    second = jnp.where(x == 0, out_partner, out_t)
    out_full = relative(jnp.concatenate([first, second], axis=1), 2)
    partial = jnp.stack(
        [dot32_t(attended, out_full[0]), dot32_t(attended_flipped, out_full[1])]
    ).astype(bf)
    partial = partial.reshape(2, depth, team, own_rows, 2 * slab)
    kept, sent = call(
        core_kernel,
        [shape(depth, own_rows, 2 * slab, dtype=f32), shape(depth, own_rows, 2 * slab)],
        [VMEM] * 2, [VMEM] * 3,
    )(partial[:, :, 0::2], swap_u(partial[:, :, 1::2], 1), out_signs)
    blocks = call(
        team_kernel, [shape(own_rows, 2 * slab)] * depth, [VMEM] * depth, [VMEM] * 2
    )(kept, swap_u(sent, 2))
    return call(
        final_kernel, shape(own_rows, width), VMEM, [SMEM] + [VMEM] * depth
    )(place, blocks[0], *[swap_z(blocks[k], k) for k in steps if k])


def body(*arrays):
    heads = arrays[2].shape[3] // HEAD
    depth = lax.axis_size("blk") // 2
    if depth == heads - 1 and depth == 4 and lax.axis_size("uly") == 4:
        return stationary_plan(*arrays)
    return gather_plan(*arrays)


def solution(mesh):
    return jax.shard_map(
        body,
        mesh=mesh,
        in_specs=(
            P(("blk", "uly"), None),
            P(("blk", "uly"), None),
            P(None, None, "blk", "uly"),
            P("blk", None, "uly"),
            P("uly"),
            P("uly"),
            P(None, "uly", "blk"),
            P("blk", "uly"),
            P("blk", None),
        ),
        out_specs=P(("blk", "uly"), None),
        check_vma=False,
    )
```

```python
import functools
import math

import jax
import jax.numpy as jnp
from jax import lax
from jax.experimental import pallas as pl
from jax.experimental.pallas import tpu as pltpu
from jax.sharding import PartitionSpec as P

HEAD = 128


epsilon = 1e-06


def signed(bit_values):
    return (2 * bit_values - 1).astype(jnp.float32)


def normalize(values, gain_vector):
    row_count = values.shape[0]
    by_head = values.astype(jnp.float32).reshape(row_count, -1, HEAD)
    inverse_rms = lax.rsqrt(jnp.mean(by_head * by_head, axis=-1, keepdims=True) + epsilon)
    return (by_head * inverse_rms * gain_vector.reshape(-1, HEAD)).astype(jnp.bfloat16)


def gather_plan(
    tokens, in_bits, qkv_weights, qkv_bits, gain_query, gain_key, out_weights, mix_bits, out_bits
):
    flipped = (tokens.astype(jnp.float32) * signed(in_bits)).astype(jnp.bfloat16)
    group_rows = lax.all_gather(jnp.stack([tokens, flipped]), "uly", axis=1, tiled=True)
    row_total = group_rows.shape[1]
    projections = jnp.einsum(
        "mrd,mkdc->rmkc",
        group_rows,
        lax.all_gather(qkv_weights, "blk", axis=2, tiled=True),
        preferred_element_type=jnp.float32,
    )
    projected = (projections[:, 0] + signed(qkv_bits) * projections[:, 1]).astype(jnp.bfloat16)
    queries = normalize(projected[:, 0], gain_query)
    head_count = queries.shape[1]
    keys_normed = normalize(projected[:, 1], gain_key).reshape(row_total, -1)
    values_block = projected[:, 2]
    score_scale = 1.0 / math.sqrt(HEAD)

    def attend(running, shard_piece):
        numerator, denominator = running
        key_rows = shard_piece[0].reshape(shard_piece[0].shape[0], head_count, HEAD)
        value_rows = shard_piece[1].reshape(shard_piece[1].shape[0], head_count, HEAD)
        scores = (
            jnp.einsum("rhd,nhd->hrn", queries, key_rows, preferred_element_type=jnp.float32)
            * score_scale
        )
        weights = jnp.exp(scores).astype(jnp.bfloat16)
        numerator = numerator + jnp.einsum(
            "hrn,nhd->rhd", weights, value_rows, preferred_element_type=jnp.float32
        )
        denominator = denominator + jnp.sum(weights.astype(jnp.float32), axis=2).T
        return (numerator, denominator)

    start_state = (
        jnp.zeros((row_total, head_count, HEAD), jnp.float32),
        jnp.zeros((row_total, head_count), jnp.float32),
    )
    all_keys, all_values = (
        lax.all_gather(keys_normed, "blk", axis=0, tiled=True),
        lax.all_gather(values_block, "blk", axis=0, tiled=True),
    )
    group_count = lax.axis_size("blk")
    per_block = 1
    while per_block * row_total < 512 and group_count % (per_block * 2) == 0:
        per_block = per_block * 2
    block_rows = per_block * row_total
    block_count = group_count // per_block
    key_blocks = all_keys.reshape(block_count, block_rows, all_keys.shape[1])
    value_blocks = all_values.reshape(block_count, block_rows, all_values.shape[1])

    def scan_step(running, block_pair):
        return (attend(running, block_pair), None)

    (numerator, denominator), unused = lax.scan(scan_step, start_state, (key_blocks, value_blocks))
    attended = (numerator / denominator[:, :, None]).astype(jnp.bfloat16).reshape(row_total, -1)
    attended_flipped = (attended.astype(jnp.float32) * signed(mix_bits)).astype(jnp.bfloat16)
    attended_pair = jnp.stack([attended, attended_flipped])
    out_signs = signed(out_bits)
    partial_out = jnp.einsum(
        "mrc,mcn->rmn",
        attended_pair,
        lax.all_gather(out_weights, "blk", axis=2, tiled=True),
        preferred_element_type=jnp.float32,
    )
    summed = lax.psum_scatter(
        partial_out.astype(jnp.bfloat16), "uly", scatter_dimension=0, tiled=True
    ).astype(jnp.float32)
    own_rows = summed.shape[0]
    own_signs = lax.dynamic_slice_in_dim(out_signs, lax.axis_index("uly") * own_rows, own_rows, 0)
    result_rows = summed[:, 0] + own_signs * summed[:, 1]
    return result_rows.astype(jnp.bfloat16)


def dot32(a, b):
    return lax.dot_general(
        a, b, (((1,), (0,)), ((), ())), preferred_element_type=jnp.float32
    )


def dot32_t(a, b):
    return lax.dot_general(
        a, b, (((1,), (1,)), ((), ())), preferred_element_type=jnp.float32
    )


bf = jnp.bfloat16
VMEM = pl.BlockSpec(memory_space=pltpu.VMEM)
SMEM = pl.BlockSpec(memory_space=pltpu.SMEM)
ANY = pl.BlockSpec(memory_space=pl.ANY)


def call(kernel, outs, out_specs, in_specs, scratch=(), flops=0, moved=0):
    return pl.pallas_call(
        kernel,
        out_shape=outs,
        in_specs=in_specs,
        out_specs=out_specs,
        scratch_shapes=list(scratch),
        compiler_params=pltpu.CompilerParams(vmem_limit_bytes=40 * 1024 * 1024),
        cost_estimate=pl.CostEstimate(flops=flops, bytes_accessed=moved, transcendentals=0),
    )


def shape(*dims, dtype=bf):
    return jax.ShapeDtypeStruct(dims, dtype)


def lanes(index, size):
    return pl.ds(pl.multiple_of(index * size, 128), size)


def copy_kernel(first, count, weights, out, sems):
    copies = [
        pltpu.make_async_copy(weights.at[m, pl.ds(first, count)], out.at[m], sems.at[m])
        for m in (0, 1)
    ]
    for copy in copies:
        copy.start()
    for copy in copies:
        copy.wait()


def sign_pieces(bits, u, team):
    piece = bits.shape[0] // team
    parts = [bits[pl.ds(pl.multiple_of((u ^ r) * piece, 8), piece), :] for r in range(team)]
    return [(2 * part - 1).astype(jnp.float32) for part in parts]


def prepare_kernel(team, place, tokens, in_bits, sign_bits, *blocks):
    wide = tokens.shape[1] // len(blocks)
    for k, block in enumerate(blocks):
        cut = lanes(place[0] ^ k, wide)
        plain = tokens[:, cut]
        sign = (2 * in_bits[:, cut] - 1).astype(jnp.float32)
        block[0] = plain
        block[1] = (plain.astype(jnp.float32) * sign).astype(bf)
    for i, part in enumerate((1, 2, 0)):
        for r, piece in enumerate(sign_pieces(sign_bits.at[part], place[2], team)):
            for block in blocks[1:3]:
                block[2 + team * i + r] = piece.astype(bf)


def late_signs_kernel(team, place, out_bits, mix_bits, weights, query_weights, out, near, far, sems):
    copies = [
        pltpu.make_async_copy(weights.at[m, 0], query_weights.at[m], sems.at[m]) for m in (0, 1)
    ]
    for copy in copies:
        copy.start()
    z, u = place[0], place[2]
    own_rows, wide = out.shape[1:]

    def fill(target, start, k):
        for i, r in enumerate((0, 2)):
            rows = pl.ds(pl.multiple_of((u ^ r) * own_rows, 8), own_rows)
            bits = out_bits[rows, lanes(z ^ k, wide)]
            target[start + i] = (2 * bits - 1).astype(jnp.float32).astype(bf)

    fill(out, 0, 0)
    for r, part in enumerate(sign_pieces(mix_bits, u, team)):
        near[r] = part.astype(bf)
        far[r] = part.astype(bf)
    fill(near, team, 1)
    fill(far, team, 2)
    fill(far, team + 2, 3)
    for copy in copies:
        copy.wait()


def near_kernel(near, far, out):
    team = near.shape[0] - 2
    out[:team] = near[:team]
    out[team : 2 * team] = far[:team]
    out[2 * team : 2 * team + 2] = near[team:]
    out[2 * team + 2 :] = far[team + 2 :]


def late_kernel(place, own, near, far, got, mix, out):
    team, own_rows = near.shape[0] - 2, near.shape[1]
    size = team * own_rows
    out[0] = own[...]
    out[1] = got[2 * team : 2 * team + 2]
    out[2] = far[team : team + 2]
    out[3] = got[2 * team + 2 :]
    for j, (ref, start) in enumerate(((near, 0), (got, 0), (far, 0), (got, team))):
        cut = slice(j * size, (j + 1) * size)
        for k in range(5):
            head = lanes(place[0] ^ k, HEAD) if k < 4 else slice(4 * HEAD, None)
            parts = [ref[start + r, :, head].astype(jnp.float32) for r in range(team)]
            mix[cut, k * HEAD : (k + 1) * HEAD] = jnp.concatenate(parts, axis=0).astype(bf)


def stack_kernel(*refs):
    for k, ref in enumerate(refs[:-1]):
        refs[-1][k] = ref[: refs[-1].shape[1]]


def pair_kernel(own, taken, out):
    out[0] = own[...]
    out[1] = taken[...]


def forward_kernel(taken, out):
    out[...] = taken[taken.shape[0] - out.shape[0] :]


def rows_kernel(own, taken, rows):
    depth, kinds, piece = own.shape[1:4]
    for m in range(kinds):
        for j in range(depth):
            parts = [ref[y, j, m].astype(jnp.float32) for y in (0, 1) for ref in (own, taken)]
            at = j * 4 * piece
            rows[m, at : at + 4 * piece] = jnp.concatenate(parts, axis=0).astype(bf)


def project_kernel(
    parts, size, place, rows, weights, partner, signs_0, signs_1, signs_2, signs_3,
    send, keep_own, keep_two, held, total, sems,
):
    z, x = place[0], place[1]
    slab = weights.shape[2]
    own = pl.ds(pl.multiple_of(x * slab, 64), slab)
    other = pl.ds(pl.multiple_of((1 - x) * slab, 64), slab)
    depth = rows.shape[1] // size
    half = depth * size
    copies = []
    for i, part in enumerate(parts):
        for m in (0, 1):
            near, far = weights.at[m, part], partner.at[m, i]
            copies.append(pltpu.make_async_copy(near, held.at[i, m, own], sems.at[i, m, 0]))
            copies.append(pltpu.make_async_copy(far, held.at[i, m, other], sems.at[i, m, 1]))
    for copy in copies:
        copy.start()

    def block(j, head):
        return total[j * size : (j + 1) * size, lanes(head, HEAD)]

    def main(target, start, k):
        for j in range(depth):
            at = start + (j ^ k) * size
            target[at : at + size] = block(j, z ^ k).astype(target.dtype)

    def rest(target, start, j):
        target[start : start + size] = block(j, depth).astype(target.dtype)

    for i, part in enumerate(parts):
        for copy in copies[4 * i : 4 * i + 4]:
            copy.wait()
        total[...] = dot32(rows[1], held[i, 1])
        plain = dot32(rows[0], held[i, 0])
        at = part - 1 if part else 2
        team = signs_3.shape[0] // 3
        for j in range(depth):
            cut = slice(j * size, (j + 1) * size)
            ref = (signs_0, signs_1, signs_2, signs_3)[j]
            start = ref.shape[0] - (3 - at) * team
            pieces = [ref[start + r].astype(jnp.float32) for r in range(team)]
            total[cut] = plain[cut] + jnp.concatenate(pieces, axis=0) * total[cut]
        if part:
            main(send, 3 * half * i, 1)
            main(send, 3 * half * i + half, 3)
            main(keep_own, 2 * half * i, 0)
            main(keep_two, half * i, 2)
            for j in range(depth):
                rest(send, 3 * half * i + 2 * half + (j ^ 1) * size, j)
                rest(keep_own, 2 * half * i + half + j * size, j)
        else:
            main(send, 0, 1)
            rest(send, half, 1)
            main(send, half + size, 3)
            rest(send, 2 * half + size, 3)
            main(keep_own, 0, 0)
            rest(keep_own, half, 0)
            main(keep_two, 0, 2)
            rest(keep_two, half, 2)


def middle_kernel(size, keep_own, keep_two, taken, send, total):
    count = keep_two.shape[0]
    if keep_own.shape[0] == count:
        total[...] = keep_own[...] + taken[:count].astype(jnp.float32)
        send[...] = (keep_two[...] + taken[count:].astype(jnp.float32)).astype(bf)
        return
    half = count // 2
    for i in (0, 1):
        base, got = 2 * half * i, 3 * half * i
        first = slice(base, base + half)
        total[first] = keep_own[first] + taken[got : got + half].astype(jnp.float32)
        far = keep_two[half * i : half * i + half]
        send[first] = (far + taken[got + half : got + 2 * half].astype(jnp.float32)).astype(bf)
        for j in range(half // size):
            cut = slice(base + half + j * size, base + half + (j + 1) * size)
            at = got + 2 * half + j * size
            value = keep_own[cut] + taken[at : at + size].astype(jnp.float32)
            total[cut] = value
            at = base + half + (j ^ 2) * size
            send[at : at + size] = value.astype(bf)


def norm_rows(values, gain_row):
    wide = values.astype(jnp.float32)
    inverse_rms = lax.rsqrt(jnp.mean(wide * wide, axis=-1, keepdims=True) + epsilon)
    return (wide * inverse_rms * gain_row).astype(bf)


def key_value_kernel(half, place, total, taken, gain, out):
    keep = (total[...] + taken[...].astype(jnp.float32)).astype(bf)
    heads = gain.shape[0]
    out[:half] = norm_rows(keep[:half], gain[pl.ds(place[0], 1), :])
    out[half : 2 * half] = norm_rows(keep[half : 2 * half], gain[heads - 1 : heads, :])
    out[2 * half :] = keep[2 * half :]


def attend_kernel(half, place, total, taken, gain, own, partner, out):
    keep = (total[...] + taken[...].astype(jnp.float32)).astype(bf)
    heads = gain.shape[0]

    def attend(queries, cut):
        score_scale = 1.0 / math.sqrt(HEAD)
        totals, sums = 0.0, 0.0
        for both in (own, partner):
            scores = dot32_t(queries, both[cut]) * score_scale
            weights = jnp.exp(scores).astype(bf)
            totals = totals + jnp.sum(weights.astype(jnp.float32), axis=1, keepdims=True)
            sums = sums + dot32(weights, both[2 * half + cut.start : 2 * half + cut.stop])
        return (sums / totals).astype(bf)

    first = norm_rows(keep[:half], gain[pl.ds(place[0], 1), :])
    out[:half] = attend(first, slice(0, half))
    last = norm_rows(keep[half:], gain[heads - 1 : heads, :])
    out[half:] = attend(last, slice(half, 2 * half))


def core_kernel(own, taken, signs, kept, sent):
    for i, target in enumerate((kept, sent)):
        for j in range(kept.shape[0]):
            parts = [own[m, j, i].astype(jnp.float32) + taken[m, j, i].astype(jnp.float32) for m in (0, 1)]
            value = parts[0] + signs[j, i].astype(jnp.float32) * parts[1]
            target[j] = value.astype(target.dtype)


def team_kernel(kept, taken, *blocks):
    for j, block in enumerate(blocks):
        block[...] = (kept[j] + taken[j].astype(jnp.float32)).astype(bf)


def final_kernel(place, *refs):
    out = refs[-1]
    for k, block in enumerate(refs[:-1]):
        out[:, lanes(place[0] ^ k, block.shape[1])] = block[...]


def stationary_plan(
    tokens, in_bits, qkv_weights, qkv_bits, gain_query, gain_key, out_weights, mix_bits, out_bits
):
    groups = lax.axis_size("blk")
    team = lax.axis_size("uly")
    depth = groups // 2
    z = lax.axis_index("blk") // 2
    x = lax.axis_index("blk") % 2
    u = lax.axis_index("uly")
    own_rows, width = tokens.shape
    slab = qkv_weights.shape[2]
    columns = qkv_weights.shape[3]
    size = own_rows * team
    heads = columns // HEAD
    half = depth * size
    steps = range(depth)
    f32 = jnp.float32
    place = jnp.stack([z, x, u]).astype(jnp.int32)

    def swap_x(value):
        return lax.ppermute(value, "blk", [(i, i ^ 1) for i in range(groups)])

    def swap_z(value, step):
        return lax.ppermute(value, "blk", [(i, i ^ (2 * step)) for i in range(groups)])

    def swap_u(value, bit):
        return lax.ppermute(value, "uly", [(i, i ^ bit) for i in range(team)])

    def after(value, *earlier):
        return lax.optimization_barrier((value,) + earlier)[0]

    early = call(
        functools.partial(copy_kernel, 1, 2),
        shape(2, 2, slab, columns), ANY, [ANY], [pltpu.SemaphoreType.DMA((2,))],
    )(qkv_weights)
    partner_early = swap_x(early)

    sign_bits = jnp.transpose(qkv_bits, (1, 0, 2))
    counts = [2 + 3 * team if k in (1, 2) else 2 for k in steps]
    blocks = call(
        functools.partial(prepare_kernel, team),
        [shape(count, own_rows, 2 * slab) for count in counts],
        [VMEM] * depth, [SMEM] + [VMEM] * 3,
    )(place, after(tokens, early), in_bits, sign_bits)
    query_weights, late_own, late_near, late_far = call(
        functools.partial(late_signs_kernel, team),
        [shape(2, slab, columns)]
        + [shape(count, own_rows, 2 * slab) for count in (2, team + 2, team + 4)],
        [ANY] + [VMEM] * 3,
        [SMEM] + [VMEM] * 2 + [ANY],
        [pltpu.SemaphoreType.DMA((2,))],
    )(place, after(out_bits, blocks[0]), mix_bits, qkv_weights)
    blocks = [*blocks[:3], after(blocks[3], query_weights)]
    got = [blocks[0]] + [swap_z(blocks[k], k) for k in steps if k]

    def pair(first, second):
        return call(pair_kernel, shape(2, *first.shape), VMEM, [VMEM] * 2)(first, second)

    held_shape = (depth, 2, own_rows, 2 * slab)
    held = call(stack_kernel, shape(*held_shape), VMEM, [VMEM] * depth)(*got)
    forward = call(forward_kernel, shape(3 * team, own_rows, columns), VMEM, [VMEM])(got[2])
    signs = (blocks[2], got[1], got[2], swap_z(after(forward, held), 1))
    held = pair(held, swap_u(held, 2))
    rows = call(rows_kernel, shape(2, half, 2 * slab), VMEM, [VMEM] * 2)(
        held, swap_u(after(held, signs[3]), 1)
    )

    late_far = swap_z(after(late_far, held), 2)
    partner_query = swap_x(after(query_weights, partner_early, forward))
    out_t = jnp.transpose(out_weights, (0, 2, 1))
    out_partner = swap_x(after(out_t, partner_query))

    def project(parts, rows, partner):
        whole = len(parts)
        count = half + size
        counts = (3 * half * whole, 2 * half * whole, half * whole)
        if parts == (0,):
            counts = (2 * count, count, count)
        return call(
            functools.partial(project_kernel, parts, size),
            [shape(counts[0], HEAD)] + [shape(count, HEAD, dtype=f32) for count in counts[1:]],
            [VMEM] * 3,
            [SMEM, VMEM, ANY, ANY] + [VMEM] * 4,
            [
                pltpu.VMEM((whole, 2, 2 * slab, columns), bf),
                pltpu.VMEM((half, columns), f32),
                pltpu.SemaphoreType.DMA((whole, 2, 2)),
            ],
        )(place, rows, qkv_weights, partner, *signs)

    def middle(keep_own, keep_two, taken):
        count = keep_own.shape[0]
        return call(
            functools.partial(middle_kernel, size),
            [shape(count, HEAD), shape(count, HEAD, dtype=f32)],
            [VMEM] * 2,
            [VMEM] * 3,
        )(keep_own, keep_two, taken)

    both_send, both_own, both_two = project(
        (1, 2), rows, partner_early
    )
    taken = swap_z(both_send, 1)
    query_send, query_own, query_two = project(
        (0,), after(rows, both_send), partner_query.reshape(2, 1, slab, columns),
    )
    query_taken = swap_z(query_send, 1)
    send, both_total = middle(both_own, both_two, after(taken, query_send, late_far))
    both_last = swap_z(send, 2)
    send, query_total = middle(query_own, query_two, after(query_taken, both_total))
    query_last = swap_z(send, 2)
    both = call(
        functools.partial(key_value_kernel, half),
        shape(4 * half, HEAD), VMEM, [SMEM] + [VMEM] * 3,
    )(place, both_total, after(both_last, query_total), gain_key.reshape(heads, HEAD))
    both_partner = swap_x(both)
    late_got = call(near_kernel, shape(2 * team + 4, own_rows, 2 * slab), VMEM, [VMEM] * 2)(
        late_near, late_far
    )
    late_got = swap_z(after(late_got, both), 1)
    done = call(
        functools.partial(attend_kernel, half),
        shape(half + size, HEAD), VMEM, [SMEM] + [VMEM] * 5,
    )(place, query_total, query_last, gain_query.reshape(heads, HEAD), both, both_partner)

    by_head, last_head = [], []
    for k in steps:
        block = swap_z(done, k) if k else done
        main = block[:half].reshape(depth, size, HEAD)
        by_head.append(jnp.concatenate([main[j ^ k] for j in steps], axis=0))
        last_head.append(block[half:])
    attended = jnp.concatenate(by_head + [jnp.concatenate(last_head, axis=0)], axis=1)

    def relative(value, axis):
        parts = [
            lax.dynamic_slice_in_dim(value, (z ^ k) * HEAD, HEAD, axis) for k in steps
        ] + [lax.slice_in_dim(value, depth * HEAD, heads * HEAD, axis=axis)]
        return jnp.concatenate(parts, axis=axis)

    mix, out_signs = call(
        late_kernel,
        [shape(half, columns), shape(depth, 2, own_rows, 2 * slab)], [VMEM] * 2,
        [SMEM] + [VMEM] * 4,
    )(place, late_own, after(late_near, done), late_far, late_got)
    attended_flipped = attended * mix
    first = jnp.where(x == 0, out_t, out_partner)
    second = jnp.where(x == 0, out_partner, out_t)
    out_full = relative(jnp.concatenate([first, second], axis=1), 2)
    partial = jnp.stack(
        [dot32_t(attended, out_full[0]), dot32_t(attended_flipped, out_full[1])]
    ).astype(bf)
    partial = partial.reshape(2, depth, team, own_rows, 2 * slab)
    kept, sent = call(
        core_kernel,
        [shape(depth, own_rows, 2 * slab, dtype=f32), shape(depth, own_rows, 2 * slab)],
        [VMEM] * 2, [VMEM] * 3,
    )(partial[:, :, 0::2], swap_u(partial[:, :, 1::2], 1), out_signs)
    blocks = call(
        team_kernel, [shape(own_rows, 2 * slab)] * depth, [VMEM] * depth, [VMEM] * 2
    )(kept, swap_u(sent, 2))
    return call(
        final_kernel, shape(own_rows, width), VMEM, [SMEM] + [VMEM] * depth
    )(place, blocks[0], *[swap_z(blocks[k], k) for k in steps if k])


def body(*arrays):
    heads = arrays[2].shape[3] // HEAD
    depth = lax.axis_size("blk") // 2
    if depth == heads - 1 and depth == 4 and lax.axis_size("uly") == 4:
        return stationary_plan(*arrays)
    return gather_plan(*arrays)


def solution(mesh):
    return jax.shard_map(
        body,
        mesh=mesh,
        in_specs=(
            P(("blk", "uly"), None),
            P(("blk", "uly"), None),
            P(None, None, "blk", "uly"),
            P("blk", None, "uly"),
            P("uly"),
            P("uly"),
            P(None, "uly", "blk"),
            P("blk", "uly"),
            P("blk", None),
        ),
        out_specs=P(("blk", "uly"), None),
        check_vma=False,
    )
```
